32 devices in a mesh: dp: 4 (over z), fsdp: 8 (over y, x, core).
Axes of the slice: x: 2, y: 2, z: 4, core: 2. Of those that a mesh axis runs over, the one named last changes fastest.
Arguments:
- activations: bfloat16 [64, 1024, 512], P(('dp', 'fsdp')), may hold values from -6 to 6
- window_lengths: int32 [64, 4], P(('dp', 'fsdp')), may hold values from 0 to 512, as said below
- query_weight: bfloat16 [512, 512], P('fsdp', 'dp'), may hold values from -0.25 to 0.25
- key_weight: bfloat16 [512, 512], P('fsdp', 'dp'), may hold values from -0.25 to 0.25
- value_weight: bfloat16 [512, 512], P('fsdp', 'dp'), may hold values from -0.25 to 0.25
- output_weight: bfloat16 [512, 512], P('fsdp', 'dp'), may hold values from -1 to 1
- inner_weight: bfloat16 [512, 2048], P('fsdp', 'dp'), may hold values from -0.25 to 0.25
- outer_weight: bfloat16 [2048, 512], P('fsdp', 'dp'), may hold values from -0.1875 to 0.1875
- vectors: bfloat16 [8, 512], P('dp', 'fsdp')
- positions: bfloat16 [1024, 512], P('dp', 'fsdp'), may hold values from -3 to 3
- inner_bias: bfloat16 [2048], P(('dp', 'fsdp')), may hold values from -3 to 3
- output_cotangent: bfloat16 [64, 1024, 512], P(('dp', 'fsdp')), may hold values from -6 to 6
Outputs:
- block_out: bfloat16 [64, 1024, 512], P(('dp', 'fsdp'))
- input_grad: bfloat16 [64, 1024, 512], P(('dp', 'fsdp'))
- query_grad: float32 [512, 512], P('fsdp', 'dp')
- key_grad: float32 [512, 512], P('fsdp', 'dp')
- value_grad: float32 [512, 512], P('fsdp', 'dp')
- output_grad: float32 [512, 512], P('fsdp', 'dp')
- inner_grad: float32 [512, 2048], P('fsdp', 'dp')
- outer_grad: float32 [2048, 512], P('fsdp', 'dp')
- vectors_grad: float32 [8, 512], P('dp', 'fsdp')
- positions_grad: float32 [1024, 512], P('dp', 'fsdp')
- inner_bias_grad: float32 [2048], P(('dp', 'fsdp'))
The draws below stay inside these ranges and needn't reach their ends.
Inputs may be any that keep to these rules, and one draw needn't show every extreme that they name: `window_lengths`: each row holds windows of 256 or 512 characters that sum to 1024, then zeros.
All inputs are finite; a program needn't handle non-finite values.
Results may differ from the reference program's by a relative error of at most 0.014.
The reference program's roundings to bfloat16 on the way count: a program that leaves them out, or rounds other values in their place, can miss the bound.
Values may be sent and summed in bfloat16 or wider, within the bound.
A program may use at most 192 MiB of HBM per device.

```python
import jax
import jax.numpy as jnp
import numpy as np
from jax import lax

D = 512
H = 8
HD = 64
FF = 2048
WIN = 256
VEC = 8
SEQ = 1024
ROWS = 64


def draw_window_lengths(key, part):
    table = jnp.array(np.array([[1, 1, 1, 1], [2, 1, 1, 0], [1, 2, 1, 0], [1, 1, 2, 0], [2, 2, 0, 0]], np.int32))
    picks = jax.random.randint(key, (ROWS,), 0, 5)
    picks = jnp.where(jnp.arange(ROWS) == 0, 4, picks)
    return (table[picks] * WIN).astype(jnp.int32)


def draw_vectors(key, part):
    base = 0.35 * jax.random.normal(key, (VEC, D), jnp.float32)
    marks = jnp.arange(VEC)[:, None]
    gains = (marks == 3) | (marks == 6)
    return jnp.where(gains, 1.0 + base, base).astype(jnp.bfloat16)


def shard_levels(stream_key, extent, shards, low, high):
    factor_of = 1.0
    for position, shards_of in shards:
        steps = jax.random.uniform(jax.random.fold_in(jax.random.fold_in(stream_key, 6), position), (shards_of,), jnp.float32, low / len(shards), high / len(shards))
        factor_of = factor_of * jnp.repeat(jnp.exp(steps), extent[position] // shards_of).reshape((-1,) + (1,) * (len(extent) - 1 - position))
    return factor_of


def noise(stream_key, dims, width, reach, cuts=(), kind=jnp.bfloat16):
    values = width * jax.random.normal(stream_key, dims, jnp.float32)
    if cuts:
        values = values * shard_levels(stream_key, dims, cuts, -0.22, 0.18)
    return jnp.clip(values, -reach, reach).astype(kind)


def setup_inputs(seed: int = 0) -> dict:
    keys = jax.random.split(jax.random.key(seed), 13)
    activations = noise(keys[0], (ROWS, SEQ, D), 1.0, 6.0, ((0, 32),))
    window_lengths = draw_window_lengths(jax.random.fold_in(keys[12], 71), 0)
    query_weight = noise(keys[2], (D, D), D ** -0.5, 0.25, ((0, 8), (1, 4)))
    key_weight = noise(keys[3], (D, D), D ** -0.5, 0.25, ((0, 8), (1, 4)))
    value_weight = noise(keys[4], (D, D), D ** -0.5, 0.25, ((0, 8), (1, 4)))
    output_weight = noise(keys[5], (D, D), (D // 16) ** -0.5, 1.0, ((0, 8), (1, 4)))
    inner_weight = noise(keys[6], (D, FF), D ** -0.5, 0.25, ((0, 8), (1, 4)))
    outer_weight = noise(keys[7], (FF, D), (FF // 2) ** -0.5, 0.1875, ((0, 8), (1, 4)))
    vectors = draw_vectors(jax.random.fold_in(keys[12], 71), 0)
    positions = noise(keys[9], (SEQ, D), 0.5, 3.0, ((0, 4), (1, 8)))
    inner_bias = noise(keys[10], (FF,), 0.5, 3.0, ((0, 32),))
    output_cotangent = noise(keys[11], (ROWS, SEQ, D), 1.0, 6.0, ((0, 32),))
    return {"activations": activations, "window_lengths": window_lengths, "query_weight": query_weight, "key_weight": key_weight, "value_weight": value_weight, "output_weight": output_weight, "inner_weight": inner_weight, "outer_weight": outer_weight, "vectors": vectors, "positions": positions, "inner_bias": inner_bias, "output_cotangent": output_cotangent}


@jax.custom_vjp
def low(v):
    return lax.optimization_barrier(v.astype(jnp.bfloat16)).astype(jnp.float32)

@jax.custom_vjp
def low_back(v):
    return v

def low_keep(v):
    return (low(v), None)

def low_pass(kept, grad):
    return (grad,)

def back_keep(v):
    return (v, None)

def back_low(kept, grad):
    return (low(grad),)
low.defvjp(low_keep, low_pass)
low_back.defvjp(back_keep, back_low)

def rounded_both(value):
    return low(low_back(value))

def gelu_tanh(value):
    return 0.5 * value * (1.0 + jnp.tanh(0.7978845608028654 * (value + 0.044715 * value * value * value)))

def layer_norm(value, gain, shift):
    center = value - lax.optimization_barrier(jnp.mean(value, -1, keepdims=True))
    spread = lax.optimization_barrier(jnp.mean(center * center, -1, keepdims=True))
    return center * lax.rsqrt(spread + 1e-05) * gain + shift

def window_ids(window_lengths, length):
    bounds = jnp.cumsum(window_lengths, -1).astype(jnp.int32)
    places = jnp.arange(length, dtype=jnp.int32)
    return lax.optimization_barrier(jnp.sum((places[None, :, None] >= bounds[:, None, :]).astype(jnp.int32), -1))

def matmul(left, right):
    return jnp.dot(left, right, precision=lax.Precision.HIGHEST, preferred_element_type=jnp.float32)

def attend_row(item):
    query_row, key_row, value_row, window_row = item
    query_heads = query_row.reshape(SEQ, H, HD)
    key_heads = key_row.reshape(SEQ, H, HD)
    value_heads = value_row.reshape(SEQ, H, HD)
    scores = low_back(jnp.einsum('qhd,khd->hqk', query_heads, key_heads, precision=lax.Precision.HIGHEST) * 0.125)
    places = jnp.arange(SEQ, dtype=jnp.int32)
    allowed = (window_row[:, None] == window_row[None, :]) & (places[None, :] <= places[:, None])
    scores = jnp.where(allowed[None], scores, -1e+30)
    probs = low(jax.nn.softmax(scores, -1))
    context = jnp.einsum('hqk,khd->qhd', probs, value_heads, precision=lax.Precision.HIGHEST)
    return context.reshape(SEQ, D)

def forward(activations, query_weight, key_weight, value_weight, output_weight, inner_weight, outer_weight, vectors, positions, inner_bias, window):
    row_count = activations.shape[0]
    start_sum = (activations + positions[None]).reshape(-1, D)
    start_low = low(start_sum)
    queries = rounded_both(matmul(start_low, query_weight) + vectors[0])
    keys_all = rounded_both(matmul(start_low, key_weight))
    values_all = rounded_both(matmul(start_low, value_weight) + vectors[1])
    context = lax.map(jax.checkpoint(attend_row), (queries.reshape(row_count, SEQ, D), keys_all.reshape(row_count, SEQ, D), values_all.reshape(row_count, SEQ, D), window))
    context = rounded_both(context.reshape(-1, D))
    attn_out = low_back(matmul(context, output_weight) + vectors[2])
    normed = layer_norm(start_sum + attn_out, vectors[3], vectors[4])
    pre_act = low_back(matmul(low(normed), inner_weight) + inner_bias)
    act_low = low(gelu_tanh(pre_act))
    branch = low_back(matmul(act_low, outer_weight) + vectors[5])
    result = layer_norm(normed + branch, vectors[6], vectors[7])
    return result.reshape(row_count, SEQ, D)

def reference(activations, window_lengths, query_weight, key_weight, value_weight, output_weight, inner_weight, outer_weight, vectors, positions, inner_bias, output_cotangent):
    window = window_ids(window_lengths, SEQ)
    floats = [a.astype(jnp.float32) for a in (activations, query_weight, key_weight, value_weight, output_weight, inner_weight, outer_weight, vectors, positions, inner_bias)]

    def closed(*inputs):
        return forward(*inputs, window)
    result, pull = jax.vjp(closed, *floats)
    grads = pull(output_cotangent.astype(jnp.float32))
    return (result.astype(jnp.bfloat16), grads[0].astype(jnp.bfloat16), grads[1], grads[2], grads[3], grads[4], grads[5], grads[6], grads[7], grads[8], grads[9])
```

```python
import functools

import jax
import jax.numpy as jnp
from jax import lax
from jax.experimental import pallas as pl
from jax.experimental.pallas import tpu as pltpu
from jax.sharding import PartitionSpec as P

H = 8
HD = 64
WIN = 256
PAIR = 2 * HD
VMEM_LIMIT = 60 * 1024 * 1024
F32 = jnp.float32
BF16 = jnp.bfloat16
MESH = pl.DeviceIdType.MESH
SMALL = 16


def nn(left, right):
    return lax.dot_general(left, right, (((1,), (0,)), ((), ())), preferred_element_type=F32)


def nt(left, right):
    return lax.dot_general(left, right, (((1,), (1,)), ((), ())), preferred_element_type=F32)


def tn(left, right):
    return lax.dot_general(left, right, (((0,), (0,)), ((), ())), preferred_element_type=F32)


def column_sum(value):
    return jnp.sum(value.astype(F32), 0, keepdims=True)


def head_rows(pair, which):
    zeros = jnp.zeros((HD, pair.shape[1]), pair.dtype)
    if which == 0:
        return jnp.concatenate([pair[:HD], zeros], 0)
    return jnp.concatenate([zeros, pair[HD:]], 0)


def head_lanes(pair, which):
    lane = lax.broadcasted_iota(jnp.int32, pair.shape, 1)
    keep = (lane < HD) if which == 0 else (lane >= HD)
    return jnp.where(keep, pair, jnp.zeros_like(pair))


def causal(scores):
    key = lax.broadcasted_iota(jnp.int32, scores.shape, 0)
    query = lax.broadcasted_iota(jnp.int32, scores.shape, 1)
    return jnp.where(key <= query, scores, -1e30)


def mesh_place():
    fsdp = lax.axis_index("fsdp")
    return lax.axis_index("dp"), fsdp // 2, lax.rem(fsdp, 2), lax.axis_size("dp"), lax.axis_size("fsdp") // 2


def remote(src, dst, send, recv, device):
    return pltpu.make_async_remote_copy(
        src_ref=src, dst_ref=dst, send_sem=send, recv_sem=recv, device_id=device, device_id_type=MESH
    )


def meet():
    d, chip, core, dp, chips = mesh_place()
    barrier = pltpu.get_barrier_semaphore()
    for n in range(1, dp):
        pl.semaphore_signal(barrier, inc=1, device_id={"dp": lax.rem(d + n, dp)}, device_id_type=MESH)
    for n in range(1, chips):
        other = lax.rem(chip + n, chips) * 2 + core
        pl.semaphore_signal(barrier, inc=1, device_id={"fsdp": other}, device_id_type=MESH)
    pl.semaphore_signal(barrier, inc=1, device_id={"fsdp": chip * 2 + 1 - core}, device_id_type=MESH)
    pl.semaphore_wait(barrier, dp + chips - 1)


class Gather:
    def __init__(self, buf, sems):
        self.buf = buf
        self.zs, self.zr, self.xs, self.xr, self.cs, self.cr = sems
        self.d, self.chip, self.core, self.dp, self.chips = mesh_place()

    @staticmethod
    def semaphores(dp, chips):
        dma = pltpu.SemaphoreType.DMA
        return [dma((dp,)), dma((dp,)), dma((dp, chips)), dma((dp, chips)), dma((chips,)), dma((chips,))]

    def source(self, o):
        return lax.rem(self.d - o + self.dp, self.dp)

    def chip_at(self, p):
        return lax.rem(self.chip + p + self.chips, self.chips)

    def along_dp(self, o):
        block = self.buf.at[self.d, self.chip, self.core]
        to = {"dp": lax.rem(self.d + o, self.dp)}
        return remote(block, block, self.zs.at[o], self.zr.at[o], to)

    def to_chip(self, o, p):
        block = self.buf.at[self.source(o), self.chip, self.core]
        to = {"fsdp": self.chip_at(p) * 2 + self.core}
        return remote(block, block, self.xs.at[o, p], self.xr.at[o, p], to)

    def to_core(self, p):
        block = self.buf.at[:, self.chip_at(-p), self.core]
        return remote(block, block, self.cs.at[p], self.cr.at[p], {"fsdp": self.chip * 2 + 1 - self.core})

    def begin(self):
        for o in range(1, self.dp):
            self.along_dp(o).start()
        for p in range(1, self.chips):
            self.to_chip(0, p).start()

    def spread(self):
        for o in range(1, self.dp):
            self.along_dp(o).wait_recv()
            for p in range(1, self.chips):
                self.to_chip(o, p).start()
        self.to_core(0).start()

    def share(self):
        for p in range(1, self.chips):
            for o in range(self.dp):
                self.to_chip(o, p).wait_recv()
            self.to_core(p).start()

    def arrive(self):
        for p in range(self.chips):
            self.to_core(p).wait_recv()

    def close(self):
        for o in range(1, self.dp):
            self.along_dp(o).wait_send()
        for p in range(1, self.chips):
            for o in range(self.dp):
                self.to_chip(o, p).wait_send()
        for p in range(self.chips):
            self.to_core(p).wait_send()


def forward_attention(
    joined_ref, act_ref, wq_ref, wk_ref, wv_ref, wo_ref, wi_ref, w2_ref, table_ref, place_ref, line_ref,
    q_ref, qt_ref, k_ref, kt_ref, v_ref, ctx_ref, lse_ref, weight_ref, pos_ref, vec_ref, bias_ref, late_ref,
    vt_ref, ctxt_ref, early_ref, own_ref, own_sem, *sems,
):
    row = pl.program_id(0)
    rows = pl.num_programs(0)
    width = act_ref.shape[2]
    blocks = act_ref.shape[1] // WIN
    d, chip, core, dp, chips = mesh_place()
    r, c = wq_ref.shape
    held, narrow = place_ref.shape
    folds = c // narrow
    per = held // folds
    early = Gather(early_ref, sems[:6])
    late = Gather(late_ref, sems[6:])

    def own_copy():
        return pltpu.make_async_copy(own_ref, late_ref.at[d, chip, core], own_sem)

    @pl.when(row == 0)
    def _():
        for n, ref in enumerate((wq_ref, wk_ref, wv_ref)):
            early_ref[d, chip, core, n * r : (n + 1) * r, :] = ref[...]
        place = place_ref[...]
        early_ref[d, chip, core, 3 * r : 3 * r + per, :] = jnp.concatenate(
            [place[n * per : (n + 1) * per] for n in range(folds)], 1
        )
        wide = lambda x: jnp.concatenate([x, jnp.zeros((x.shape[0], c - x.shape[1]), F32)], 1)
        table = wide(table_ref[...].astype(F32))
        line = wide(line_ref[...].astype(F32))
        few = table.shape[0]
        small = jnp.concatenate([table, line, jnp.zeros((SMALL - few - 1, c), F32)], 0)
        early_ref[d, chip, core, 3 * r + per :, :] = small.astype(BF16)
        own_ref[:r, :] = wo_ref[...]
        wide_parts = wi_ref.shape[1] // c
        for n in range(wide_parts):
            own_ref[(1 + n) * r : (2 + n) * r, :] = wi_ref[:, n * c : (n + 1) * c]
        own_ref[(1 + wide_parts) * r :, :] = w2_ref[...]
        own_copy().start()
        meet()
        early.begin()
        early.spread()
        early.share()
        own_copy().wait()
        early.arrive()
        late.begin()
        for a in range(chips):
            for b in range(2):
                f = 2 * a + b
                for n in range(3):
                    weight_ref[f * r : (f + 1) * r, n * width : (n + 1) * width] = jnp.concatenate(
                        [early_ref[e, a, b, n * r : (n + 1) * r, :] for e in range(dp)], 1
                    )
        members = [(a, b) for a in range(chips) for b in range(2)]
        tables = []
        lines = []
        for e in range(dp):
            for n in range(folds):
                at = slice(e * held + n * per, e * held + (n + 1) * per)
                pos_ref[at, :] = jnp.concatenate(
                    [
                        early_ref[e, a, b, 3 * r : 3 * r + per, :][:, n * narrow : (n + 1) * narrow]
                        for a, b in members
                    ],
                    1,
                )
            smalls = [early_ref[e, a, b, 3 * r + per :, :].astype(F32) for a, b in members]
            tables.append(jnp.concatenate([x[:few, :narrow] for x in smalls], 1))
            lines.extend(x[few : few + 1, : line_ref.shape[1]] for x in smalls)
        vec_ref[...] = jnp.concatenate(tables, 0)
        bias_ref[...] = jnp.concatenate(lines, 1)

    def project(step, carry):
        at = pl.ds(pl.multiple_of(step * WIN, WIN), WIN)
        low = (act_ref[0, at, :].astype(F32) + pos_ref[at, :].astype(F32)).astype(BF16)
        every = nn(low, weight_ref[...])
        q = (every[:, :width] + vec_ref[0:1, :]).astype(BF16)
        q = (q.astype(F32) * 0.125).astype(BF16)
        k = every[:, width : 2 * width].astype(BF16)
        v = (every[:, 2 * width :] + vec_ref[1:2, :]).astype(BF16)
        q_ref[0, at, :] = q
        k_ref[0, at, :] = k
        v_ref[0, at, :] = v
        qt_ref[0, :, at] = q.T
        kt_ref[0, :, at] = k.T
        vt_ref[:, at] = v.T
        return carry

    lax.fori_loop(0, blocks, project, 0)

    @pl.when(row == 0)
    def _():
        late.spread()

    @pl.when(row == rows - 1)
    def _():
        late.share()

    def attend(block, pair, joined):
        at = pl.ds(pl.multiple_of(block * WIN, WIN), WIN)
        feats = pl.ds(pl.multiple_of(pair * PAIR, PAIR), PAIR)
        qt = qt_ref[0, feats, at]
        k_own = k_ref[0, at, feats]
        vt_own = vt_ref[feats, at]
        if joined:
            before = pl.ds(pl.multiple_of((block - 1) * WIN, WIN), WIN)
            k_prev = k_ref[0, before, feats]
            vt_prev = vt_ref[feats, before]
            apart = joined_ref[row, block]
        for which in range(2):
            half = slice(which * HD, (which + 1) * HD)
            q_head = head_rows(qt, which)
            own = causal(nn(k_own, q_head))
            peak = jnp.max(own, 0, keepdims=True)
            if joined:
                prev = nn(k_prev, q_head)
                peak = jnp.maximum(peak, jnp.max(prev, 0, keepdims=True) + apart)
            own = jnp.exp(own - peak)
            total = jnp.sum(own, 0, keepdims=True)
            out = nn(vt_own[half], own.astype(BF16))
            if joined:
                prev = jnp.exp(prev - (peak - apart))
                total = total + jnp.sum(prev, 0, keepdims=True)
                out = out + nn(vt_prev[half], prev.astype(BF16))
            ctxt_ref[half, :] = (out * (1.0 / total)).astype(BF16)
            lse_ref[0, pair, which : which + 1, at] = peak + jnp.log(total)
        ctx_ref[0, at, feats] = ctxt_ref[...].T

    def first(pair, carry):
        attend(0, pair, False)
        return carry

    def other(n, carry):
        attend(n // (H // 2) + 1, lax.rem(n, H // 2), True)
        return carry

    lax.fori_loop(0, H // 2, first, 0)
    lax.fori_loop(0, (blocks - 1) * (H // 2), other, 0)

    @pl.when(row == rows - 1)
    def _():
        late.arrive()
        early.close()
        late.close()


def backward_attention(
    joined_ref, q_ref, qt_ref, k_ref, kt_ref, v_ref, lse_ref, grad_ref, first_ref, act_ref, pos_ref, weight_ref,
    input_ref, wgrad_ref, posgrad_ref, sums_ref,
    gradt_ref, dq_ref, dk_ref, dv_ref, wacc_ref,
):
    row = pl.program_id(0)
    rows = pl.num_programs(0)
    width = act_ref.shape[2]
    blocks = act_ref.shape[1] // WIN

    def turn(step, carry):
        at = pl.ds(pl.multiple_of(step * WIN, WIN), WIN)
        gradt_ref[:, at] = grad_ref[0, at, :].T
        return carry

    lax.fori_loop(0, blocks, turn, 0)

    def attend(block, pair, joined):
        at = pl.ds(pl.multiple_of(block * WIN, WIN), WIN)
        feats = pl.ds(pl.multiple_of(pair * PAIR, PAIR), PAIR)
        before = pl.ds(pl.multiple_of(jnp.maximum(block - 1, 0) * WIN, WIN), WIN)
        qt = qt_ref[0, feats, at]
        gt = gradt_ref[feats, at]
        q = q_ref[0, at, feats]
        g = grad_ref[0, at, feats]
        places = [at, before] if joined else [at]
        probs = [[], []]
        score_grads = [[], []]
        dq_halves = []
        for which in range(2):
            half = slice(which * HD, (which + 1) * HD)
            q_head = head_rows(qt, which)
            g_head = head_rows(gt, which)
            lse = lse_ref[0, pair, which : which + 1, at]
            part = []
            inner = None
            for n, place in enumerate(places):
                s = nn(k_ref[0, place, feats], q_head)
                if n == 0:
                    s = causal(s)
                p = jnp.exp(s - lse)
                dp = nn(v_ref[0, place, feats], g_head)
                part.append((p, dp))
                term = jnp.sum(p * dp, 0, keepdims=True)
                inner = term if inner is None else inner + term
            dq = None
            for n, place in enumerate(places):
                p, dp = part[n]
                ds = (p * (dp - inner)).astype(BF16)
                probs[n if len(places) > n else 0].append(p.astype(BF16))
                score_grads[n].append(ds)
                term = nn(kt_ref[0, feats, place][half], ds)
                dq = term if dq is None else dq + term
            dq_halves.append((dq * 0.125).astype(BF16))
        dq_ref[at, feats] = jnp.concatenate(dq_halves, 0).T
        g_both = jnp.concatenate([head_lanes(g, 0), head_lanes(g, 1)], 0)
        q_both = jnp.concatenate([head_lanes(q, 0), head_lanes(q, 1)], 0)
        for n, place in enumerate(places):
            dv = nn(jnp.concatenate(probs[n], 1), g_both)
            dk = nn(jnp.concatenate(score_grads[n], 1), q_both)
            if n == 0:
                dv_ref[place, feats] = dv
                dk_ref[place, feats] = dk
            else:
                dv_ref[place, feats] += dv
                dk_ref[place, feats] += dk

    def one_block(block, carry):
        together = joined_ref[row, block] == 1

        @pl.when(together)
        def _():
            lax.fori_loop(0, H // 2, lambda p, c: (attend(block, p, True), c)[1], 0)

        @pl.when(jnp.logical_not(together))
        def _():
            lax.fori_loop(0, H // 2, lambda p, c: (attend(block, p, False), c)[1], 0)

        return carry

    lax.fori_loop(0, blocks, one_block, 0)

    @pl.when(row == 0)
    def _():
        wacc_ref[...] = jnp.zeros_like(wacc_ref)
        sums_ref[...] = jnp.zeros_like(sums_ref)
        posgrad_ref[...] = jnp.zeros_like(posgrad_ref)

    tile = 2 * WIN

    def finish(step, carry):
        at = pl.ds(pl.multiple_of(step * tile, tile), tile)
        dq = dq_ref[at, :]
        dk = dk_ref[at, :].astype(BF16)
        dv = dv_ref[at, :].astype(BF16)
        every = jnp.concatenate([dq, dk, dv], 1)
        start_grad = first_ref[0, at, :] + nt(every, weight_ref[...])
        input_ref[0, at, :] = start_grad.astype(BF16)
        posgrad_ref[at, :] += start_grad
        low = (act_ref[0, at, :].astype(F32) + pos_ref[at, :].astype(F32)).astype(BF16)
        wacc_ref[...] += nn(low.T, every)
        sums_ref[0:1, :] += column_sum(dq)
        sums_ref[1:2, :] += column_sum(dv)
        return carry

    lax.fori_loop(0, act_ref.shape[1] // tile, finish, 0)

    @pl.when(row == rows - 1)
    def _():
        wgrad_ref[...] = wacc_ref[...].astype(wgrad_ref.dtype)


def feed_forward(
    ctx_ref, act_ref, pos_ref, cot_ref, late_ref, vec_ref, bias_ref,
    out_ref, first_ref, grad_ref, wog_ref, wig_ref, w2g_ref, sums_ref, bsum_ref,
    wo_acc, wi_acc, w2_acc, slope_ref, wo_ref, wi_ref, w2_ref,
):
    step = pl.program_id(0)
    width = ctx_ref.shape[1]
    dp, chips, _, _, c = late_ref.shape
    r = width // (2 * chips)
    hidden = bias_ref.shape[1]
    part = 512

    @pl.when(step == 0)
    def _():
        wo_acc[...] = jnp.zeros_like(wo_acc)
        wi_acc[...] = jnp.zeros_like(wi_acc)
        w2_acc[...] = jnp.zeros_like(w2_acc)
        sums_ref[...] = jnp.zeros_like(sums_ref)
        bsum_ref[...] = jnp.zeros_like(bsum_ref)
        parts = hidden // dp // c
        tall = hidden // (2 * chips)

        def unpack(chip, carry):
            for core in range(2):
                f = 2 * chip + core
                at = pl.ds(pl.multiple_of(f * r, r), r)
                block = lambda e, lo, n: late_ref[e, chip, core, lo : lo + n, :]
                wo_ref[at, :] = jnp.concatenate([block(e, 0, r) for e in range(dp)], 1)
                wi_ref[at, :] = jnp.concatenate(
                    [block(e, (1 + n) * r, r) for e in range(dp) for n in range(parts)], 1
                )
                w2_ref[pl.ds(pl.multiple_of(f * tall, tall), tall), :] = jnp.concatenate(
                    [block(e, (1 + parts) * r, tall) for e in range(dp)], 1
                )
            return carry

        lax.fori_loop(0, chips, unpack, 0)

    vec = lambda n: vec_ref[n : n + 1, :]
    ctx = ctx_ref[...]
    first_sum = act_ref[...].astype(F32) + pos_ref[...].astype(F32) + (nn(ctx, wo_ref[...]) + vec(2))
    center = first_sum - jnp.mean(first_sum, -1, keepdims=True)
    scale_one = lax.rsqrt(jnp.mean(center * center, -1, keepdims=True) + 1e-05)
    z_one = center * scale_one
    normed = z_one * vec(3) + vec(4)
    normed_low = normed.astype(BF16)
    branch = None
    acts = []
    for n in range(hidden // part):
        cols = slice(n * part, (n + 1) * part)
        pre = nn(normed_low, wi_ref[:, cols]) + bias_ref[:, cols]
        square = pre * pre
        t = jnp.tanh(pre * (0.7978845608028654 + (0.7978845608028654 * 0.044715) * square))
        half = 0.5 + 0.5 * t
        act = (pre * half).astype(BF16)
        slope_ref[:, cols] = half + (0.5 * pre) * (1.0 - t * t) * (
            0.7978845608028654 + (3.0 * 0.7978845608028654 * 0.044715) * square
        )
        acts.append(act)
        term = nn(act, w2_ref[cols, :])
        branch = term if branch is None else branch + term
    second_sum = normed + (branch + vec(5))
    center = second_sum - jnp.mean(second_sum, -1, keepdims=True)
    scale_two = lax.rsqrt(jnp.mean(center * center, -1, keepdims=True) + 1e-05)
    z_two = center * scale_two
    out_ref[...] = (z_two * vec(6) + vec(7)).astype(BF16)
    cot = cot_ref[...].astype(F32)
    sums_ref[6:7, :] += column_sum(cot * z_two)
    sums_ref[7:8, :] += column_sum(cot)
    e = cot * vec(6)
    second_grad = scale_two * (
        e - jnp.mean(e, -1, keepdims=True) - z_two * jnp.mean(e * z_two, -1, keepdims=True)
    )
    branch_grad = second_grad.astype(BF16)
    sums_ref[5:6, :] += column_sum(branch_grad)
    branch_t = branch_grad.T
    normed_t = normed_low.T
    normed_grad = second_grad
    for n in range(hidden // part):
        cols = slice(n * part, (n + 1) * part)
        pre_grad = nt(branch_grad, w2_ref[cols, :]) * slope_ref[:, cols]
        pre_low = pre_grad.astype(BF16)
        w2_acc[:, cols] += nn(branch_t, acts[n])
        wi_acc[:, cols] += nn(normed_t, pre_low)
        bsum_ref[:, cols] += column_sum(pre_low)
        normed_grad = normed_grad + nt(pre_low, wi_ref[:, cols])
    sums_ref[3:4, :] += column_sum(normed_grad * z_one)
    sums_ref[4:5, :] += column_sum(normed_grad)
    e = normed_grad * vec(3)
    first_grad = scale_one * (
        e - jnp.mean(e, -1, keepdims=True) - z_one * jnp.mean(e * z_one, -1, keepdims=True)
    )
    first_ref[...] = first_grad
    attn_grad = first_grad.astype(BF16)
    sums_ref[2:3, :] += column_sum(attn_grad)
    wo_acc[...] += nn(ctx.T, attn_grad)
    grad_ref[...] = nt(attn_grad, wo_ref[...]).astype(BF16)

    @pl.when(step == pl.num_programs(0) - 1)
    def _():
        wog_ref[...] = wo_acc[...].astype(wog_ref.dtype)
        wig_ref[...] = wi_acc[...].astype(wig_ref.dtype)
        w2g_ref[...] = w2_acc[...].astype(w2g_ref.dtype)


def whole(shape):
    return pl.BlockSpec(shape, lambda *_: (0,) * len(shape))


def run_forward(apart, act, wq, wk, wv, wo, wi, w2, table, place, line):
    rows, seq, width = act.shape
    dp, fsdp = lax.axis_size("dp"), lax.axis_size("fsdp")
    chips = fsdp // 2
    r, c = wq.shape
    hidden = wi.shape[1] * dp
    first_rows = 3 * r + place.shape[0] * place.shape[1] // c + SMALL
    late_rows = r + r * wi.shape[1] // c + w2.shape[0]
    row3 = lambda shape: pl.BlockSpec((1,) + shape, lambda i: (i,) + (0,) * len(shape))
    seqs = row3((seq, width))
    turned = row3((width, seq))
    st, tt = jax.ShapeDtypeStruct((rows, seq, width), BF16), jax.ShapeDtypeStruct((rows, width, seq), BF16)
    late = (dp, chips, 2, late_rows, c)
    small = [x.shape for x in (wq, wk, wv, wo, wi, w2, table, place, line)]
    return pl.pallas_call(
        forward_attention,
        grid=(rows,),
        in_specs=[pl.BlockSpec(memory_space=pltpu.SMEM), seqs] + [whole(x) for x in small],
        out_specs=[seqs, turned, seqs, turned, seqs, seqs, row3((H // 2, 2, seq)), whole((width, 3 * width)),
                   whole((seq, width)), whole((table.shape[0] * dp, width)), whole((1, hidden)),
                   pl.BlockSpec(memory_space=pl.ANY)],
        scratch_shapes=[
            pltpu.VMEM((width, seq), BF16),
            pltpu.VMEM((PAIR, WIN), BF16),
            pltpu.VMEM((dp, chips, 2, first_rows, c), BF16),
            pltpu.VMEM((late_rows, c), BF16),
            pltpu.SemaphoreType.DMA,
        ] + Gather.semaphores(dp, chips) * 2,
        out_shape=[
            st, tt, st, tt, st, st, jax.ShapeDtypeStruct((rows, H // 2, 2, seq), F32),
            jax.ShapeDtypeStruct((width, 3 * width), BF16),
            jax.ShapeDtypeStruct((seq, width), BF16),
            jax.ShapeDtypeStruct((table.shape[0] * dp, width), F32),
            jax.ShapeDtypeStruct((1, hidden), F32),
            jax.ShapeDtypeStruct(late, BF16),
        ],
        compiler_params=pltpu.CompilerParams(
            vmem_limit_bytes=VMEM_LIMIT, collective_id=0, has_side_effects=True
        ),
        name="forward_attention",
    )(apart, act, wq, wk, wv, wo, wi, w2, table, place, line)


def run_backward(joined, q, qt, k, kt, v, lse, grad, first, act, pos, weight):
    rows, seq, width = act.shape
    row3 = lambda shape: pl.BlockSpec((1,) + shape, lambda r, *_: (r,) + (0,) * len(shape))
    seqs = row3((seq, width))
    turned = row3((width, seq))
    return pl.pallas_call(
        backward_attention,
        grid_spec=pltpu.PrefetchScalarGridSpec(
            num_scalar_prefetch=1,
            grid=(rows,),
            in_specs=[seqs, turned, seqs, turned, seqs, row3((H // 2, 2, seq)), seqs, seqs, seqs,
                      whole((seq, width)), whole((width, 3 * width))],
            out_specs=[seqs, whole((width, 3 * width)), whole((seq, width)), whole((8, width))],
            scratch_shapes=[
                pltpu.VMEM((width, seq), BF16),
                pltpu.VMEM((seq, width), BF16),
                pltpu.VMEM((seq, width), F32),
                pltpu.VMEM((seq, width), F32),
                pltpu.VMEM((width, 3 * width), F32),
            ],
        ),
        out_shape=[
            jax.ShapeDtypeStruct((rows, seq, width), BF16),
            jax.ShapeDtypeStruct((width, 3 * width), BF16),
            jax.ShapeDtypeStruct((seq, width), F32),
            jax.ShapeDtypeStruct((8, width), F32),
        ],
        compiler_params=pltpu.CompilerParams(vmem_limit_bytes=VMEM_LIMIT),
        name="backward_attention",
    )(joined, q, qt, k, kt, v, lse, grad, first, act, pos, weight)


def run_feed_forward(ctx, act, pos, cot, late, vec, bias, tile=256):
    tokens, width = ctx.shape
    seq = pos.shape[0]
    hidden = bias.shape[1]
    per_row = seq // tile
    tok = pl.BlockSpec((tile, width), lambda t: (t, 0))
    once = lambda shape: pl.BlockSpec(shape, lambda *_: (0,) * len(shape), pipeline_mode=pl.Buffered(1))
    return pl.pallas_call(
        feed_forward,
        grid=(tokens // tile,),
        in_specs=[tok, tok, pl.BlockSpec((tile, width), lambda t: (t % per_row, 0)), tok,
                  once(late.shape), whole(vec.shape), whole(bias.shape)],
        out_specs=[tok, tok, tok, whole((width, width)), whole((width, hidden)), whole((width, hidden)),
                   whole((8, width)), whole((1, hidden))],
        scratch_shapes=[
            pltpu.VMEM((width, width), F32),
            pltpu.VMEM((width, hidden), F32),
            pltpu.VMEM((width, hidden), F32),
            pltpu.VMEM((tile, hidden), F32),
            pltpu.VMEM((width, width), BF16),
            pltpu.VMEM((width, hidden), BF16),
            pltpu.VMEM((hidden, width), BF16),
        ],
        out_shape=[
            jax.ShapeDtypeStruct((tokens, width), BF16),
            jax.ShapeDtypeStruct((tokens, width), F32),
            jax.ShapeDtypeStruct((tokens, width), BF16),
            jax.ShapeDtypeStruct((width, width), BF16),
            jax.ShapeDtypeStruct((width, hidden), BF16),
            jax.ShapeDtypeStruct((width, hidden), BF16),
            jax.ShapeDtypeStruct((8, width), F32),
            jax.ShapeDtypeStruct((1, hidden), F32),
        ],
        compiler_params=pltpu.CompilerParams(vmem_limit_bytes=VMEM_LIMIT),
        name="feed_forward",
    )(ctx, act, pos, cot, late, vec, bias)


def joined_blocks(window_lengths, seq):
    bounds = jnp.cumsum(window_lengths, -1)
    starts = jnp.arange(seq // WIN, dtype=jnp.int32) * WIN
    cut = jnp.any(bounds[:, None, :] == starts[None, :, None], -1)
    return jnp.where(cut | (starts == 0)[None], 0, 1).astype(jnp.int32)


def shards(
    activations, window_lengths, query_weight, key_weight, value_weight, output_weight, inner_weight, outer_weight,
    vectors, positions, inner_bias, output_cotangent,
):
    rows, seq, width = activations.shape
    dp, fsdp = lax.axis_size("dp"), lax.axis_size("fsdp")
    both = ("dp", "fsdp")

    joined = joined_blocks(window_lengths, seq)
    apart = jnp.where(joined == 1, 0.0, -1e30).astype(F32)
    q, qt, k, kt, v, ctx, lse, weight, pos, vec, bias, late = run_forward(
        apart, activations, query_weight, key_weight, value_weight, output_weight, inner_weight, outer_weight,
        vectors, positions, inner_bias.reshape(1, -1),
    )
    c = query_weight.shape[1]
    flat = lambda x: x.reshape(rows * seq, width)
    out, first, grad, wog, wig, w2g, sums, bsum = run_feed_forward(
        flat(ctx), flat(activations), pos, flat(output_cotangent), late, vec, bias
    )
    deep = lambda x: x.reshape(rows, seq, width)
    input_grad, wgrad, posgrad, more = run_backward(
        joined, q, qt, k, kt, v, lse, deep(grad), deep(first), activations, pos, weight
    )
    sums = jnp.concatenate([more[0:2], sums[2:]], 0)

    def scatter(x):
        return lax.psum_scatter(x, both, scatter_dimension=0, tiled=True)[0].astype(F32)

    def split_columns(x, r, c):
        return x.reshape(fsdp, r, dp, c).transpose(2, 0, 1, 3).reshape(dp * fsdp, r, c)

    r = query_weight.shape[0]
    own = [scatter(split_columns(g, r, c)) for g in (wgrad[:, :width], wgrad[:, width:2 * width], wgrad[:, 2 * width:], wog)]
    own.append(scatter(split_columns(wig, *inner_weight.shape)))
    own.append(scatter(split_columns(w2g.T, *outer_weight.shape)))
    split_rows = lambda x, s: x.reshape(dp, s[0], fsdp, s[1]).transpose(0, 2, 1, 3).reshape((dp * fsdp,) + s)
    own.append(scatter(split_rows(sums, vectors.shape)))
    own.append(scatter(split_rows(posgrad, positions.shape)))
    own.append(scatter(bsum.reshape(dp * fsdp, -1)))
    return (deep(out), input_grad) + tuple(own)


def solution(mesh):
    tokens = P(("dp", "fsdp"), None, None)
    matrix = P("fsdp", "dp")
    table = P("dp", "fsdp")
    line = P(("dp", "fsdp"))
    return jax.shard_map(
        shards,
        mesh=mesh,
        in_specs=(tokens, P(("dp", "fsdp"), None)) + (matrix,) * 6 + (table, table, line, tokens),
        out_specs=(tokens, tokens) + (matrix,) * 6 + (table, table, line),
        check_vma=False,
    )
```

```python
import functools

import jax
import jax.numpy as jnp
from jax import lax
from jax.experimental import pallas as pl
from jax.experimental.pallas import tpu as pltpu
from jax.sharding import PartitionSpec as P

H = 8
HD = 64
WIN = 256
PAIR = 2 * HD
VMEM_LIMIT = 62 * 1024 * 1024
F32 = jnp.float32
BF16 = jnp.bfloat16
MESH = pl.DeviceIdType.MESH
SMALL = 16


def nn(left, right):
    return lax.dot_general(left, right, (((1,), (0,)), ((), ())), preferred_element_type=F32)


def nt(left, right):
    return lax.dot_general(left, right, (((1,), (1,)), ((), ())), preferred_element_type=F32)


def tn(left, right):
    return lax.dot_general(left, right, (((0,), (0,)), ((), ())), preferred_element_type=F32)


def column_sum(value):
    return jnp.sum(value.astype(F32), 0, keepdims=True)


def head_rows(pair, which):
    zeros = jnp.zeros((HD, pair.shape[1]), pair.dtype)
    if which == 0:
        return jnp.concatenate([pair[:HD], zeros], 0)
    return jnp.concatenate([zeros, pair[HD:]], 0)


def head_lanes(pair, which):
    lane = lax.broadcasted_iota(jnp.int32, pair.shape, 1)
    keep = (lane < HD) if which == 0 else (lane >= HD)
    return jnp.where(keep, pair, jnp.zeros_like(pair))


def causal(scores):
    key = lax.broadcasted_iota(jnp.int32, scores.shape, 0)
    query = lax.broadcasted_iota(jnp.int32, scores.shape, 1)
    return jnp.where(key <= query, scores, -1e30)


def mesh_place():
    fsdp = lax.axis_index("fsdp")
    return lax.axis_index("dp"), fsdp // 2, lax.rem(fsdp, 2), lax.axis_size("dp"), lax.axis_size("fsdp") // 2


def remote(src, dst, send, recv, device):
    return pltpu.make_async_remote_copy(
        src_ref=src, dst_ref=dst, send_sem=send, recv_sem=recv, device_id=device, device_id_type=MESH
    )


def meet():
    d, chip, core, dp, chips = mesh_place()
    barrier = pltpu.get_barrier_semaphore()
    for n in range(1, dp):
        pl.semaphore_signal(barrier, inc=1, device_id={"dp": lax.rem(d + n, dp)}, device_id_type=MESH)
    for n in range(1, chips):
        other = lax.rem(chip + n, chips) * 2 + core
        pl.semaphore_signal(barrier, inc=1, device_id={"fsdp": other}, device_id_type=MESH)
    pl.semaphore_signal(barrier, inc=1, device_id={"fsdp": chip * 2 + 1 - core}, device_id_type=MESH)
    pl.semaphore_wait(barrier, dp + chips - 1)


class Gather:
    def __init__(self, buf, sems):
        self.buf = buf
        self.zs, self.zr, self.xs, self.xr, self.cs, self.cr = sems
        self.d, self.chip, self.core, self.dp, self.chips = mesh_place()

    @staticmethod
    def semaphores(dp, chips):
        dma = pltpu.SemaphoreType.DMA
        return [dma((dp,)), dma((dp,)), dma((dp, chips)), dma((dp, chips)), dma((chips,)), dma((chips,))]

    def source(self, o):
        return lax.rem(self.d - o + self.dp, self.dp)

    def chip_at(self, p):
        return lax.rem(self.chip + p + self.chips, self.chips)

    def along_dp(self, o):
        block = self.buf.at[self.d, self.chip, self.core]
        to = {"dp": lax.rem(self.d + o, self.dp)}
        return remote(block, block, self.zs.at[o], self.zr.at[o], to)

    def to_chip(self, o, p):
        block = self.buf.at[self.source(o), self.chip, self.core]
        to = {"fsdp": self.chip_at(p) * 2 + self.core}
        return remote(block, block, self.xs.at[o, p], self.xr.at[o, p], to)

    def to_core(self, p):
        block = self.buf.at[:, self.chip_at(-p), self.core]
        return remote(block, block, self.cs.at[p], self.cr.at[p], {"fsdp": self.chip * 2 + 1 - self.core})

    def begin(self):
        for o in range(1, self.dp):
            self.along_dp(o).start()
        for p in range(1, self.chips):
            self.to_chip(0, p).start()

    def spread(self):
        for o in range(1, self.dp):
            self.along_dp(o).wait_recv()
            for p in range(1, self.chips):
                self.to_chip(o, p).start()
        self.to_core(0).start()

    def share(self):
        for p in range(1, self.chips):
            for o in range(self.dp):
                self.to_chip(o, p).wait_recv()
            self.to_core(p).start()

    def arrive(self):
        for p in range(self.chips):
            self.to_core(p).wait_recv()

    def close(self):
        for o in range(1, self.dp):
            self.along_dp(o).wait_send()
        for p in range(1, self.chips):
            for o in range(self.dp):
                self.to_chip(o, p).wait_send()
        for p in range(self.chips):
            self.to_core(p).wait_send()


class Reduce:
    def __init__(self, part, scratch):
        (self.part, (self.pair, self.plane, self.mine, self.line,
                     self.cs, self.cr, self.xs, self.xr, self.zs, self.zr)) = part, scratch
        self.d, self.chip, self.core, self.dp, self.chips = mesh_place()

    @staticmethod
    def scratch(dp, chips, rows, c):
        dma = pltpu.SemaphoreType.DMA
        return [
            pltpu.VMEM((dp, chips, rows, c), BF16),
            pltpu.VMEM((chips - 1, dp, rows, c), BF16),
            pltpu.VMEM((dp, rows, c), BF16),
            pltpu.VMEM((dp, rows, c), BF16),
            dma((chips,)), dma((chips,)), dma((chips,)), dma((chips,)), dma((dp,)), dma((dp,)),
        ]

    COUNT = 10

    def chip_at(self, p):
        return lax.rem(self.chip + p + self.chips, self.chips)

    def to_core(self, p):
        at = self.chip_at(p)
        return remote(
            self.part.at[:, at, 1 - self.core], self.pair.at[:, at], self.cs.at[p], self.cr.at[p],
            {"fsdp": self.chip * 2 + 1 - self.core},
        )

    def to_chip(self, p):
        at = self.chip_at(p)
        return remote(
            self.pair.at[:, at], self.plane.at[p - 1], self.xs.at[p], self.xr.at[p], {"fsdp": at * 2 + self.core}
        )

    def along_dp(self, o):
        to = lax.rem(self.d + o, self.dp)
        return remote(self.mine.at[to], self.line.at[o], self.zs.at[o], self.zr.at[o], {"dp": to})

    def order(self):
        return list(range(1, self.chips)) + [0]

    def begin(self):
        for p in self.order():
            self.to_core(p).start()

    def across(self):
        for p in self.order():
            at = self.chip_at(p)
            self.to_core(p).wait_recv()

            def add(e, carry):
                both = self.part[e, at, self.core].astype(F32) + self.pair[e, at].astype(F32)
                self.pair[e, at] = both.astype(BF16)
                return carry

            lax.fori_loop(0, self.dp, add, 0)
            if p:
                self.to_chip(p).start()

    def along(self):
        for p in range(1, self.chips):
            self.to_chip(p).wait_recv()

        def add(n, carry):
            e = lax.rem(self.d + 1 + n, self.dp)
            total = self.pair[e, self.chip].astype(F32)
            for p in range(1, self.chips):
                total = total + self.plane[p - 1, e].astype(F32)
            self.mine[e] = total.astype(BF16)
            return carry

        for n in range(self.dp):
            add(n, 0)
            if n < self.dp - 1:
                self.along_dp(n + 1).start()

    def result(self):
        for o in range(1, self.dp):
            self.along_dp(o).wait_recv()
        total = self.mine[self.d].astype(F32)
        for o in range(1, self.dp):
            total = total + self.line[o].astype(F32)
        return total

    def close(self):
        for p in range(self.chips):
            self.to_core(p).wait_send()
        for p in range(1, self.chips):
            self.to_chip(p).wait_send()
        for o in range(1, self.dp):
            self.along_dp(o).wait_send()


def forward_attention(
    joined_ref, act_ref, wq_ref, wk_ref, wv_ref, wo_ref, wi_ref, w2_ref, table_ref, place_ref, line_ref,
    q_ref, qt_ref, k_ref, kt_ref, v_ref, ctx_ref, lse_ref, weight_ref, pos_ref, vec_ref, bias_ref, late_ref,
    vt_ref, ctxt_ref, early_ref, own_ref, own_sem, *sems,
):
    row = pl.program_id(0)
    rows = pl.num_programs(0)
    width = act_ref.shape[2]
    blocks = act_ref.shape[1] // WIN
    d, chip, core, dp, chips = mesh_place()
    r, c = wq_ref.shape
    held, narrow = place_ref.shape
    folds = c // narrow
    per = held // folds
    early = Gather(early_ref, sems[:6])
    late = Gather(late_ref, sems[6:])

    def own_copy():
        return pltpu.make_async_copy(own_ref, late_ref.at[d, chip, core], own_sem)

    @pl.when(row == 0)
    def _():
        for n, ref in enumerate((wq_ref, wk_ref, wv_ref)):
            early_ref[d, chip, core, n * r : (n + 1) * r, :] = ref[...]
        place = place_ref[...]
        early_ref[d, chip, core, 3 * r : 3 * r + per, :] = jnp.concatenate(
            [place[n * per : (n + 1) * per] for n in range(folds)], 1
        )
        wide = lambda x: jnp.concatenate([x, jnp.zeros((x.shape[0], c - x.shape[1]), F32)], 1)
        table = wide(table_ref[...].astype(F32))
        line = wide(line_ref[...].astype(F32))
        few = table.shape[0]
        small = jnp.concatenate([table, line, jnp.zeros((SMALL - few - 1, c), F32)], 0)
        early_ref[d, chip, core, 3 * r + per :, :] = small.astype(BF16)
        own_ref[:r, :] = wo_ref[...]
        wide_parts = wi_ref.shape[1] // c
        for n in range(wide_parts):
            own_ref[(1 + n) * r : (2 + n) * r, :] = wi_ref[:, n * c : (n + 1) * c]
        own_ref[(1 + wide_parts) * r :, :] = w2_ref[...]
        own_copy().start()
        meet()
        early.begin()
        early.spread()
        early.share()
        own_copy().wait()
        early.arrive()
        late.begin()
        for a in range(chips):
            for b in range(2):
                f = 2 * a + b
                for n in range(3):
                    weight_ref[f * r : (f + 1) * r, n * width : (n + 1) * width] = jnp.concatenate(
                        [early_ref[e, a, b, n * r : (n + 1) * r, :] for e in range(dp)], 1
                    )
        members = [(a, b) for a in range(chips) for b in range(2)]
        tables = []
        lines = []
        for e in range(dp):
            for n in range(folds):
                at = slice(e * held + n * per, e * held + (n + 1) * per)
                pos_ref[at, :] = jnp.concatenate(
                    [
                        early_ref[e, a, b, 3 * r : 3 * r + per, :][:, n * narrow : (n + 1) * narrow]
                        for a, b in members
                    ],
                    1,
                )
            smalls = [early_ref[e, a, b, 3 * r + per :, :].astype(F32) for a, b in members]
            tables.append(jnp.concatenate([x[:few, :narrow] for x in smalls], 1))
            lines.extend(x[few : few + 1, : line_ref.shape[1]] for x in smalls)
        vec_ref[...] = jnp.concatenate(tables, 0)
        bias_ref[...] = jnp.concatenate(lines, 1)

    def project(step, carry):
        at = pl.ds(pl.multiple_of(step * WIN, WIN), WIN)
        low = (act_ref[0, at, :].astype(F32) + pos_ref[at, :].astype(F32)).astype(BF16)
        every = nn(low, weight_ref[...])
        q = (every[:, :width] + vec_ref[0:1, :]).astype(BF16)
        q = (q.astype(F32) * 0.125).astype(BF16)
        k = every[:, width : 2 * width].astype(BF16)
        v = (every[:, 2 * width :] + vec_ref[1:2, :]).astype(BF16)
        q_ref[0, at, :] = q
        k_ref[0, at, :] = k
        v_ref[0, at, :] = v
        qt_ref[0, :, at] = q.T
        kt_ref[0, :, at] = k.T
        vt_ref[:, at] = v.T
        return carry

    lax.fori_loop(0, blocks, project, 0)

    @pl.when(row == 0)
    def _():
        late.spread()

    @pl.when(row == rows - 1)
    def _():
        late.share()

    def attend(block, pair, joined):
        at = pl.ds(pl.multiple_of(block * WIN, WIN), WIN)
        feats = pl.ds(pl.multiple_of(pair * PAIR, PAIR), PAIR)
        qt = qt_ref[0, feats, at]
        k_own = k_ref[0, at, feats]
        vt_own = vt_ref[feats, at]
        if joined:
            before = pl.ds(pl.multiple_of((block - 1) * WIN, WIN), WIN)
            k_prev = k_ref[0, before, feats]
            vt_prev = vt_ref[feats, before]
            apart = joined_ref[row, block]
        for which in range(2):
            half = slice(which * HD, (which + 1) * HD)
            q_head = head_rows(qt, which)
            own = causal(nn(k_own, q_head))
            peak = jnp.max(own, 0, keepdims=True)
            if joined:
                prev = nn(k_prev, q_head)
                peak = jnp.maximum(peak, jnp.max(prev, 0, keepdims=True) + apart)
            own = jnp.exp(own - peak)
            total = jnp.sum(own, 0, keepdims=True)
            out = nn(vt_own[half], own.astype(BF16))
            if joined:
                prev = jnp.exp(prev - (peak - apart))
                total = total + jnp.sum(prev, 0, keepdims=True)
                out = out + nn(vt_prev[half], prev.astype(BF16))
            ctxt_ref[half, :] = (out * (1.0 / total)).astype(BF16)
            lse_ref[0, pair, which : which + 1, at] = peak + jnp.log(total)
        ctx_ref[0, at, feats] = ctxt_ref[...].T

    def first(pair, carry):
        attend(0, pair, False)
        return carry

    def other(n, carry):
        attend(n // (H // 2) + 1, lax.rem(n, H // 2), True)
        return carry

    lax.fori_loop(0, H // 2, first, 0)
    lax.fori_loop(0, (blocks - 1) * (H // 2), other, 0)

    @pl.when(row == rows - 1)
    def _():
        late.arrive()
        early.close()
        late.close()


def backward_attention(
    joined_ref, q_ref, qt_ref, k_ref, kt_ref, v_ref, lse_ref, grad_ref, first_ref, act_ref, pos_ref, weight_ref,
    late_ref, sums_ref, bsum_ref,
    input_ref, wqg_ref, wkg_ref, wvg_ref, wog_ref, wig_ref, w2g_ref, table_ref, place_ref, line_ref,
    gradt_ref, dq_ref, dk_ref, dv_ref, wacc_ref, posgrad_ref, total_ref, wpart_ref, ppart_ref, *scratch,
):
    row = pl.program_id(0)
    rows = pl.num_programs(0)
    width = act_ref.shape[2]
    blocks = act_ref.shape[1] // WIN
    d, chip, core, dp, chips = mesh_place()
    r, c = wqg_ref.shape
    held, narrow = place_ref.shape
    folds = c // narrow
    per = held // folds
    few = table_ref.shape[0]
    single = line_ref.shape[1]
    n = Reduce.COUNT
    late = Reduce(late_ref, scratch[:n])
    weights = Reduce(wpart_ref, scratch[n : 2 * n])
    places = Reduce(ppart_ref, scratch[2 * n :])
    members = [(a, b) for a in range(chips) for b in range(2)]

    @pl.when(row == 0)
    def _():
        meet()
        late.begin()

    def turn(step, carry):
        at = pl.ds(pl.multiple_of(step * WIN, WIN), WIN)
        gradt_ref[:, at] = grad_ref[0, at, :].T
        return carry

    lax.fori_loop(0, blocks, turn, 0)

    def attend(block, pair, joined):
        at = pl.ds(pl.multiple_of(block * WIN, WIN), WIN)
        feats = pl.ds(pl.multiple_of(pair * PAIR, PAIR), PAIR)
        qt = qt_ref[0, feats, at]
        gt = gradt_ref[feats, at]
        q = q_ref[0, at, feats]
        g = grad_ref[0, at, feats]
        spots = [at]
        if joined:
            spots.append(pl.ds(pl.multiple_of((block - 1) * WIN, WIN), WIN))
            apart = joined_ref[row, block]
        probs = [[], []]
        score_grads = [[], []]
        dq_halves = []
        for which in range(2):
            half = slice(which * HD, (which + 1) * HD)
            q_head = head_rows(qt, which)
            g_head = head_rows(gt, which)
            lse = lse_ref[0, pair, which : which + 1, at]
            part = []
            inner = None
            for n, spot in enumerate(spots):
                s = nn(k_ref[0, spot, feats], q_head)
                if n == 0:
                    p = jnp.exp(causal(s) - lse)
                else:
                    p = jnp.exp(s - (lse - apart))
                dp_ = nn(v_ref[0, spot, feats], g_head)
                part.append((p, dp_))
                term = jnp.sum(p * dp_, 0, keepdims=True)
                inner = term if inner is None else inner + term
            dq = None
            for n, spot in enumerate(spots):
                p, dp_ = part[n]
                ds = (p * (dp_ - inner)).astype(BF16)
                probs[n].append(p.astype(BF16))
                score_grads[n].append(ds)
                term = nn(kt_ref[0, feats, spot][half], ds)
                dq = term if dq is None else dq + term
            dq_halves.append((dq * 0.125).astype(BF16))
        dq_ref[at, feats] = jnp.concatenate(dq_halves, 0).T
        g_both = jnp.concatenate([head_lanes(g, 0), head_lanes(g, 1)], 0)
        q_both = jnp.concatenate([head_lanes(q, 0), head_lanes(q, 1)], 0)
        for n, spot in enumerate(spots):
            dv = nn(jnp.concatenate(probs[n], 1), g_both)
            dk = nn(jnp.concatenate(score_grads[n], 1), q_both)
            if n == 0:
                dv_ref[spot, feats] = dv
                dk_ref[spot, feats] = dk
            else:
                dv_ref[spot, feats] += dv
                dk_ref[spot, feats] += dk

    def first(pair, carry):
        attend(0, pair, False)
        return carry

    def other(n, carry):
        attend(n // (H // 2) + 1, lax.rem(n, H // 2), True)
        return carry

    lax.fori_loop(0, H // 2, first, 0)

    @pl.when(row == 0)
    def _():
        late.across()

    @pl.when(row == rows - 1)
    def _():
        late.along()

    lax.fori_loop(0, (blocks - 1) * (H // 2), other, 0)

    @pl.when(row == 0)
    def _():
        wacc_ref[...] = jnp.zeros_like(wacc_ref)
        total_ref[...] = sums_ref[...]
        posgrad_ref[...] = jnp.zeros_like(posgrad_ref)

    tile = 2 * WIN
    tiles = act_ref.shape[1] // tile

    def gather_tile(step, carry):
        at = pl.ds(pl.multiple_of(step * tile, tile), tile)
        dq = dq_ref[at, :]
        dk = dk_ref[at, :].astype(BF16)
        dv = dv_ref[at, :].astype(BF16)
        every = jnp.concatenate([dq, dk, dv], 1)
        low = (act_ref[0, at, :].astype(F32) + pos_ref[at, :].astype(F32)).astype(BF16)
        wacc_ref[...] += nn(low.T, every)
        total_ref[0:1, :] += column_sum(dq)
        total_ref[1:2, :] += column_sum(dv)
        return carry

    lax.fori_loop(0, tiles, gather_tile, 0)

    @pl.when(row == rows - 1)
    def _():
        packed = jnp.zeros((SMALL - few - 1, c), F32)
        wide = lambda x: jnp.concatenate([x, jnp.zeros((x.shape[0], c - x.shape[1]), F32)], 1)
        for e in range(dp):
            for f, (a, b) in enumerate(members):
                for n in range(3):
                    lanes = slice(n * width + e * c, n * width + (e + 1) * c)
                    wpart_ref[e, a, b, n * r : (n + 1) * r, :] = wacc_ref[f * r : (f + 1) * r, lanes].astype(BF16)
                table = total_ref[e * few : (e + 1) * few, f * narrow : (f + 1) * narrow]
                spot = (e * len(members) + f) * single
                line = bsum_ref[:, spot : spot + single]
                wpart_ref[e, a, b, 3 * r :, :] = jnp.concatenate([wide(table), wide(line), packed], 0).astype(BF16)
        weights.begin()

    def spread_tile(step, carry):
        at = pl.ds(pl.multiple_of(step * tile, tile), tile)
        every = jnp.concatenate([dq_ref[at, :], dk_ref[at, :].astype(BF16), dv_ref[at, :].astype(BF16)], 1)
        start_grad = first_ref[0, at, :] + nt(every, weight_ref[...])
        input_ref[0, at, :] = start_grad.astype(BF16)
        posgrad_ref[at, :] += start_grad
        return carry

    lax.fori_loop(0, tiles, spread_tile, 0)

    @pl.when(row == rows - 1)
    def _():
        weights.across()
        for e in range(dp):
            for f, (a, b) in enumerate(members):
                lanes = slice(f * narrow, (f + 1) * narrow)
                ppart_ref[e, a, b] = jnp.concatenate(
                    [
                        posgrad_ref[e * held + n * per : e * held + (n + 1) * per, lanes].astype(BF16)
                        for n in range(folds)
                    ],
                    1,
                )
        places.begin()
        owned = late.result()
        wide_parts = wig_ref.shape[1] // c
        wog_ref[...] = owned[:r]
        for n in range(wide_parts):
            wig_ref[:, n * c : (n + 1) * c] = owned[(1 + n) * r : (2 + n) * r]
        w2g_ref[...] = owned[(1 + wide_parts) * r :]
        places.across()
        weights.along()
        places.along()
        owned = weights.result()
        for n, ref in enumerate((wqg_ref, wkg_ref, wvg_ref)):
            ref[...] = owned[n * r : (n + 1) * r]
        table_ref[...] = owned[3 * r : 3 * r + few, :narrow]
        line_ref[...] = owned[3 * r + few : 3 * r + few + 1, :single]
        owned = places.result()
        for n in range(folds):
            place_ref[n * per : (n + 1) * per, :] = owned[:, n * narrow : (n + 1) * narrow]
        late.close()
        weights.close()
        places.close()


def feed_forward(
    ctx_ref, act_ref, pos_ref, cot_ref, late_ref, vec_ref, bias_ref,
    out_ref, first_ref, grad_ref, part_ref, sums_ref, bsum_ref,
    wo_acc, wi_acc, w2_acc, slope_ref, wo_ref, wi_ref, w2_ref,
):
    step = pl.program_id(0)
    width = ctx_ref.shape[1]
    dp, chips, _, _, c = late_ref.shape
    r = width // (2 * chips)
    parts = bias_ref.shape[1] // dp // c
    tall = bias_ref.shape[1] // (2 * chips)
    hidden = bias_ref.shape[1]
    part = 512

    @pl.when(step == 0)
    def _():
        wo_acc[...] = jnp.zeros_like(wo_acc)
        wi_acc[...] = jnp.zeros_like(wi_acc)
        w2_acc[...] = jnp.zeros_like(w2_acc)
        sums_ref[...] = jnp.zeros_like(sums_ref)
        bsum_ref[...] = jnp.zeros_like(bsum_ref)

        def unpack(chip, carry):
            for core in range(2):
                f = 2 * chip + core
                at = pl.ds(pl.multiple_of(f * r, r), r)
                block = lambda e, lo, n: late_ref[e, chip, core, lo : lo + n, :]
                wo_ref[at, :] = jnp.concatenate([block(e, 0, r) for e in range(dp)], 1)
                wi_ref[at, :] = jnp.concatenate(
                    [block(e, (1 + n) * r, r) for e in range(dp) for n in range(parts)], 1
                )
                w2_ref[pl.ds(pl.multiple_of(f * tall, tall), tall), :] = jnp.concatenate(
                    [block(e, (1 + parts) * r, tall) for e in range(dp)], 1
                )
            return carry

        lax.fori_loop(0, chips, unpack, 0)

    vec = lambda n: vec_ref[n : n + 1, :]
    ctx = ctx_ref[...]
    first_sum = act_ref[...].astype(F32) + pos_ref[...].astype(F32) + (nn(ctx, wo_ref[...]) + vec(2))
    center = first_sum - jnp.mean(first_sum, -1, keepdims=True)
    scale_one = lax.rsqrt(jnp.mean(center * center, -1, keepdims=True) + 1e-05)
    z_one = center * scale_one
    normed = z_one * vec(3) + vec(4)
    normed_low = normed.astype(BF16)
    branch = None
    acts = []
    for n in range(hidden // part):
        cols = slice(n * part, (n + 1) * part)
        pre = nn(normed_low, wi_ref[:, cols]) + bias_ref[:, cols]
        square = pre * pre
        t = jnp.tanh(pre * (0.7978845608028654 + (0.7978845608028654 * 0.044715) * square))
        half = 0.5 + 0.5 * t
        act = (pre * half).astype(BF16)
        slope_ref[:, cols] = half + (0.5 * pre) * (1.0 - t * t) * (
            0.7978845608028654 + (3.0 * 0.7978845608028654 * 0.044715) * square
        )
        acts.append(act)
        term = nn(act, w2_ref[cols, :])
        branch = term if branch is None else branch + term
    second_sum = normed + (branch + vec(5))
    center = second_sum - jnp.mean(second_sum, -1, keepdims=True)
    scale_two = lax.rsqrt(jnp.mean(center * center, -1, keepdims=True) + 1e-05)
    z_two = center * scale_two
    out_ref[...] = (z_two * vec(6) + vec(7)).astype(BF16)
    cot = cot_ref[...].astype(F32)
    sums_ref[6:7, :] += column_sum(cot * z_two)
    sums_ref[7:8, :] += column_sum(cot)
    e = cot * vec(6)
    second_grad = scale_two * (
        e - jnp.mean(e, -1, keepdims=True) - z_two * jnp.mean(e * z_two, -1, keepdims=True)
    )
    branch_grad = second_grad.astype(BF16)
    sums_ref[5:6, :] += column_sum(branch_grad)
    branch_t = branch_grad.T
    normed_t = normed_low.T
    normed_grad = second_grad
    for n in range(hidden // part):
        cols = slice(n * part, (n + 1) * part)
        pre_grad = nt(branch_grad, w2_ref[cols, :]) * slope_ref[:, cols]
        pre_low = pre_grad.astype(BF16)
        w2_acc[:, cols] += nn(branch_t, acts[n])
        wi_acc[:, cols] += nn(normed_t, pre_low)
        bsum_ref[:, cols] += column_sum(pre_low)
        normed_grad = normed_grad + nt(pre_low, wi_ref[:, cols])
    sums_ref[3:4, :] += column_sum(normed_grad * z_one)
    sums_ref[4:5, :] += column_sum(normed_grad)
    e = normed_grad * vec(3)
    first_grad = scale_one * (
        e - jnp.mean(e, -1, keepdims=True) - z_one * jnp.mean(e * z_one, -1, keepdims=True)
    )
    first_ref[...] = first_grad
    attn_grad = first_grad.astype(BF16)
    sums_ref[2:3, :] += column_sum(attn_grad)
    wo_acc[...] += nn(ctx.T, attn_grad)
    grad_ref[...] = nt(attn_grad, wo_ref[...]).astype(BF16)

    @pl.when(step == pl.num_programs(0) - 1)
    def _():
        for e in range(dp):
            lanes = slice(e * c, (e + 1) * c)
            for f in range(2 * chips):
                rows = slice(f * r, (f + 1) * r)
                a, b = f // 2, f % 2
                part_ref[e, a, b, :r, :] = wo_acc[rows, lanes].astype(BF16)
                for n in range(parts):
                    wide = slice((e * parts + n) * c, (e * parts + n + 1) * c)
                    part_ref[e, a, b, (1 + n) * r : (2 + n) * r, :] = wi_acc[rows, wide].astype(BF16)
                turned = w2_acc[lanes, f * tall : (f + 1) * tall].astype(BF16)
                part_ref[e, a, b, (1 + parts) * r :, :] = turned.T


def whole(shape):
    return pl.BlockSpec(shape, lambda *_: (0,) * len(shape))


def once(shape):
    return pl.BlockSpec(shape, lambda *_: (0,) * len(shape), pipeline_mode=pl.Buffered(1))


def run_forward(apart, act, wq, wk, wv, wo, wi, w2, table, place, line):
    rows, seq, width = act.shape
    dp, fsdp = lax.axis_size("dp"), lax.axis_size("fsdp")
    chips = fsdp // 2
    r, c = wq.shape
    hidden = wi.shape[1] * dp
    first_rows = 3 * r + place.shape[0] * place.shape[1] // c + SMALL
    late_rows = r + r * wi.shape[1] // c + w2.shape[0]
    row3 = lambda shape: pl.BlockSpec((1,) + shape, lambda i: (i,) + (0,) * len(shape))
    seqs = row3((seq, width))
    turned = row3((width, seq))
    st, tt = jax.ShapeDtypeStruct((rows, seq, width), BF16), jax.ShapeDtypeStruct((rows, width, seq), BF16)
    late = (dp, chips, 2, late_rows, c)
    small = [x.shape for x in (wq, wk, wv, wo, wi, w2, table, place, line)]
    return pl.pallas_call(
        forward_attention,
        grid=(rows,),
        in_specs=[pl.BlockSpec(memory_space=pltpu.SMEM), seqs] + [whole(x) for x in small],
        out_specs=[seqs, turned, seqs, turned, seqs, seqs, row3((H // 2, 2, seq)), whole((width, 3 * width)),
                   whole((seq, width)), whole((table.shape[0] * dp, width)), whole((1, hidden)),
                   pl.BlockSpec(memory_space=pl.ANY)],
        scratch_shapes=[
            pltpu.VMEM((width, seq), BF16),
            pltpu.VMEM((PAIR, WIN), BF16),
            pltpu.VMEM((dp, chips, 2, first_rows, c), BF16),
            pltpu.VMEM((late_rows, c), BF16),
            pltpu.SemaphoreType.DMA,
        ] + Gather.semaphores(dp, chips) * 2,
        out_shape=[
            st, tt, st, tt, st, st, jax.ShapeDtypeStruct((rows, H // 2, 2, seq), F32),
            jax.ShapeDtypeStruct((width, 3 * width), BF16),
            jax.ShapeDtypeStruct((seq, width), BF16),
            jax.ShapeDtypeStruct((table.shape[0] * dp, width), F32),
            jax.ShapeDtypeStruct((1, hidden), F32),
            jax.ShapeDtypeStruct(late, BF16),
        ],
        compiler_params=pltpu.CompilerParams(
            vmem_limit_bytes=VMEM_LIMIT, collective_id=0, has_side_effects=True
        ),
        name="forward_attention",
    )(apart, act, wq, wk, wv, wo, wi, w2, table, place, line)


def run_backward(apart, q, qt, k, kt, v, lse, grad, first, act, pos, weight, late, sums, bsum, shapes):
    rows, seq, width = act.shape
    dp, fsdp = lax.axis_size("dp"), lax.axis_size("fsdp")
    chips = fsdp // 2
    r, c = shapes[0]
    held, narrow = shapes[7]
    first_rows = 3 * r + SMALL
    place_rows = held * narrow // c
    row3 = lambda shape: pl.BlockSpec((1,) + shape, lambda i: (i,) + (0,) * len(shape))
    seqs = row3((seq, width))
    turned = row3((width, seq))
    lone = pl.BlockSpec((1, seq, width), lambda i: (i, 0, 0), pipeline_mode=pl.Buffered(1))
    return pl.pallas_call(
        backward_attention,
        grid=(rows,),
        in_specs=[pl.BlockSpec(memory_space=pltpu.SMEM), seqs, turned, seqs, turned, seqs,
                  row3((H // 2, 2, seq)), lone, lone, lone, once(pos.shape), once(weight.shape), once(late.shape),
                  once(sums.shape), once(bsum.shape)],
        out_specs=[seqs] + [whole(x) for x in shapes],
        scratch_shapes=[
            pltpu.VMEM((width, seq), BF16),
            pltpu.VMEM((seq, width), BF16),
            pltpu.VMEM((seq, width), F32),
            pltpu.VMEM((seq, width), F32),
            pltpu.VMEM((width, 3 * width), F32),
            pltpu.VMEM((seq, width), F32),
            pltpu.VMEM((8, width), F32),
            pltpu.VMEM((dp, chips, 2, first_rows, c), BF16),
            pltpu.VMEM((dp, chips, 2, place_rows, c), BF16),
        ]
        + Reduce.scratch(dp, chips, late.shape[3], c)
        + Reduce.scratch(dp, chips, first_rows, c)
        + Reduce.scratch(dp, chips, place_rows, c),
        out_shape=[jax.ShapeDtypeStruct((rows, seq, width), BF16)] + [jax.ShapeDtypeStruct(x, F32) for x in shapes],
        compiler_params=pltpu.CompilerParams(
            vmem_limit_bytes=VMEM_LIMIT, collective_id=1, has_side_effects=True
        ),
        name="backward_attention",
    )(apart, q, qt, k, kt, v, lse, grad, first, act, pos, weight, late, sums, bsum)


def run_feed_forward(ctx, act, pos, cot, late, vec, bias, tile=256):
    tokens, width = ctx.shape
    seq = pos.shape[0]
    hidden = bias.shape[1]
    per_row = seq // tile
    tok = pl.BlockSpec((tile, width), lambda t: (t, 0))
    return pl.pallas_call(
        feed_forward,
        grid=(tokens // tile,),
        in_specs=[tok, tok, pl.BlockSpec((tile, width), lambda t: (t % per_row, 0)), tok,
                  once(late.shape), whole(vec.shape), whole(bias.shape)],
        out_specs=[tok, tok, tok, whole(late.shape), whole((8, width)), whole((1, hidden))],
        scratch_shapes=[
            pltpu.VMEM((width, width), F32),
            pltpu.VMEM((width, hidden), F32),
            pltpu.VMEM((width, hidden), F32),
            pltpu.VMEM((tile, hidden), F32),
            pltpu.VMEM((width, width), BF16),
            pltpu.VMEM((width, hidden), BF16),
            pltpu.VMEM((hidden, width), BF16),
        ],
        out_shape=[
            jax.ShapeDtypeStruct((tokens, width), BF16),
            jax.ShapeDtypeStruct((tokens, width), F32),
            jax.ShapeDtypeStruct((tokens, width), BF16),
            jax.ShapeDtypeStruct(late.shape, BF16),
            jax.ShapeDtypeStruct((8, width), F32),
            jax.ShapeDtypeStruct((1, hidden), F32),
        ],
        compiler_params=pltpu.CompilerParams(vmem_limit_bytes=VMEM_LIMIT),
        name="feed_forward",
    )(ctx, act, pos, cot, late, vec, bias)


def joined_blocks(window_lengths, seq):
    bounds = jnp.cumsum(window_lengths, -1)
    starts = jnp.arange(seq // WIN, dtype=jnp.int32) * WIN
    cut = jnp.any(bounds[:, None, :] == starts[None, :, None], -1)
    return jnp.where(cut | (starts == 0)[None], 0, 1).astype(jnp.int32)


def shards(
    activations, window_lengths, query_weight, key_weight, value_weight, output_weight, inner_weight, outer_weight,
    vectors, positions, inner_bias, output_cotangent,
):
    rows, seq, width = activations.shape
    joined = joined_blocks(window_lengths, seq)
    apart = jnp.where(joined == 1, 0.0, -1e30).astype(F32)
    q, qt, k, kt, v, ctx, lse, weight, pos, vec, bias, late = run_forward(
        apart, activations, query_weight, key_weight, value_weight, output_weight, inner_weight, outer_weight,
        vectors, positions, inner_bias.reshape(1, -1),
    )
    flat = lambda x: x.reshape(rows * seq, width)
    deep = lambda x: x.reshape(rows, seq, width)
    out, first, grad, part, sums, bsum = run_feed_forward(
        flat(ctx), flat(activations), pos, flat(output_cotangent), late, vec, bias
    )
    shapes = [x.shape for x in (query_weight, key_weight, value_weight, output_weight, inner_weight, outer_weight,
                                vectors, positions)] + [(1, inner_bias.shape[0])]
    input_grad, *owned = run_backward(
        apart, q, qt, k, kt, v, lse, deep(grad), deep(first), activations, pos, weight, part, sums, bsum, shapes
    )
    owned[8] = owned[8].reshape(-1)
    return (deep(out), input_grad) + tuple(owned)


def solution(mesh):
    tokens = P(("dp", "fsdp"), None, None)
    matrix = P("fsdp", "dp")
    table = P("dp", "fsdp")
    line = P(("dp", "fsdp"))
    return jax.shard_map(
        shards,
        mesh=mesh,
        in_specs=(tokens, P(("dp", "fsdp"), None)) + (matrix,) * 6 + (table, table, line, tokens),
        out_specs=(tokens, tokens) + (matrix,) * 6 + (table, table, line),
        check_vma=False,
    )
```

```python
import functools

import jax
import jax.numpy as jnp
from jax import lax
from jax.experimental import pallas as pl
from jax.experimental.pallas import tpu as pltpu
from jax.sharding import PartitionSpec as P

H = 8
HD = 64
WIN = 256
PAIR = 2 * HD
VMEM_LIMIT = 62 * 1024 * 1024
F32 = jnp.float32
BF16 = jnp.bfloat16
MESH = pl.DeviceIdType.MESH
SMALL = 16


def nn(left, right):
    return lax.dot_general(left, right, (((1,), (0,)), ((), ())), preferred_element_type=F32)


def nt(left, right):
    return lax.dot_general(left, right, (((1,), (1,)), ((), ())), preferred_element_type=F32)


def tn(left, right):
    return lax.dot_general(left, right, (((0,), (0,)), ((), ())), preferred_element_type=F32)


def column_sum(value):
    return jnp.sum(value.astype(F32), 0, keepdims=True)


def head_rows(pair, which):
    zeros = jnp.zeros((HD, pair.shape[1]), pair.dtype)
    if which == 0:
        return jnp.concatenate([pair[:HD], zeros], 0)
    return jnp.concatenate([zeros, pair[HD:]], 0)


def head_lanes(pair, which):
    lane = lax.broadcasted_iota(jnp.int32, pair.shape, 1)
    keep = (lane < HD) if which == 0 else (lane >= HD)
    return jnp.where(keep, pair, jnp.zeros_like(pair))


def causal(scores):
    key = lax.broadcasted_iota(jnp.int32, scores.shape, 0)
    query = lax.broadcasted_iota(jnp.int32, scores.shape, 1)
    return jnp.where(key <= query, scores, -1e30)


def block_of(block):
    return slice(block * WIN, (block + 1) * WIN)


def spots_of(block):
    return [block_of(n) for n in (block, block - 1) if n >= 0]


def pair_of(head):
    return slice(head // 2 * PAIR, (head // 2 + 1) * PAIR)


def staggered(tasks, stages):
    held = {}
    for step in range(len(tasks) + len(stages) - 1):
        for n, stage in enumerate(stages):
            task = step - n
            if 0 <= task < len(tasks):
                args = (held.pop(task),) if n else ()
                held[task] = stage(*tasks[task], *args)


class Place:
    def __init__(self):
        fsdp = lax.axis_index("fsdp")
        self.d, self.dp = lax.axis_index("dp"), lax.axis_size("dp")
        self.side = side_of(lax.axis_size("fsdp"))
        self.chip, self.core = fsdp // 2, lax.rem(fsdp, 2)
        y, x = self.chip // self.side, lax.rem(self.chip, self.side)
        self.a = y + self.core * (x - y)
        self.b = x + self.core * (y - x)

    def device(self, a, b):
        straight, turned = a * self.side + b, b * self.side + a
        return {"fsdp": (straight + self.core * (turned - straight)) * 2 + self.core}

    def sibling(self):
        return {"fsdp": self.chip * 2 + 1 - self.core}

    def at_a(self, n):
        return lax.rem(self.a + n + self.side, self.side)

    def at_b(self, n):
        return lax.rem(self.b + n + self.side, self.side)

    def at_dp(self, n):
        return lax.rem(self.d + n + self.dp, self.dp)


def side_of(fsdp):
    side = 1
    while side * side * 2 < fsdp:
        side += 1
    assert side * side * 2 == fsdp
    return side


def members(side):
    found = []
    for f in range(2 * side * side):
        y, x = f // 2 // side, f // 2 % side
        found.append((x, y, 1) if f % 2 else (y, x, 0))
    return found


def remote(src, dst, send, recv, device):
    return pltpu.make_async_remote_copy(
        src_ref=src, dst_ref=dst, send_sem=send, recv_sem=recv, device_id=device, device_id_type=MESH
    )


def meet(at):
    barrier = pltpu.get_barrier_semaphore()
    others = [{"dp": at.at_dp(n)} for n in range(1, at.dp)]
    others += [at.device(at.a, at.at_b(n)) for n in range(1, at.side)]
    others += [at.device(at.at_a(n), at.b) for n in range(1, at.side)]
    others.append(at.sibling())
    for other in others:
        pl.semaphore_signal(barrier, inc=1, device_id=other, device_id_type=MESH)
    pl.semaphore_wait(barrier, len(others))


class Gather:
    COUNT = 8

    def __init__(self, buf, sems, at):
        self.buf, self.at = buf, at
        self.zs, self.zr, self.bs, self.br, self.sa, self.ra, self.cs, self.cr = sems

    @staticmethod
    def semaphores(dp, side):
        dma = pltpu.SemaphoreType.DMA
        shapes = [(dp,), (dp, side), (dp, side, side), (side, side)]
        return [dma(x) for x in shapes for _ in range(2)]

    def along_dp(self, o):
        at = self.at
        block = self.buf.at[at.d, at.a, at.b, at.core]
        return remote(block, block, self.zs.at[o], self.zr.at[o], {"dp": at.at_dp(o)})

    def along_b(self, o, p):
        at = self.at
        block = self.buf.at[at.at_dp(-o), at.a, at.b, at.core]
        return remote(block, block, self.bs.at[o, p], self.br.at[o, p], at.device(at.a, at.at_b(p)))

    def along_a(self, o, p, q):
        at = self.at
        block = self.buf.at[at.at_dp(-o), at.a, at.at_b(-p), at.core]
        return remote(block, block, self.sa.at[o, p, q], self.ra.at[o, p, q], at.device(at.at_a(q), at.b))

    def to_core(self, q, p):
        at = self.at
        block = self.buf.at[:, at.at_a(-q), at.at_b(-p), at.core]
        return remote(block, block, self.cs.at[q, p], self.cr.at[q, p], at.sibling())

    def begin(self):
        for o in range(1, self.at.dp):
            self.along_dp(o).start()
        self.pass_on(0)

    def pass_on(self, o):
        for p in range(1, self.at.side):
            self.along_b(o, p).start()
        for q in range(1, self.at.side):
            self.along_a(o, 0, q).start()

    def spread(self, o):
        self.along_dp(o).wait_recv()
        self.pass_on(o)

    def relay(self, o):
        for p in range(1, self.at.side):
            self.along_b(o, p).wait_recv()
            for q in range(1, self.at.side):
                self.along_a(o, p, q).start()

    def near(self):
        for p in range(self.at.side):
            self.to_core(0, p).start()

    def share(self):
        for p in range(self.at.side):
            for q in range(1, self.at.side):
                for o in range(self.at.dp):
                    self.along_a(o, p, q).wait_recv()
                self.to_core(q, p).start()

    def arrive(self):
        for q in range(self.at.side):
            for p in range(self.at.side):
                self.to_core(q, p).wait_recv()

    def close(self):
        for o in range(1, self.at.dp):
            self.along_dp(o).wait_send()
        for o in range(self.at.dp):
            for p in range(1, self.at.side):
                self.along_b(o, p).wait_send()
            for p in range(self.at.side):
                for q in range(1, self.at.side):
                    self.along_a(o, p, q).wait_send()
        for q in range(self.at.side):
            for p in range(self.at.side):
                self.to_core(q, p).wait_send()


def add_up(terms):
    if len(terms) == 2:
        return terms[0] + terms[1]
    return sum(x.astype(F32) for x in terms).astype(BF16)


class Reduce:
    COUNT = 13

    def __init__(self, part, scratch, at, own=None):
        self.part, self.at = part, at
        self.own, self.own_sem = own or (None, None)
        (self.pair, self.plane, self.row, self.mine, self.line,
         self.cs, self.cr, self.sa, self.ra, self.bs, self.br, self.zs, self.zr) = scratch

    @staticmethod
    def scratch(dp, side, rows, c):
        dma = pltpu.SemaphoreType.DMA
        return [
            pltpu.VMEM((dp, side, side, rows, c), BF16),
            pltpu.VMEM((side - 1, dp, side, rows, c), BF16),
            pltpu.VMEM((side - 1, dp, rows, c), BF16),
            pltpu.VMEM((dp, rows, c), BF16),
            pltpu.VMEM((dp - 1, rows, c), BF16),
        ] + [dma((dp,))] * 2 + [dma((dp, side))] * 4 + [dma((dp,))] * 2

    def to_core(self, e):
        at = self.at
        return remote(self.part.at[e, :, :, 1 - at.core], self.pair.at[e], self.cs.at[e], self.cr.at[e], at.sibling())

    def along_a(self, e, q):
        at = self.at
        to = at.at_a(q)
        return remote(
            self.pair.at[e, to], self.plane.at[q - 1, e], self.sa.at[e, q], self.ra.at[e, q], at.device(to, at.b)
        )

    def along_b(self, e, p):
        at = self.at
        to = at.at_b(p)
        return remote(
            self.pair.at[e, at.a, to], self.row.at[p - 1, e], self.bs.at[e, p], self.br.at[e, p], at.device(at.a, to)
        )

    def along_dp(self, o):
        at = self.at
        to = at.at_dp(o)
        return remote(self.mine.at[to], self.line.at[o - 1], self.zs.at[o], self.zr.at[o], {"dp": to})

    def own_half(self):
        return pltpu.make_async_copy(self.part.at[:, :, :, self.at.core], self.own, self.own_sem)

    def begin(self, e):
        self.to_core(e).start()

    def across(self, e):
        at = self.at
        self.to_core(e).wait_recv()
        for n in list(range(1, at.side)) + [0]:
            a = at.at_a(n)
            for b in range(at.side):
                own = self.part[e, a, b, at.core] if self.own is None else self.own[e, a, b]
                self.pair[e, a, b] = add_up([own, self.pair[e, a, b]])
            if n:
                self.along_a(e, n).start()

    def middle(self, e):
        at = self.at
        for q in range(1, at.side):
            self.along_a(e, q).wait_recv()
        for n in list(range(1, at.side)) + [0]:
            b = at.at_b(n)
            terms = [self.pair[e, at.a, b]] + [self.plane[q - 1, e, b] for q in range(1, at.side)]
            self.pair[e, at.a, b] = add_up(terms)
            if n:
                self.along_b(e, n).start()

    def along(self, e):
        at = self.at
        for p in range(1, at.side):
            self.along_b(e, p).wait_recv()
        self.mine[e] = add_up([self.pair[e, at.a, at.b]] + [self.row[p - 1, e] for p in range(1, at.side)])

        @pl.when(e != at.d)
        def _():
            self.along_dp(lax.rem(e - at.d + at.dp, at.dp)).start()

    def result(self):
        at = self.at
        for o in range(1, at.dp):
            self.along_dp(o).wait_recv()
        total = self.mine[at.d].astype(F32)
        for o in range(1, at.dp):
            total = total + self.line[o - 1].astype(F32)
        return total

    def close(self):
        at = self.at
        for e in range(at.dp):
            self.to_core(e).wait_send()
            for n in range(1, at.side):
                self.along_a(e, n).wait_send()
                self.along_b(e, n).wait_send()
        for o in range(1, at.dp):
            self.along_dp(o).wait_send()


def apart(lengths_ref, row, block):
    total = jnp.int32(0)
    cut = jnp.bool_(False)
    for n in range(lengths_ref.shape[1]):
        total = total + lengths_ref[row, n]
        cut = cut | (total == block * WIN)
    return jnp.where(cut, jnp.float32(-1e30), jnp.float32(0.0))


def forward_attention(
    lengths_ref, act_ref, wq_ref, wk_ref, wv_ref, wo_ref, wi_ref, w2_ref, table_ref, place_ref, line_ref,
    q_ref, qt_ref, k_ref, kt_ref, v_ref, ctx_ref, lse_ref, weight_ref, pos_ref, vec_ref, bias_ref, late_ref,
    vt_ref, ctxt_ref, early_ref, own_ref, own_sem, *sems,
):
    row = pl.program_id(0)
    rows = pl.num_programs(0)
    width = act_ref.shape[2]
    blocks = act_ref.shape[1] // WIN
    at = Place()
    dp = at.dp
    here = (at.d, at.a, at.b, at.core)
    r, c = wq_ref.shape
    narrow, held = place_ref.shape
    folds = c // narrow
    per = held // folds
    early = Gather(early_ref, sems[: Gather.COUNT], at)
    late = Gather(late_ref, sems[Gather.COUNT :], at)

    def own_copy():
        return pltpu.make_async_copy(own_ref, late_ref.at[here], own_sem)

    @pl.when(row == 0)
    def _():
        for n, ref in enumerate((wq_ref, wk_ref, wv_ref)):
            early_ref[here + (slice(n * r, (n + 1) * r),)] = ref[...]
        place = place_ref[...].T
        early_ref[here + (slice(3 * r, 3 * r + per),)] = jnp.concatenate(
            [place[n * per : (n + 1) * per] for n in range(folds)], 1
        )
        wide = lambda x: jnp.concatenate([x, jnp.zeros((x.shape[0], c - x.shape[1]), F32)], 1)
        table = wide(table_ref[...].astype(F32))
        line = wide(line_ref[...].astype(F32))
        few = table.shape[0]
        small = jnp.concatenate([table, line, jnp.zeros((SMALL - few - 1, c), F32)], 0)
        early_ref[here + (slice(3 * r + per, None),)] = small.astype(BF16)
        own_ref[:r, :] = wo_ref[...]
        wide_parts = wi_ref.shape[1] // c
        for n in range(wide_parts):
            own_ref[(1 + n) * r : (2 + n) * r, :] = wi_ref[:, n * c : (n + 1) * c]
        own_ref[(1 + wide_parts) * r :, :] = w2_ref[...]
        own_copy().start()
        meet(at)
        early.begin()
        early.relay(0)
        for o in range(1, dp):
            early.spread(o)
        for o in range(1, dp):
            early.relay(o)
        early.near()
        own_copy().wait()
        late.begin()
        early.share()
        early.arrive()
        group = members(at.side)
        for f, (a, b, core) in enumerate(group):
            for n in range(3):
                weight_ref[f * r : (f + 1) * r, n * width : (n + 1) * width] = jnp.concatenate(
                    [early_ref[e, a, b, core, n * r : (n + 1) * r, :] for e in range(dp)], 1
                )
        tables = []
        lines = []
        for e in range(dp):
            for n in range(folds):
                spot = slice(e * held + n * per, e * held + (n + 1) * per)
                pos_ref[spot, :] = jnp.concatenate(
                    [
                        early_ref[e, a, b, core, 3 * r : 3 * r + per, :][:, n * narrow : (n + 1) * narrow]
                        for a, b, core in group
                    ],
                    1,
                )
            smalls = [early_ref[e, a, b, core, 3 * r + per :, :].astype(F32) for a, b, core in group]
            tables.append(jnp.concatenate([x[:few, :narrow] for x in smalls], 1))
            lines.extend(x[few : few + 1, : line_ref.shape[1]] for x in smalls)
        vec_ref[...] = jnp.concatenate(tables, 0)
        bias_ref[...] = jnp.concatenate(lines, 1)

    def project(step, carry):
        spot = pl.ds(pl.multiple_of(step * WIN, WIN), WIN)
        low = (act_ref[0, spot, :].astype(F32) + pos_ref[spot, :].astype(F32)).astype(BF16)
        every = nn(low, weight_ref[...])
        q = (every[:, :width] + vec_ref[0:1, :]).astype(BF16)
        q = (q.astype(F32) * 0.125).astype(BF16)
        k = every[:, width : 2 * width].astype(BF16)
        v = (every[:, 2 * width :] + vec_ref[1:2, :]).astype(BF16)
        q_ref[0, spot, :] = q
        k_ref[0, spot, :] = k
        v_ref[0, spot, :] = v
        qt_ref[0, :, spot] = q.T
        kt_ref[0, :, spot] = k.T
        vt_ref[:, spot] = v.T
        return carry

    lax.fori_loop(0, blocks, project, 0)

    @pl.when(row == 0)
    def _():
        late.relay(0)

    @pl.when(row == rows - 1)
    def _():
        for o in range(dp // 2, dp):
            late.relay(o)
        late.near()

    def score(block, head):
        q_head = head_rows(qt_ref[0, pair_of(head), block_of(block)], head % 2)
        return [nn(k_ref[0, spot, pair_of(head)], q_head) for spot in spots_of(block)]

    def soften(block, head, scores):
        scores[0] = causal(scores[0])
        peaks = [jnp.max(x, 0, keepdims=True) for x in scores]
        peak = peaks[0]
        if block:
            peak = jnp.maximum(peak, peaks[1] + apart(lengths_ref, row, block))
        expo = [jnp.exp(scores[0] - peak)]
        if block:
            expo.append(jnp.exp(scores[1] - (peak - apart(lengths_ref, row, block))))
        total = sum(jnp.sum(x, 0, keepdims=True) for x in expo)
        lse_ref[0, head // 2, head % 2 : head % 2 + 1, block_of(block)] = peak + jnp.log(total)
        return [x.astype(BF16) for x in expo], total

    def combine(block, head, soft):
        expo, total = soft
        half = slice(head * HD, (head + 1) * HD)
        out = sum(nn(vt_ref[half, spot], x) for spot, x in zip(spots_of(block), expo))
        ctxt_ref[block % 2, half, :] = (out * (1.0 / total)).astype(BF16)
        if head == H - 1:
            ctx_ref[0, block_of(block), :] = ctxt_ref[block % 2].T

    stages = (score, soften, combine)
    tasks = [(block, head) for block in range(blocks) for head in range(H)]
    quarter = len(tasks) // 4
    staggered(tasks[:quarter], stages)

    @pl.when(row == 0)
    def _():
        for o in range(1, dp // 2):
            late.spread(o)

    staggered(tasks[quarter : 2 * quarter], stages)

    @pl.when(row == 0)
    def _():
        for o in range(dp // 2, dp):
            late.spread(o)

    @pl.when(row == rows - 1)
    def _():
        late.share()

    staggered(tasks[2 * quarter : 3 * quarter], stages)

    @pl.when(row == 0)
    def _():
        for o in range(1, dp // 2):
            late.relay(o)

    staggered(tasks[3 * quarter :], stages)

    @pl.when(row == rows - 1)
    def _():
        late.arrive()
        early.close()
        late.close()


def backward_attention(
    lengths_ref, q_ref, qt_ref, k_ref, kt_ref, v_ref, lse_ref, grad_ref, first_ref, act_ref, pos_ref, weight_ref,
    late_ref, sums_ref, bsum_ref,
    input_ref, late_sum_ref, weight_sum_ref, place_sum_ref,
    lowt_ref, gradt_ref, dqt_ref, dk_ref, dv_ref, every_ref, start_ref, total_ref, wpart_ref, ppart_ref, own_ref,
    own_sem, first_sem, *scratch,
):
    step = pl.program_id(0)
    last = H // 2 - 1
    rows, seq, width = act_ref.shape
    blocks = seq // WIN
    at = Place()
    dp = at.dp
    group = members(at.side)
    r = width // len(group)
    c = width // dp
    narrow = r
    held = seq // dp
    folds = c // narrow
    per = held // folds
    few = sums_ref.shape[0] // dp
    single = bsum_ref.shape[1] // (dp * len(group))
    shared = dp // (H // 2)
    count = Reduce.COUNT
    late = Reduce(late_ref, scratch[:count], at, (own_ref, own_sem))
    weights = Reduce(wpart_ref, scratch[count : 2 * count], at)
    places = Reduce(ppart_ref, scratch[2 * count :], at)
    first_copy = pltpu.make_async_copy(first_ref, start_ref, first_sem)
    pieces = lambda j: [j * shared + n for n in range(shared)]
    nearest = [at.at_dp(n + 1) for n in range(dp)]

    @pl.when(step == 0)
    def _():
        first_copy.start()
        late.own_half().start()
        meet(at)
        for e in nearest:
            late.begin(e)
        total_ref[...] = sums_ref[...]
        for row in range(rows):
            for block in range(blocks):
                spot = block_of(block)
                low = (act_ref[row, spot, :].astype(F32) + pos_ref[spot, :].astype(F32)).astype(BF16)
                lowt_ref[:, row * seq + block * WIN : row * seq + (block + 1) * WIN] = low.T

    for row in range(rows):
        for block in range(blocks):
            gradt_ref[row, :, block_of(block)] = grad_ref[row, block_of(block), :].T

    def score(row, block, head):
        q_head = head_rows(qt_ref[row, :, block_of(block)], head)
        g_head = head_rows(gradt_ref[row, :, block_of(block)], head)
        scores = [nn(k_ref[row, spot, :], q_head) for spot in spots_of(block)]
        return scores, [nn(v_ref[row, spot, :], g_head) for spot in spots_of(block)]

    def soften(row, block, head, products):
        scores, prob_grads = products
        lse = lse_ref[row, 0, head : head + 1, block_of(block)]
        probs = [jnp.exp(causal(scores[0]) - lse)]
        if block:
            probs.append(jnp.exp(scores[1] - (lse - apart(lengths_ref, row, block))))
        inner = sum(jnp.sum(p * g, 0, keepdims=True) for p, g in zip(probs, prob_grads))
        score_grads = [(p * (g - inner)).astype(BF16) for p, g in zip(probs, prob_grads)]
        return [p.astype(BF16) for p in probs], score_grads

    waiting = {}

    def combine(row, block, head, soft):
        half = slice(head * HD, (head + 1) * HD)
        dq = sum(nn(kt_ref[row, half, spot], x) for spot, x in zip(spots_of(block), soft[1]))
        dqt_ref[row, half, block_of(block)] = (dq * 0.125).astype(BF16)
        if head == 0:
            waiting[row, block] = soft
            return
        even = waiting.pop((row, block))
        g = grad_ref[row, block_of(block), :]
        q = q_ref[row, block_of(block), :]
        g_both = jnp.concatenate([head_lanes(g, 0), head_lanes(g, 1)], 0)
        q_both = jnp.concatenate([head_lanes(q, 0), head_lanes(q, 1)], 0)
        for n, spot in enumerate(spots_of(block)):
            dv = nn(jnp.concatenate([even[0][n], soft[0][n]], 1), g_both)
            dk = nn(jnp.concatenate([even[1][n], soft[1][n]], 1), q_both)
            if n == 0:
                dv_ref[row, spot, :] = dv
                dk_ref[row, spot, :] = dk
            else:
                dv_ref[row, spot, :] += dv
                dk_ref[row, spot, :] += dk

    def attend(row):
        staggered([(row, block, head) for block in range(blocks) for head in range(2)], (score, soften, combine))

    for row in range(rows - 1):
        attend(row)

    @pl.when(step == 0)
    def _():
        late.own_half().wait()
        for e in nearest:
            late.across(e)

    @pl.when(step == 2)
    def _():
        for e in nearest:
            late.middle(e)

    @pl.when(step == last)
    def _():
        for e in nearest:
            late.along(e)
        for e in pieces(last - 3):
            weights.along(e)

    @pl.when(step > 0)
    def _():
        for e in pieces(step - 1):
            weights.across(e)

    attend(rows - 1)

    feats = pl.ds(pl.multiple_of(step * PAIR, PAIR), PAIR)
    for row in range(rows):
        for block in range(blocks):
            spot = block_of(block)
            every = [dqt_ref[row, :, spot].T, dk_ref[row, spot, :].astype(BF16), dv_ref[row, spot, :].astype(BF16)]
            every_ref[row * seq + block * WIN : row * seq + (block + 1) * WIN, :] = jnp.concatenate(every, 1)
    total_ref[0:1, feats] = column_sum(every_ref[:, :PAIR])
    total_ref[1:2, feats] = column_sum(every_ref[:, 2 * PAIR :])
    owned = nn(lowt_ref[...], every_ref[...])
    for i, e in enumerate(pieces(step)):
        for f, (a, b, core) in enumerate(group):
            for n in range(3):
                lanes = slice(n * PAIR + i * c, n * PAIR + (i + 1) * c)
                wpart_ref[e, a, b, core, n * r : (n + 1) * r, :] = owned[f * r : (f + 1) * r, lanes].astype(BF16)
        weights.begin(e)

    @pl.when(step > 1)
    def _():
        for e in pieces(step - 2):
            weights.middle(e)

    column = jnp.concatenate(
        [weight_ref[:, pl.ds(pl.multiple_of(n * width + step * PAIR, PAIR), PAIR)] for n in range(3)], 1
    )

    @pl.when(step == 0)
    def _():
        first_copy.wait()

    @pl.when(step < last)
    def _():
        tile = 2 * WIN
        for row in range(rows):
            for n in range(seq // tile):
                spot = slice(n * tile, (n + 1) * tile)
                start_ref[row, spot, :] += nt(every_ref[row * seq + n * tile : row * seq + (n + 1) * tile, :], column)

    @pl.when(step == last)
    def _():
        wide = lambda x: jnp.concatenate([x, jnp.zeros((x.shape[0], c - x.shape[1]), F32)], 1)

        def finish(e):
            total = None
            for row in range(rows):
                spot = slice(e * held, (e + 1) * held)
                grad = start_ref[row, spot, :] + nt(every_ref[row * seq + e * held : row * seq + (e + 1) * held, :], column)
                input_ref[row, spot, :] = grad.astype(BF16)
                total = grad if total is None else total + grad
            total = total.astype(BF16)
            for f, (a, b, core) in enumerate(group):
                lanes = slice(f * narrow, (f + 1) * narrow)
                ppart_ref[e, a, b, core, :per, :] = jnp.concatenate(
                    [total[n * per : (n + 1) * per, lanes] for n in range(folds)], 1
                )
                table = total_ref[e * few : (e + 1) * few, lanes]
                spot = (e * len(group) + f) * single
                line = bsum_ref[:, spot : spot + single]
                filler = jnp.zeros((SMALL - few - 1, c), F32)
                ppart_ref[e, a, b, core, per:, :] = jnp.concatenate([wide(table), wide(line), filler], 0).astype(BF16)
            places.begin(e)

        for n in range(dp + 3):
            if n < dp:
                finish(n)
            if n == 0:
                for e in pieces(last):
                    weights.across(e)
                for e in pieces(last - 1):
                    weights.middle(e)
                for e in pieces(last - 2):
                    weights.along(e)
            if n == 1:
                for e in pieces(last):
                    weights.middle(e)
                for e in pieces(last - 1):
                    weights.along(e)
            if n == 2:
                for e in pieces(last):
                    weights.along(e)
            if n == 3:
                late_sum_ref[...] = late.result()
            if 0 <= n - 1 < dp:
                places.across(n - 1)
            if 0 <= n - 2 < dp:
                places.middle(n - 2)
            if 0 <= n - 3 < dp:
                places.along(n - 3)
        weight_sum_ref[...] = weights.result()
        place_sum_ref[...] = places.result()
        late.close()
        weights.close()
        places.close()


def hand_out(
    late_ref, weight_ref, place_ref, input_ref,
    out_ref, wq_ref, wk_ref, wv_ref, wo_ref, wi_ref, w2_ref, table_ref, placet_ref, line_ref,
):
    @pl.when(pl.program_id(0) >= 0)
    def _():
        out_ref[...] = input_ref[...]

    r, c = wq_ref.shape
    few, narrow = table_ref.shape
    held = placet_ref.shape[1]
    folds = c // narrow
    per = held // folds
    for n, ref in enumerate((wq_ref, wk_ref, wv_ref)):
        ref[...] = weight_ref[n * r : (n + 1) * r, :]
    wide_parts = wi_ref.shape[1] // c
    wo_ref[...] = late_ref[:r, :]
    for n in range(wide_parts):
        wi_ref[:, n * c : (n + 1) * c] = late_ref[(1 + n) * r : (2 + n) * r, :]
    w2_ref[...] = late_ref[(1 + wide_parts) * r :, :]
    place = place_ref[:per, :]
    placet_ref[...] = jnp.concatenate([place[:, n * narrow : (n + 1) * narrow] for n in range(folds)], 0).T
    table_ref[...] = place_ref[per : per + few, :narrow]
    line_ref[...] = place_ref[per + few : per + few + 1, : line_ref.shape[1]]


def feed_forward(
    ctx_ref, act_ref, pos_ref, cot_ref, late_ref, vec_ref, bias_ref,
    out_ref, first_ref, grad_ref, part_ref, sums_ref, bsum_ref,
    wo_acc, wi_acc, w2_acc, slope_ref, wo_ref, wi_ref, w2_ref,
):
    step = pl.program_id(0)
    width = ctx_ref.shape[1]
    dp, side, _, _, _, c = late_ref.shape
    group = members(side)
    r = width // len(group)
    parts = bias_ref.shape[1] // dp // c
    tall = bias_ref.shape[1] // len(group)
    hidden = bias_ref.shape[1]
    part = 512

    @pl.when(step == 0)
    def _():
        wo_acc[...] = jnp.zeros_like(wo_acc)
        wi_acc[...] = jnp.zeros_like(wi_acc)
        w2_acc[...] = jnp.zeros_like(w2_acc)
        sums_ref[...] = jnp.zeros_like(sums_ref)
        bsum_ref[...] = jnp.zeros_like(bsum_ref)
        for f, (a, b, core) in enumerate(group):
            rows = slice(f * r, (f + 1) * r)
            block = lambda e, lo, n: late_ref[e, a, b, core, lo : lo + n, :]
            wo_ref[rows, :] = jnp.concatenate([block(e, 0, r) for e in range(dp)], 1)
            wi_ref[rows, :] = jnp.concatenate([block(e, (1 + n) * r, r) for e in range(dp) for n in range(parts)], 1)
            w2_ref[f * tall : (f + 1) * tall, :] = jnp.concatenate(
                [block(e, (1 + parts) * r, tall) for e in range(dp)], 1
            )

    vec = lambda n: vec_ref[n : n + 1, :]
    ctx = ctx_ref[...]
    first_sum = act_ref[...].astype(F32) + pos_ref[...].astype(F32) + (nn(ctx, wo_ref[...]) + vec(2))
    center = first_sum - jnp.mean(first_sum, -1, keepdims=True)
    scale_one = lax.rsqrt(jnp.mean(center * center, -1, keepdims=True) + 1e-05)
    z_one = center * scale_one
    normed = z_one * vec(3) + vec(4)
    normed_low = normed.astype(BF16)
    branch = None
    acts = []
    C = hidden // part
    cols = [slice(n * part, (n + 1) * part) for n in range(C)]
    pre_next = nn(normed_low, wi_ref[:, cols[0]])
    for n in range(C):
        pre = pre_next + bias_ref[:, cols[n]]
        if n + 1 < C:
            pre_next = nn(normed_low, wi_ref[:, cols[n + 1]])
        if n >= 1:
            term = nn(acts[n - 1], w2_ref[cols[n - 1], :])
            branch = term if branch is None else branch + term
        square = pre * pre
        t = jnp.tanh(pre * (0.7978845608028654 + (0.7978845608028654 * 0.044715) * square))
        half = 0.5 + 0.5 * t
        acts.append((pre * half).astype(BF16))
        slope_ref[:, cols[n]] = half + (0.5 * pre) * (1.0 - t * t) * (
            0.7978845608028654 + (3.0 * 0.7978845608028654 * 0.044715) * square
        )
    term = nn(acts[C - 1], w2_ref[cols[C - 1], :])
    branch = term if branch is None else branch + term
    second_sum = normed + (branch + vec(5))
    center = second_sum - jnp.mean(second_sum, -1, keepdims=True)
    scale_two = lax.rsqrt(jnp.mean(center * center, -1, keepdims=True) + 1e-05)
    z_two = center * scale_two
    out_ref[...] = (z_two * vec(6) + vec(7)).astype(BF16)
    cot = cot_ref[...].astype(F32)
    sums_ref[6:7, :] += column_sum(cot * z_two)
    sums_ref[7:8, :] += column_sum(cot)
    e = cot * vec(6)
    second_grad = scale_two * (
        e - jnp.mean(e, -1, keepdims=True) - z_two * jnp.mean(e * z_two, -1, keepdims=True)
    )
    branch_grad = second_grad.astype(BF16)
    sums_ref[5:6, :] += column_sum(branch_grad)
    branch_t = branch_grad.T
    normed_t = normed_low.T
    normed_grad = second_grad
    grad_next = nt(branch_grad, w2_ref[cols[0], :])
    lows = []

    def weights(n):
        wi_acc[:, cols[n]] += nn(normed_t, lows[n])
        return nt(lows[n], wi_ref[:, cols[n]])

    for n in range(C):
        pre_grad = grad_next * slope_ref[:, cols[n]]
        if n + 1 < C:
            grad_next = nt(branch_grad, w2_ref[cols[n + 1], :])
        w2_acc[:, cols[n]] += nn(branch_t, acts[n])
        if n >= 1:
            normed_grad = normed_grad + weights(n - 1)
        lows.append(pre_grad.astype(BF16))
        bsum_ref[:, cols[n]] += column_sum(lows[n])
    normed_grad = normed_grad + weights(C - 1)
    sums_ref[3:4, :] += column_sum(normed_grad * z_one)
    sums_ref[4:5, :] += column_sum(normed_grad)
    e = normed_grad * vec(3)
    first_grad = scale_one * (
        e - jnp.mean(e, -1, keepdims=True) - z_one * jnp.mean(e * z_one, -1, keepdims=True)
    )
    first_ref[...] = first_grad
    attn_grad = first_grad.astype(BF16)
    sums_ref[2:3, :] += column_sum(attn_grad)
    wo_acc[...] += nn(ctx.T, attn_grad)
    grad_ref[...] = nt(attn_grad, wo_ref[...]).astype(BF16)

    @pl.when(step == pl.num_programs(0) - 1)
    def _():
        for e in range(dp):
            lanes = slice(e * c, (e + 1) * c)
            for f, (a, b, core) in enumerate(group):
                rows = slice(f * r, (f + 1) * r)
                part_ref[e, a, b, core, :r, :] = wo_acc[rows, lanes].astype(BF16)
                for n in range(parts):
                    wide = slice((e * parts + n) * c, (e * parts + n + 1) * c)
                    part_ref[e, a, b, core, (1 + n) * r : (2 + n) * r, :] = wi_acc[rows, wide].astype(BF16)
                turned = w2_acc[lanes, f * tall : (f + 1) * tall].astype(BF16)
                part_ref[e, a, b, core, (1 + parts) * r :, :] = turned.T


def whole(shape):
    return pl.BlockSpec(shape, lambda *_: (0,) * len(shape))


def once(shape):
    return pl.BlockSpec(shape, lambda *_: (0,) * len(shape), pipeline_mode=pl.Buffered(1))


def run_forward(lengths, act, wq, wk, wv, wo, wi, w2, table, place, line):
    rows, seq, width = act.shape
    dp, side = lax.axis_size("dp"), side_of(lax.axis_size("fsdp"))
    r, c = wq.shape
    hidden = wi.shape[1] * dp
    first_rows = 3 * r + place.shape[0] * place.shape[1] // c + SMALL
    late_rows = r + r * wi.shape[1] // c + w2.shape[0]
    row3 = lambda shape: pl.BlockSpec((1,) + shape, lambda i: (i,) + (0,) * len(shape))
    seqs = row3((seq, width))
    turned = row3((width, seq))
    st, tt = jax.ShapeDtypeStruct((rows, seq, width), BF16), jax.ShapeDtypeStruct((rows, width, seq), BF16)
    small = [x.shape for x in (wq, wk, wv, wo, wi, w2, table, place, line)]
    return pl.pallas_call(
        forward_attention,
        grid=(rows,),
        in_specs=[pl.BlockSpec(memory_space=pltpu.SMEM), seqs] + [whole(x) for x in small],
        out_specs=[seqs, turned, seqs, turned, seqs, seqs, row3((H // 2, 2, seq)), whole((width, 3 * width)),
                   whole((seq, width)), whole((table.shape[0] * dp, width)), whole((1, hidden)),
                   pl.BlockSpec(memory_space=pl.ANY)],
        scratch_shapes=[
            pltpu.VMEM((width, seq), BF16),
            pltpu.VMEM((2, width, WIN), BF16),
            pltpu.VMEM((dp, side, side, 2, first_rows, c), BF16),
            pltpu.VMEM((late_rows, c), BF16),
            pltpu.SemaphoreType.DMA,
        ]
        + Gather.semaphores(dp, side) * 2,
        out_shape=[
            st, tt, st, tt, st, st, jax.ShapeDtypeStruct((rows, H // 2, 2, seq), F32),
            jax.ShapeDtypeStruct((width, 3 * width), BF16),
            jax.ShapeDtypeStruct((seq, width), BF16),
            jax.ShapeDtypeStruct((table.shape[0] * dp, width), F32),
            jax.ShapeDtypeStruct((1, hidden), F32),
            jax.ShapeDtypeStruct((dp, side, side, 2, late_rows, c), BF16),
        ],
        compiler_params=pltpu.CompilerParams(
            vmem_limit_bytes=VMEM_LIMIT, collective_id=0, has_side_effects=True
        ),
        name="forward_attention",
    )(lengths, act, wq, wk, wv, wo, wi, w2, table, place, line)


def run_backward(lengths, q, qt, k, kt, v, lse, grad, first, act, pos, weight, late, sums, bsum):
    rows, seq, width = act.shape
    dp, side = late.shape[:2]
    late_rows, c = late.shape[4:]
    r = width // (2 * side * side)
    weight_rows = 3 * r
    place_rows = (seq // dp) * r // c + SMALL
    lanes = pl.BlockSpec((rows, seq, PAIR), lambda j: (0, 0, j))
    turned = pl.BlockSpec((rows, PAIR, seq), lambda j: (0, j, 0))
    anywhere = pl.BlockSpec(memory_space=pl.ANY)
    totals = [(n, c) for n in (late_rows, weight_rows, place_rows)]
    return pl.pallas_call(
        backward_attention,
        grid=(H // 2,),
        in_specs=[pl.BlockSpec(memory_space=pltpu.SMEM), lanes, turned, lanes, turned, lanes,
                  pl.BlockSpec((rows, 1, 2, seq), lambda j: (0, j, 0, 0)), lanes, anywhere, once(act.shape),
                  once(pos.shape), once(weight.shape), anywhere, once(sums.shape), once(bsum.shape)],
        out_specs=[whole(act.shape)] + [whole(x) for x in totals],
        scratch_shapes=[
            pltpu.VMEM((width, rows * seq), BF16),
            pltpu.VMEM((rows, PAIR, seq), BF16),
            pltpu.VMEM((rows, PAIR, seq), BF16),
            pltpu.VMEM((rows, seq, PAIR), F32),
            pltpu.VMEM((rows, seq, PAIR), F32),
            pltpu.VMEM((rows * seq, 3 * PAIR), BF16),
            pltpu.VMEM((rows, seq, width), F32),
            pltpu.VMEM(sums.shape, F32),
            pltpu.VMEM((dp, side, side, 2, weight_rows, c), BF16),
            pltpu.VMEM((dp, side, side, 2, place_rows, c), BF16),
            pltpu.VMEM((dp, side, side, late_rows, c), BF16),
            pltpu.SemaphoreType.DMA,
            pltpu.SemaphoreType.DMA,
        ]
        + Reduce.scratch(dp, side, late_rows, c)
        + Reduce.scratch(dp, side, weight_rows, c)
        + Reduce.scratch(dp, side, place_rows, c),
        out_shape=[jax.ShapeDtypeStruct(act.shape, BF16)] + [jax.ShapeDtypeStruct(x, F32) for x in totals],
        compiler_params=pltpu.CompilerParams(
            vmem_limit_bytes=VMEM_LIMIT, collective_id=1, has_side_effects=True
        ),
        name="backward_attention",
    )(lengths, q, qt, k, kt, v, lse, grad, first, act, pos, weight, late, sums, bsum)


def run_hand_out(late, weight, place, grad, shapes):
    steps = 4
    block = pl.BlockSpec((1, grad.shape[0] * grad.shape[1] // steps, grad.shape[2]), lambda i: (i, 0, 0))
    rows = grad.reshape(steps, -1, grad.shape[2])
    return pl.pallas_call(
        hand_out,
        grid=(steps,),
        in_specs=[whole(x.shape) for x in (late, weight, place)] + [block],
        out_specs=[block] + [whole(x) for x in shapes],
        out_shape=[jax.ShapeDtypeStruct(rows.shape, BF16)] + [jax.ShapeDtypeStruct(x, F32) for x in shapes],
        name="hand_out",
    )(late, weight, place, rows)


def run_feed_forward(ctx, act, pos, cot, late, vec, bias, tile=512):
    tokens, width = ctx.shape
    seq = pos.shape[0]
    hidden = bias.shape[1]
    per_row = seq // tile
    tok = pl.BlockSpec((tile, width), lambda t: (t, 0))
    return pl.pallas_call(
        feed_forward,
        grid=(tokens // tile,),
        in_specs=[tok, tok, pl.BlockSpec((tile, width), lambda t: (t % per_row, 0)), tok,
                  once(late.shape), whole(vec.shape), whole(bias.shape)],
        out_specs=[tok, tok, tok, whole(late.shape), whole((8, width)), whole((1, hidden))],
        scratch_shapes=[
            pltpu.VMEM((width, width), F32),
            pltpu.VMEM((width, hidden), F32),
            pltpu.VMEM((width, hidden), F32),
            pltpu.VMEM((tile, hidden), F32),
            pltpu.VMEM((width, width), BF16),
            pltpu.VMEM((width, hidden), BF16),
            pltpu.VMEM((hidden, width), BF16),
        ],
        out_shape=[
            jax.ShapeDtypeStruct((tokens, width), BF16),
            jax.ShapeDtypeStruct((tokens, width), F32),
            jax.ShapeDtypeStruct((tokens, width), BF16),
            jax.ShapeDtypeStruct(late.shape, BF16),
            jax.ShapeDtypeStruct((8, width), F32),
            jax.ShapeDtypeStruct((1, hidden), F32),
        ],
        compiler_params=pltpu.CompilerParams(vmem_limit_bytes=VMEM_LIMIT),
        name="feed_forward",
    )(ctx, act, pos, cot, late, vec, bias)


def shards(
    activations, window_lengths, query_weight, key_weight, value_weight, output_weight, inner_weight, outer_weight,
    vectors, positions, inner_bias, output_cotangent,
):
    rows, seq, width = activations.shape
    q, qt, k, kt, v, ctx, lse, weight, pos, vec, bias, late = run_forward(
        window_lengths, activations, query_weight, key_weight, value_weight, output_weight, inner_weight, outer_weight,
        vectors, positions.T, inner_bias.reshape(1, -1),
    )
    flat = lambda x: x.reshape(rows * seq, width)
    deep = lambda x: x.reshape(rows, seq, width)
    out, first, grad, part, sums, bsum = run_feed_forward(
        flat(ctx), flat(activations), pos, flat(output_cotangent), late, vec, bias
    )
    input_grad, *sums = run_backward(
        window_lengths, q, qt, k, kt, v, lse, deep(grad), deep(first), activations, pos, weight, part, sums, bsum
    )
    shapes = [x.shape for x in (query_weight, key_weight, value_weight, output_weight, inner_weight, outer_weight,
                                vectors, positions.T)] + [(1, inner_bias.shape[0])]
    owned = run_hand_out(*sums, input_grad, shapes)
    return (deep(out), owned[0].reshape(input_grad.shape)) + tuple(owned[1:8]) + (owned[8].T, owned[9].reshape(-1))


def solution(mesh):
    tokens = P(("dp", "fsdp"), None, None)
    matrix = P("fsdp", "dp")
    table = P("dp", "fsdp")
    line = P(("dp", "fsdp"))
    return jax.shard_map(
        shards,
        mesh=mesh,
        in_specs=(tokens, P(("dp", "fsdp"), None)) + (matrix,) * 6 + (table, table, line, tokens),
        out_specs=(tokens, tokens) + (matrix,) * 6 + (table, table, line),
        check_vma=False,
    )
```

```python
import functools

import jax
import jax.numpy as jnp
from jax import lax
from jax.experimental import pallas as pl
from jax.experimental.pallas import tpu as pltpu
from jax.sharding import PartitionSpec as P

H = 8
HD = 64
WIN = 256
PAIR = 2 * HD
VMEM_LIMIT = 62 * 1024 * 1024
F32 = jnp.float32
BF16 = jnp.bfloat16
MESH = pl.DeviceIdType.MESH
SMALL = 16


def nn(left, right):
    return lax.dot_general(left, right, (((1,), (0,)), ((), ())), preferred_element_type=F32)


def nt(left, right):
    return lax.dot_general(left, right, (((1,), (1,)), ((), ())), preferred_element_type=F32)


def tn(left, right):
    return lax.dot_general(left, right, (((0,), (0,)), ((), ())), preferred_element_type=F32)


def column_sum(value):
    return jnp.sum(value.astype(F32), 0, keepdims=True)


def head_rows(pair, which):
    zeros = jnp.zeros((HD, pair.shape[1]), pair.dtype)
    if which == 0:
        return jnp.concatenate([pair[:HD], zeros], 0)
    return jnp.concatenate([zeros, pair[HD:]], 0)


def head_lanes(pair, which):
    lane = lax.broadcasted_iota(jnp.int32, pair.shape, 1)
    keep = (lane < HD) if which == 0 else (lane >= HD)
    return jnp.where(keep, pair, jnp.zeros_like(pair))


def causal(scores):
    key = lax.broadcasted_iota(jnp.int32, scores.shape, 0)
    query = lax.broadcasted_iota(jnp.int32, scores.shape, 1)
    return jnp.where(key <= query, scores, -1e30)


def block_of(block):
    return slice(block * WIN, (block + 1) * WIN)


def spots_of(block):
    return [block_of(n) for n in (block, block - 1) if n >= 0]


def pair_of(head):
    return slice(head // 2 * PAIR, (head // 2 + 1) * PAIR)


def staggered(tasks, stages):
    held = {}
    for step in range(len(tasks) + len(stages) - 1):
        for n, stage in enumerate(stages):
            task = step - n
            if 0 <= task < len(tasks):
                args = (held.pop(task),) if n else ()
                held[task] = stage(*tasks[task], *args)


class Place:
    def __init__(self):
        fsdp = lax.axis_index("fsdp")
        self.d, self.dp = lax.axis_index("dp"), lax.axis_size("dp")
        self.side = side_of(lax.axis_size("fsdp"))
        self.chip, self.core = fsdp // 2, lax.rem(fsdp, 2)
        y, x = self.chip // self.side, lax.rem(self.chip, self.side)
        self.a = y + self.core * (x - y)
        self.b = x + self.core * (y - x)

    def device(self, a, b):
        straight, turned = a * self.side + b, b * self.side + a
        return {"fsdp": (straight + self.core * (turned - straight)) * 2 + self.core}

    def sibling(self):
        return {"fsdp": self.chip * 2 + 1 - self.core}

    def at_a(self, n):
        return lax.rem(self.a + n + self.side, self.side)

    def at_b(self, n):
        return lax.rem(self.b + n + self.side, self.side)

    def at_dp(self, n):
        return lax.rem(self.d + n + self.dp, self.dp)


def side_of(fsdp):
    side = 1
    while side * side * 2 < fsdp:
        side += 1
    assert side * side * 2 == fsdp
    return side


def members(side):
    found = []
    for f in range(2 * side * side):
        y, x = f // 2 // side, f // 2 % side
        found.append((x, y, 1) if f % 2 else (y, x, 0))
    return found


def remote(src, dst, send, recv, device):
    return pltpu.make_async_remote_copy(
        src_ref=src, dst_ref=dst, send_sem=send, recv_sem=recv, device_id=device, device_id_type=MESH
    )


def greet(at):
    barrier = pltpu.get_barrier_semaphore()
    others = [{"dp": at.at_dp(n)} for n in range(1, at.dp)]
    others += [at.device(at.a, at.at_b(n)) for n in range(1, at.side)]
    others += [at.device(at.at_a(n), at.b) for n in range(1, at.side)]
    others.append(at.sibling())
    for other in others:
        pl.semaphore_signal(barrier, inc=1, device_id=other, device_id_type=MESH)
    return len(others)


def meet(count):
    pl.semaphore_wait(pltpu.get_barrier_semaphore(), count)


class Gather:
    COUNT = 8

    def __init__(self, buf, sems, at):
        self.buf, self.at = buf, at
        self.zs, self.zr, self.bs, self.br, self.sa, self.ra, self.cs, self.cr = sems

    @staticmethod
    def semaphores(dp, side):
        dma = pltpu.SemaphoreType.DMA
        shapes = [(dp,), (dp, side), (dp, side, side), (side, side)]
        return [dma(x) for x in shapes for _ in range(2)]

    def along_dp(self, o):
        at = self.at
        block = self.buf.at[at.d, at.a, at.b, at.core]
        return remote(block, block, self.zs.at[o], self.zr.at[o], {"dp": at.at_dp(o)})

    def along_b(self, o, p):
        at = self.at
        block = self.buf.at[at.at_dp(-o), at.a, at.b, at.core]
        return remote(block, block, self.bs.at[o, p], self.br.at[o, p], at.device(at.a, at.at_b(p)))

    def along_a(self, o, p, q):
        at = self.at
        block = self.buf.at[at.at_dp(-o), at.a, at.at_b(-p), at.core]
        return remote(block, block, self.sa.at[o, p, q], self.ra.at[o, p, q], at.device(at.at_a(q), at.b))

    def to_core(self, q, p):
        at = self.at
        block = self.buf.at[:, at.at_a(-q), at.at_b(-p), at.core]
        return remote(block, block, self.cs.at[q, p], self.cr.at[q, p], at.sibling())

    def begin(self):
        for o in range(1, self.at.dp):
            self.along_dp(o).start()

    def pass_on(self, o):
        for p in range(1, self.at.side):
            self.along_b(o, p).start()

    def far(self, o):
        for q in range(1, self.at.side):
            self.along_a(o, 0, q).start()

    def spread(self, o):
        self.along_dp(o).wait_recv()
        self.pass_on(o)

    def relay(self, o):
        for p in range(1, self.at.side):
            self.along_b(o, p).wait_recv()
            for q in range(1, self.at.side):
                self.along_a(o, p, q).start()

    def near(self):
        for p in range(self.at.side):
            self.to_core(0, p).start()

    def share(self):
        for p in range(self.at.side):
            for q in range(1, self.at.side):
                for o in range(self.at.dp):
                    self.along_a(o, p, q).wait_recv()
                self.to_core(q, p).start()

    def arrive(self):
        for q in range(self.at.side):
            for p in range(self.at.side):
                self.to_core(q, p).wait_recv()

    def close(self):
        for o in range(1, self.at.dp):
            self.along_dp(o).wait_send()
        for o in range(self.at.dp):
            for p in range(1, self.at.side):
                self.along_b(o, p).wait_send()
            for p in range(self.at.side):
                for q in range(1, self.at.side):
                    self.along_a(o, p, q).wait_send()
        for q in range(self.at.side):
            for p in range(self.at.side):
                self.to_core(q, p).wait_send()


def add_up(terms):
    if len(terms) == 2:
        return terms[0] + terms[1]
    return sum(x.astype(F32) for x in terms).astype(BF16)


class Reduce:
    COUNT = 13

    def __init__(self, part, scratch, at, own=None):
        self.part, self.at = part, at
        self.own, self.own_sem = own or (None, None)
        (self.pair, self.plane, self.row, self.mine, self.line,
         self.cs, self.cr, self.sa, self.ra, self.bs, self.br, self.zs, self.zr) = scratch

    @staticmethod
    def scratch(dp, side, rows, c):
        dma = pltpu.SemaphoreType.DMA
        return [
            pltpu.VMEM((dp, side, side, rows, c), BF16),
            pltpu.VMEM((side - 1, dp, side, rows, c), BF16),
            pltpu.VMEM((side - 1, dp, rows, c), BF16),
            pltpu.VMEM((dp, rows, c), BF16),
            pltpu.VMEM((dp - 1, rows, c), BF16),
        ] + [dma((dp,))] * 2 + [dma((dp, side))] * 4 + [dma((dp,))] * 2

    def to_core(self, e):
        at = self.at
        return remote(self.part.at[e, :, :, 1 - at.core], self.pair.at[e], self.cs.at[e], self.cr.at[e], at.sibling())

    def along_a(self, e, q):
        at = self.at
        to = at.at_a(q)
        return remote(
            self.pair.at[e, to], self.plane.at[q - 1, e], self.sa.at[e, q], self.ra.at[e, q], at.device(to, at.b)
        )

    def along_b(self, e, p):
        at = self.at
        to = at.at_b(p)
        return remote(
            self.pair.at[e, at.a, to], self.row.at[p - 1, e], self.bs.at[e, p], self.br.at[e, p], at.device(at.a, to)
        )

    def along_dp(self, o):
        at = self.at
        to = at.at_dp(o)
        return remote(self.mine.at[to], self.line.at[o - 1], self.zs.at[o], self.zr.at[o], {"dp": to})

    def own_half(self):
        return pltpu.make_async_copy(self.part.at[:, :, :, self.at.core], self.own, self.own_sem)

    def begin(self, e):
        self.to_core(e).start()

    def across(self, e):
        at = self.at
        self.to_core(e).wait_recv()
        for n in list(range(1, at.side)) + [0]:
            a = at.at_a(n)
            for b in range(at.side):
                own = self.part[e, a, b, at.core] if self.own is None else self.own[e, a, b]
                self.pair[e, a, b] = add_up([own, self.pair[e, a, b]])
            if n:
                self.along_a(e, n).start()

    def middle(self, e):
        at = self.at
        for q in range(1, at.side):
            self.along_a(e, q).wait_recv()
        for n in list(range(1, at.side)) + [0]:
            b = at.at_b(n)
            terms = [self.pair[e, at.a, b]] + [self.plane[q - 1, e, b] for q in range(1, at.side)]
            self.pair[e, at.a, b] = add_up(terms)
            if n:
                self.along_b(e, n).start()

    def along(self, e):
        at = self.at
        for p in range(1, at.side):
            self.along_b(e, p).wait_recv()
        self.mine[e] = add_up([self.pair[e, at.a, at.b]] + [self.row[p - 1, e] for p in range(1, at.side)])

        @pl.when(e != at.d)
        def _():
            self.along_dp(lax.rem(e - at.d + at.dp, at.dp)).start()

    def result(self):
        at = self.at
        for o in range(1, at.dp):
            self.along_dp(o).wait_recv()
        total = self.mine[at.d].astype(F32)
        for o in range(1, at.dp):
            total = total + self.line[o - 1].astype(F32)
        return total

    def close(self):
        at = self.at
        for e in range(at.dp):
            self.to_core(e).wait_send()
            for n in range(1, at.side):
                self.along_a(e, n).wait_send()
                self.along_b(e, n).wait_send()
        for o in range(1, at.dp):
            self.along_dp(o).wait_send()


def apart(lengths_ref, row, block):
    total = jnp.int32(0)
    cut = jnp.bool_(False)
    for n in range(lengths_ref.shape[1]):
        total = total + lengths_ref[row, n]
        cut = cut | (total == block * WIN)
    return jnp.where(cut, jnp.float32(-1e30), jnp.float32(0.0))


def forward_attention(
    lengths_ref, act_ref, wq_ref, wk_ref, wv_ref, wo_ref, wi_ref, w2_ref, table_ref, place_ref, line_ref,
    q_out, qt_out, k_out, kt_out, v_out, lowt_out, ctx_ref, lse_ref, weight_out, pos_out, vec_ref, bias_ref, late_ref,
    q_ref, qt_ref, k_ref, kt_ref, v_ref, lowt_ref, weight_ref, pos_ref, out_sems,
    vt_ref, ctxt_ref, early_ref, own_ref, own_sem, *sems,
):
    row = pl.program_id(0)
    rows = pl.num_programs(0)
    width = act_ref.shape[2]
    blocks = act_ref.shape[1] // WIN
    at = Place()
    dp = at.dp
    here = (at.d, at.a, at.b, at.core)
    r, c = wq_ref.shape
    narrow, held = place_ref.shape
    folds = c // narrow
    per = held // folds
    early = Gather(early_ref, sems[: Gather.COUNT], at)
    late = Gather(late_ref, sems[Gather.COUNT :], at)

    def own_copy():
        return pltpu.make_async_copy(own_ref, late_ref.at[here], own_sem)

    def row_copies(of_row):
        pairs = ((q_ref, q_out), (qt_ref, qt_out), (k_ref, k_out), (kt_ref, kt_out), (v_ref, v_out),
                 (lowt_ref, lowt_out))
        return [
            pltpu.make_async_copy(src.at[0], dst.at[of_row], out_sems.at[n]) for n, (src, dst) in enumerate(pairs)
        ]

    def table_copies():
        pairs = ((weight_ref, weight_out), (pos_ref, pos_out))
        return [pltpu.make_async_copy(src, dst, out_sems.at[6 + n]) for n, (src, dst) in enumerate(pairs)]

    @pl.when(row == 0)
    def _():
        count = greet(at)
        for n, ref in enumerate((wq_ref, wk_ref, wv_ref)):
            early_ref[here + (slice(n * r, (n + 1) * r),)] = ref[...]
        place = place_ref[...].T
        early_ref[here + (slice(3 * r, 3 * r + per),)] = jnp.concatenate(
            [place[n * per : (n + 1) * per] for n in range(folds)], 1
        )
        wide = lambda x: jnp.concatenate([x, jnp.zeros((x.shape[0], c - x.shape[1]), F32)], 1)
        table = wide(table_ref[...].astype(F32))
        line = wide(line_ref[...].astype(F32))
        few = table.shape[0]
        small = jnp.concatenate([table, line, jnp.zeros((SMALL - few - 1, c), F32)], 0)
        early_ref[here + (slice(3 * r + per, None),)] = small.astype(BF16)
        own_ref[:r, :] = wo_ref[...]
        wide_parts = wi_ref.shape[1] // c
        for n in range(wide_parts):
            own_ref[(1 + n) * r : (2 + n) * r, :] = wi_ref[:, n * c : (n + 1) * c]
        own_ref[(1 + wide_parts) * r :, :] = w2_ref[...]
        own_copy().start()
        meet(count)
        early.begin()
        early.pass_on(0)
        early.far(0)
        early.relay(0)
        for o in range(1, dp):
            early.spread(o)
        own_copy().wait()
        late.begin()
        for o in range(1, dp):
            early.relay(o)
            early.far(o)
        early.near()
        late.pass_on(0)
        late.far(0)
        early.share()
        late.relay(0)
        late.spread(1)
        late.far(1)
        early.arrive()
        group = members(at.side)
        for f, (a, b, core) in enumerate(group):
            for n in range(3):
                weight_ref[f * r : (f + 1) * r, n * width : (n + 1) * width] = jnp.concatenate(
                    [early_ref[e, a, b, core, n * r : (n + 1) * r, :] for e in range(dp)], 1
                )
        tables = []
        lines = []
        for e in range(dp):
            for n in range(folds):
                spot = slice(e * held + n * per, e * held + (n + 1) * per)
                pos_ref[spot, :] = jnp.concatenate(
                    [
                        early_ref[e, a, b, core, 3 * r : 3 * r + per, :][:, n * narrow : (n + 1) * narrow]
                        for a, b, core in group
                    ],
                    1,
                )
            smalls = [early_ref[e, a, b, core, 3 * r + per :, :].astype(F32) for a, b, core in group]
            tables.append(jnp.concatenate([x[:few, :narrow] for x in smalls], 1))
            lines.extend(x[few : few + 1, : line_ref.shape[1]] for x in smalls)
        vec_ref[...] = jnp.concatenate(tables, 0)
        bias_ref[...] = jnp.concatenate(lines, 1)
        for copy in table_copies():
            copy.start()

    @pl.when(row > 0)
    def _():
        for copy in row_copies(row - 1):
            copy.wait()

    def project(step, carry):
        spot = pl.ds(pl.multiple_of(step * WIN, WIN), WIN)
        low = (act_ref[0, spot, :].astype(F32) + pos_ref[spot, :].astype(F32)).astype(BF16)
        lowt_ref[0, :, spot] = low.T
        every = nn(low, weight_ref[...])
        q = (every[:, :width] + vec_ref[0:1, :]).astype(BF16)
        q = (q.astype(F32) * 0.125).astype(BF16)
        k = every[:, width : 2 * width].astype(BF16)
        v = (every[:, 2 * width :] + vec_ref[1:2, :]).astype(BF16)
        q_ref[0, spot, :] = q
        k_ref[0, spot, :] = k
        v_ref[0, spot, :] = v
        qt_ref[0, :, spot] = q.T
        kt_ref[0, :, spot] = k.T
        vt_ref[:, spot] = v.T
        return carry

    lax.fori_loop(0, blocks, project, 0)
    for copy in row_copies(row):
        copy.start()

    @pl.when(row == 0)
    def _():
        for o in range(2, dp // 2 + 1):
            late.spread(o)
            late.far(o)
        late.relay(1)

    def score(block, head):
        q_head = head_rows(qt_ref[0, pair_of(head), block_of(block)], head % 2)
        return [nn(k_ref[0, spot, pair_of(head)], q_head) for spot in spots_of(block)]

    def soften(block, head, scores):
        scores[0] = causal(scores[0])
        peaks = [jnp.max(x, 0, keepdims=True) for x in scores]
        peak = peaks[0]
        if block:
            peak = jnp.maximum(peak, peaks[1] + apart(lengths_ref, row, block))
        expo = [jnp.exp(scores[0] - peak)]
        if block:
            expo.append(jnp.exp(scores[1] - (peak - apart(lengths_ref, row, block))))
        total = sum(jnp.sum(x, 0, keepdims=True) for x in expo)
        lse_ref[0, head // 2, head % 2 : head % 2 + 1, block_of(block)] = peak + jnp.log(total)
        return [x.astype(BF16) for x in expo], total

    def combine(block, head, soft):
        expo, total = soft
        half = slice(head * HD, (head + 1) * HD)
        out = sum(nn(vt_ref[half, spot], x) for spot, x in zip(spots_of(block), expo))
        ctxt_ref[block % 2, half, :] = (out * (1.0 / total)).astype(BF16)
        if head == H - 1:
            ctx_ref[0, block_of(block), :] = ctxt_ref[block % 2].T

    stages = (score, soften, combine)
    tasks = [(block, head) for block in range(blocks) for head in range(H)]
    quarter = len(tasks) // 4
    staggered(tasks[:quarter], stages)

    @pl.when(row == 0)
    def _():
        for o in range(dp // 2 + 1, dp):
            late.spread(o)
            late.far(o)

    staggered(tasks[quarter : 2 * quarter], stages)

    @pl.when(row == 0)
    def _():
        for o in range(2, dp - 1):
            late.relay(o)

    @pl.when(row == rows - 1)
    def _():
        late.share()

    staggered(tasks[2 * quarter :], stages)

    @pl.when(row == 0)
    def _():
        late.relay(dp - 1)
        late.near()

    @pl.when(row == rows - 1)
    def _():
        late.arrive()
        early.close()
        late.close()
        for copy in row_copies(row) + table_copies():
            copy.wait()


def backward_attention(
    lengths_ref, q_ref, qt_ref, k_ref, kt_ref, v_ref, lse_ref, grad_ref, first_ref, lowt_in, weight_in,
    late_ref, sums_ref, bsum_ref,
    input_out, late_sum_ref, weight_sum_ref, place_sum_ref,
    weight_ref, input_ref, load_sems, input_sems, lowt_ref, gradt_ref, dqt_ref, dk_ref, dv_ref, every_ref, start_ref, total_ref, wpart_ref, ppart_ref, own_ref,
    own_sem, first_sem, *scratch,
):
    step = pl.program_id(0)
    last = H // 2 - 1
    rows, width, seq = lowt_in.shape
    blocks = seq // WIN
    at = Place()
    dp = at.dp
    group = members(at.side)
    r = width // len(group)
    c = width // dp
    narrow = r
    held = seq // dp
    folds = c // narrow
    per = held // folds
    few = sums_ref.shape[0] // dp
    single = bsum_ref.shape[1] // (dp * len(group))
    shared = dp // (H // 2)
    count = Reduce.COUNT
    late = Reduce(late_ref, scratch[:count], at, (own_ref, own_sem))
    weights = Reduce(wpart_ref, scratch[count : 2 * count], at)
    places = Reduce(ppart_ref, scratch[2 * count :], at)
    first_copy = pltpu.make_async_copy(first_ref, start_ref, first_sem)
    loads = [
        pltpu.make_async_copy(lowt_in.at[row], lowt_ref.at[:, row * seq : (row + 1) * seq], load_sems.at[row])
        for row in range(rows)
    ]
    loads.append(pltpu.make_async_copy(weight_in, weight_ref, load_sems.at[rows]))
    arriving = loads + [first_copy]

    def input_copy(e):
        spot = (slice(None), slice(e * held, (e + 1) * held))
        return pltpu.make_async_copy(input_ref.at[spot], input_out.at[spot], input_sems.at[e])

    pieces = lambda j: [j * shared + n for n in range(shared)]
    nearest = [at.at_dp(n + 1) for n in range(dp)]

    @pl.when(step == 0)
    def _():
        greet(at)
        for load in arriving:
            load.start()
        late.own_half().start()
        total_ref[...] = sums_ref[...]

    for row in range(rows):
        for block in range(blocks):
            gradt_ref[row, :, block_of(block)] = grad_ref[row, block_of(block), :].T

    @pl.when(step == 0)
    def _():
        meet(dp + 2 * at.side - 2)
        for e in nearest:
            late.begin(e)

    def score(row, block, head):
        q_head = head_rows(qt_ref[row, :, block_of(block)], head)
        g_head = head_rows(gradt_ref[row, :, block_of(block)], head)
        scores = [nn(k_ref[row, spot, :], q_head) for spot in spots_of(block)]
        return scores, [nn(v_ref[row, spot, :], g_head) for spot in spots_of(block)]

    def soften(row, block, head, products):
        scores, prob_grads = products
        lse = lse_ref[row, 0, head : head + 1, block_of(block)]
        probs = [jnp.exp(causal(scores[0]) - lse)]
        if block:
            probs.append(jnp.exp(scores[1] - (lse - apart(lengths_ref, row, block))))
        inner = sum(jnp.sum(p * g, 0, keepdims=True) for p, g in zip(probs, prob_grads))
        score_grads = [(p * (g - inner)).astype(BF16) for p, g in zip(probs, prob_grads)]
        return [p.astype(BF16) for p in probs], score_grads

    waiting = {}

    def combine(row, block, head, soft):
        half = slice(head * HD, (head + 1) * HD)
        dq = sum(nn(kt_ref[row, half, spot], x) for spot, x in zip(spots_of(block), soft[1]))
        dqt_ref[row, half, block_of(block)] = (dq * 0.125).astype(BF16)
        if head == 0:
            waiting[row, block] = soft
            return
        even = waiting.pop((row, block))
        g = grad_ref[row, block_of(block), :]
        q = q_ref[row, block_of(block), :]
        g_both = jnp.concatenate([head_lanes(g, 0), head_lanes(g, 1)], 0)
        q_both = jnp.concatenate([head_lanes(q, 0), head_lanes(q, 1)], 0)
        for n, spot in enumerate(spots_of(block)):
            dv = nn(jnp.concatenate([even[0][n], soft[0][n]], 1), g_both)
            dk = nn(jnp.concatenate([even[1][n], soft[1][n]], 1), q_both)
            if n or block == blocks - 1:
                dv_ref[row, spot, :] = dv
                dk_ref[row, spot, :] = dk
            else:
                dv_ref[row, spot, :] += dv
                dk_ref[row, spot, :] += dk

    def attend(*chosen):
        tasks = [(row, block, head) for block in chosen for row in range(rows) for head in range(2)]
        staggered(tasks, (score, soften, combine))
        for row in range(rows):
            for block in chosen:
                spot = block_of(block)
                every = [dqt_ref[row, :, spot].T, dk_ref[row, spot, :].astype(BF16), dv_ref[row, spot, :].astype(BF16)]
                every_ref[row * seq + block * WIN : row * seq + (block + 1) * WIN, :] = jnp.concatenate(every, 1)

    half = dp // 2
    downward = list(range(blocks))[::-1]
    feats = pl.ds(pl.multiple_of(step * PAIR, PAIR), PAIR)

    def sum_tokens():
        total_ref[0:1, feats] = column_sum(every_ref[:, :PAIR])
        total_ref[1:2, feats] = column_sum(every_ref[:, 2 * PAIR :])

    def send_weights():
        owned = nn(lowt_ref[...], every_ref[...])
        for i, e in enumerate(pieces(step)):
            for f, (a, b, core) in enumerate(group):
                for n in range(3):
                    lanes = slice(n * PAIR + i * c, n * PAIR + (i + 1) * c)
                    wpart_ref[e, a, b, core, n * r : (n + 1) * r, :] = owned[f * r : (f + 1) * r, lanes].astype(BF16)
            weights.begin(e)

    def column():
        return jnp.concatenate(
            [weight_ref[:, pl.ds(pl.multiple_of(n * width + step * PAIR, PAIR), PAIR)] for n in range(3)], 1
        )

    def weights_on():
        @pl.when(step > 0)
        def _():
            for e in pieces(step - 1):
                weights.across(e)

    @pl.when(step < last)
    def _():
        attend(*downward[: blocks // 2])

        @pl.when(step == 0)
        def _():
            late.own_half().wait()
            for e in nearest:
                late.across(e)

        @pl.when(step == 1)
        def _():
            for e in nearest[: half // 2]:
                late.middle(e)

        @pl.when(step == 2)
        def _():
            for e in nearest[half : half + half // 2]:
                late.middle(e)
            for e in nearest[: half // 2]:
                late.along(e)

        weights_on()
        attend(*downward[blocks // 2 :])

        @pl.when(step == 0)
        def _():
            for load in arriving:
                load.wait()

        sum_tokens()
        send_weights()

        @pl.when(step == 1)
        def _():
            for e in nearest[half // 2 : half]:
                late.middle(e)

        @pl.when(step == 2)
        def _():
            for e in nearest[half + half // 2 :]:
                late.middle(e)
            for e in nearest[half // 2 : half]:
                late.along(e)
            for e in pieces(0):
                weights.middle(e)

        tile = 2 * WIN
        turned = column()
        for row in range(rows):
            for n in range(seq // tile):
                spot = slice(n * tile, (n + 1) * tile)
                start_ref[row, spot, :] += nt(every_ref[row * seq + n * tile : row * seq + (n + 1) * tile, :], turned)

    @pl.when(step == last)
    def _():
        wide = lambda x: jnp.concatenate([x, jnp.zeros((x.shape[0], c - x.shape[1]), F32)], 1)
        turned = column()

        def finish(e):
            total = None
            for row in range(rows):
                spot = slice(e * held, (e + 1) * held)
                grad = start_ref[row, spot, :] + nt(every_ref[row * seq + e * held : row * seq + (e + 1) * held, :], turned)
                input_ref[row, spot, :] = grad.astype(BF16)
                total = grad if total is None else total + grad
            total = total.astype(BF16)
            for f, (a, b, core) in enumerate(group):
                lanes = slice(f * narrow, (f + 1) * narrow)
                ppart_ref[e, a, b, core, :per, :] = jnp.concatenate(
                    [total[n * per : (n + 1) * per, lanes] for n in range(folds)], 1
                )
                table = total_ref[e * few : (e + 1) * few, lanes]
                spot = (e * len(group) + f) * single
                line = bsum_ref[:, spot : spot + single]
                filler = jnp.zeros((SMALL - few - 1, c), F32)
                ppart_ref[e, a, b, core, per:, :] = jnp.concatenate([wide(table), wide(line), filler], 0).astype(BF16)
            places.begin(e)
            input_copy(e).start()

        def places_of(block):
            return [e for e in range(dp) if e * held // WIN == block]

        def on(step_of, *chosen):
            for block in chosen:
                for e in places_of(block):
                    step_of(e)

        attend(*downward[: blocks // 2])
        for e in nearest[half:]:
            late.along(e)
        weights_on()
        on(finish, *downward[: blocks // 2])
        attend(*downward[blocks // 2 : -1])
        on(finish, *downward[blocks // 2 : -1])
        for e in pieces(last - 2):
            weights.middle(e)
        for e in pieces(last - 3):
            weights.along(e)
        on(places.across, *downward[: blocks // 2])
        attend(downward[-1])
        sum_tokens()
        on(finish, downward[-1])
        on(places.across, *downward[blocks // 2 : -1])
        send_weights()
        for e in pieces(last - 1):
            weights.middle(e)
        on(places.middle, *downward[: blocks // 2])
        on(places.across, downward[-1])
        for e in pieces(last):
            weights.across(e)
        on(places.middle, *downward[blocks // 2 : -1])
        on(places.along, *downward[: blocks // 2])
        for e in pieces(last - 2) + pieces(last - 1):
            weights.along(e)
        on(places.middle, downward[-1])
        on(places.along, *downward[blocks // 2 : -1])
        for e in pieces(last):
            weights.middle(e)
        late_sum_ref[...] = late.result()
        on(places.along, downward[-1])
        for e in pieces(last):
            weights.along(e)
        place_sum_ref[...] = places.result()
        weight_sum_ref[...] = weights.result()
        late.close()
        weights.close()
        places.close()
        for e in range(dp):
            input_copy(e).wait()


def hand_out(
    late_ref, weight_ref, place_ref, input_ref,
    out_ref, wq_ref, wk_ref, wv_ref, wo_ref, wi_ref, w2_ref, table_ref, placet_ref, line_ref,
    held_ref, in_sems, out_sems,
):
    pieces = in_sems.shape[0]
    some = input_ref.shape[0] // pieces
    spots = [slice(n * some, (n + 1) * some) for n in range(pieces)]
    loads = [pltpu.make_async_copy(input_ref.at[x], held_ref.at[x], in_sems.at[n]) for n, x in enumerate(spots)]
    stores = [pltpu.make_async_copy(held_ref.at[x], out_ref.at[x], out_sems.at[n]) for n, x in enumerate(spots)]
    for load in loads:
        load.start()
    r, c = wq_ref.shape
    few, narrow = table_ref.shape
    held = placet_ref.shape[1]
    folds = c // narrow
    per = held // folds
    for n, ref in enumerate((wq_ref, wk_ref, wv_ref)):
        ref[...] = weight_ref[n * r : (n + 1) * r, :]
    wide_parts = wi_ref.shape[1] // c
    wo_ref[...] = late_ref[:r, :]
    for n in range(wide_parts):
        wi_ref[:, n * c : (n + 1) * c] = late_ref[(1 + n) * r : (2 + n) * r, :]
    w2_ref[...] = late_ref[(1 + wide_parts) * r :, :]
    place = place_ref[:per, :]
    placet_ref[...] = jnp.concatenate([place[:, n * narrow : (n + 1) * narrow] for n in range(folds)], 0).T
    table_ref[...] = place_ref[per : per + few, :narrow]
    line_ref[...] = place_ref[per + few : per + few + 1, : line_ref.shape[1]]
    for load, store in zip(loads, stores):
        load.wait()
        store.start()
    for store in stores:
        store.wait()


def feed_forward(
    ctx_ref, act_ref, pos_ref, cot_ref, late_ref, vec_ref, bias_ref,
    out_ref, first_ref, grad_ref, part_out, sums_ref, bsum_ref,
    wo_acc, wi_acc, w2_acc, slope_ref, wo_ref, wi_ref, w2_ref, part_ref, sems,
):
    step = pl.program_id(0)
    width = ctx_ref.shape[1]
    dp, side, _, _, _, c = late_ref.shape
    group = members(side)
    r = width // len(group)
    parts = bias_ref.shape[1] // dp // c
    tall = bias_ref.shape[1] // len(group)
    spans = [slice(0, r), slice(r, (1 + parts) * r), slice((1 + parts) * r, (1 + parts) * r + tall)]
    everywhere = (slice(None),) * 4

    def fetch(n):
        at = everywhere + (spans[n],)
        return pltpu.make_async_copy(late_ref.at[at], part_ref.at[at], sems.at[n])

    def deliver(n):
        at = everywhere + (spans[n],)
        return pltpu.make_async_copy(part_ref.at[at], part_out.at[at], sems.at[3 + n])

    hidden = bias_ref.shape[1]
    part = 512

    @pl.when(step == 0)
    def _():
        for n in range(3):
            fetch(n).start()
        wo_acc[...] = jnp.zeros_like(wo_acc)
        wi_acc[...] = jnp.zeros_like(wi_acc)
        w2_acc[...] = jnp.zeros_like(w2_acc)
        sums_ref[...] = jnp.zeros_like(sums_ref)
        bsum_ref[...] = jnp.zeros_like(bsum_ref)
        fetch(0).wait()
        for f, (a, b, core) in enumerate(group):
            wo_ref[f * r : (f + 1) * r, :] = jnp.concatenate([part_ref[e, a, b, core, :r, :] for e in range(dp)], 1)
        fetch(1).wait()
        for f, (a, b, core) in enumerate(group):
            wi_ref[f * r : (f + 1) * r, :] = jnp.concatenate(
                [part_ref[e, a, b, core, (1 + n) * r : (2 + n) * r, :] for e in range(dp) for n in range(parts)], 1
            )
        fetch(2).wait()
        for f, (a, b, core) in enumerate(group):
            w2_ref[f * tall : (f + 1) * tall, :] = jnp.concatenate(
                [part_ref[e, a, b, core, (1 + parts) * r :, :] for e in range(dp)], 1
            )

    vec = lambda n: vec_ref[n : n + 1, :]
    ctx = ctx_ref[...]
    first_sum = act_ref[...].astype(F32) + pos_ref[...].astype(F32) + (nn(ctx, wo_ref[...]) + vec(2))
    center = first_sum - jnp.mean(first_sum, -1, keepdims=True)
    scale_one = lax.rsqrt(jnp.mean(center * center, -1, keepdims=True) + 1e-05)
    z_one = center * scale_one
    normed = z_one * vec(3) + vec(4)
    normed_low = normed.astype(BF16)
    branch = None
    acts = []
    C = hidden // part
    cols = [slice(n * part, (n + 1) * part) for n in range(C)]
    pre_next = nn(normed_low, wi_ref[:, cols[0]])
    for n in range(C):
        pre = pre_next + bias_ref[:, cols[n]]
        if n + 1 < C:
            pre_next = nn(normed_low, wi_ref[:, cols[n + 1]])
        if n >= 1:
            term = nn(acts[n - 1], w2_ref[cols[n - 1], :])
            branch = term if branch is None else branch + term
        square = pre * pre
        t = jnp.tanh(pre * (0.7978845608028654 + (0.7978845608028654 * 0.044715) * square))
        half = 0.5 + 0.5 * t
        acts.append((pre * half).astype(BF16))
        slope_ref[:, cols[n]] = half + (0.5 * pre) * (1.0 - t * t) * (
            0.7978845608028654 + (3.0 * 0.7978845608028654 * 0.044715) * square
        )
    term = nn(acts[C - 1], w2_ref[cols[C - 1], :])
    branch = term if branch is None else branch + term
    second_sum = normed + (branch + vec(5))
    center = second_sum - jnp.mean(second_sum, -1, keepdims=True)
    scale_two = lax.rsqrt(jnp.mean(center * center, -1, keepdims=True) + 1e-05)
    z_two = center * scale_two
    out_ref[...] = (z_two * vec(6) + vec(7)).astype(BF16)
    cot = cot_ref[...].astype(F32)
    sums_ref[6:7, :] += column_sum(cot * z_two)
    sums_ref[7:8, :] += column_sum(cot)
    e = cot * vec(6)
    second_grad = scale_two * (
        e - jnp.mean(e, -1, keepdims=True) - z_two * jnp.mean(e * z_two, -1, keepdims=True)
    )
    branch_grad = second_grad.astype(BF16)
    sums_ref[5:6, :] += column_sum(branch_grad)
    branch_t = branch_grad.T
    normed_t = normed_low.T
    normed_grad = second_grad
    grad_next = nt(branch_grad, w2_ref[cols[0], :])
    lows = []

    def weights(n):
        wi_acc[:, cols[n]] += nn(normed_t, lows[n])
        return nt(lows[n], wi_ref[:, cols[n]])

    for n in range(C):
        pre_grad = grad_next * slope_ref[:, cols[n]]
        if n + 1 < C:
            grad_next = nt(branch_grad, w2_ref[cols[n + 1], :])
        w2_acc[:, cols[n]] += nn(branch_t, acts[n])
        if n >= 1:
            normed_grad = normed_grad + weights(n - 1)
        lows.append(pre_grad.astype(BF16))
        bsum_ref[:, cols[n]] += column_sum(lows[n])
    normed_grad = normed_grad + weights(C - 1)
    sums_ref[3:4, :] += column_sum(normed_grad * z_one)
    sums_ref[4:5, :] += column_sum(normed_grad)
    e = normed_grad * vec(3)
    first_grad = scale_one * (
        e - jnp.mean(e, -1, keepdims=True) - z_one * jnp.mean(e * z_one, -1, keepdims=True)
    )
    first_ref[...] = first_grad
    attn_grad = first_grad.astype(BF16)
    sums_ref[2:3, :] += column_sum(attn_grad)
    wo_acc[...] += nn(ctx.T, attn_grad)
    grad_ref[...] = nt(attn_grad, wo_ref[...]).astype(BF16)

    @pl.when(step == pl.num_programs(0) - 1)
    def _():
        for e in range(dp):
            for f, (a, b, core) in enumerate(group):
                for n in range(parts):
                    wide = slice((e * parts + n) * c, (e * parts + n + 1) * c)
                    rows = slice((1 + n) * r, (2 + n) * r)
                    part_ref[e, a, b, core, rows, :] = wi_acc[f * r : (f + 1) * r, wide].astype(BF16)
        deliver(1).start()
        for e in range(dp):
            for f, (a, b, core) in enumerate(group):
                turned = w2_acc[e * c : (e + 1) * c, f * tall : (f + 1) * tall].astype(BF16)
                part_ref[e, a, b, core, (1 + parts) * r :, :] = turned.T
        deliver(2).start()
        for e in range(dp):
            for f, (a, b, core) in enumerate(group):
                part_ref[e, a, b, core, :r, :] = wo_acc[f * r : (f + 1) * r, e * c : (e + 1) * c].astype(BF16)
        deliver(0).start()
        for n in range(3):
            deliver(n).wait()


def whole(shape):
    return pl.BlockSpec(shape, lambda *_: (0,) * len(shape))


def once(shape):
    return pl.BlockSpec(shape, lambda *_: (0,) * len(shape), pipeline_mode=pl.Buffered(1))


def run_forward(lengths, act, wq, wk, wv, wo, wi, w2, table, place, line):
    rows, seq, width = act.shape
    dp, side = lax.axis_size("dp"), side_of(lax.axis_size("fsdp"))
    r, c = wq.shape
    hidden = wi.shape[1] * dp
    first_rows = 3 * r + place.shape[0] * place.shape[1] // c + SMALL
    late_rows = r + r * wi.shape[1] // c + w2.shape[0]
    row3 = lambda shape: pl.BlockSpec((1,) + shape, lambda i: (i,) + (0,) * len(shape))
    seqs = row3((seq, width))
    st, tt = jax.ShapeDtypeStruct((rows, seq, width), BF16), jax.ShapeDtypeStruct((rows, width, seq), BF16)
    small = [x.shape for x in (wq, wk, wv, wo, wi, w2, table, place, line)]
    anywhere = pl.BlockSpec(memory_space=pl.ANY)
    return pl.pallas_call(
        forward_attention,
        grid=(rows,),
        in_specs=[pl.BlockSpec(memory_space=pltpu.SMEM), seqs] + [whole(x) for x in small],
        out_specs=[anywhere] * 6 + [seqs, row3((H // 2, 2, seq)), anywhere, anywhere,
                                    whole((table.shape[0] * dp, width)), whole((1, hidden)), anywhere],
        scratch_shapes=[
            pltpu.VMEM((1, seq, width), BF16),
            pltpu.VMEM((1, width, seq), BF16),
            pltpu.VMEM((1, seq, width), BF16),
            pltpu.VMEM((1, width, seq), BF16),
            pltpu.VMEM((1, seq, width), BF16),
            pltpu.VMEM((1, width, seq), BF16),
            pltpu.VMEM((width, 3 * width), BF16),
            pltpu.VMEM((seq, width), BF16),
            pltpu.SemaphoreType.DMA((8,)),
            pltpu.VMEM((width, seq), BF16),
            pltpu.VMEM((2, width, WIN), BF16),
            pltpu.VMEM((dp, side, side, 2, first_rows, c), BF16),
            pltpu.VMEM((late_rows, c), BF16),
            pltpu.SemaphoreType.DMA,
        ]
        + Gather.semaphores(dp, side) * 2,
        out_shape=[
            st, tt, st, tt, st, tt, st, jax.ShapeDtypeStruct((rows, H // 2, 2, seq), F32),
            jax.ShapeDtypeStruct((width, 3 * width), BF16),
            jax.ShapeDtypeStruct((seq, width), BF16),
            jax.ShapeDtypeStruct((table.shape[0] * dp, width), F32),
            jax.ShapeDtypeStruct((1, hidden), F32),
            jax.ShapeDtypeStruct((dp, side, side, 2, late_rows, c), BF16),
        ],
        compiler_params=pltpu.CompilerParams(
            vmem_limit_bytes=VMEM_LIMIT, collective_id=0, has_side_effects=True
        ),
        name="forward_attention",
    )(lengths, act, wq, wk, wv, wo, wi, w2, table, place, line)


def run_backward(lengths, q, qt, k, kt, v, lse, grad, first, lowt, weight, late, sums, bsum):
    rows, seq, width = grad.shape
    dp, side = late.shape[:2]
    late_rows, c = late.shape[4:]
    r = width // (2 * side * side)
    weight_rows = 3 * r
    place_rows = (seq // dp) * r // c + SMALL
    lanes = pl.BlockSpec((rows, seq, PAIR), lambda j: (0, 0, j))
    turned = pl.BlockSpec((rows, PAIR, seq), lambda j: (0, j, 0))
    anywhere = pl.BlockSpec(memory_space=pl.ANY)
    totals = [(n, c) for n in (late_rows, weight_rows, place_rows)]
    return pl.pallas_call(
        backward_attention,
        grid=(H // 2,),
        in_specs=[pl.BlockSpec(memory_space=pltpu.SMEM), lanes, turned, lanes, turned, lanes,
                  pl.BlockSpec((rows, 1, 2, seq), lambda j: (0, j, 0, 0)), lanes, anywhere, anywhere, anywhere,
                  anywhere, once(sums.shape), once(bsum.shape)],
        out_specs=[anywhere] + [whole(x) for x in totals],
        scratch_shapes=[
            pltpu.VMEM(weight.shape, BF16),
            pltpu.VMEM(grad.shape, BF16),
            pltpu.SemaphoreType.DMA((rows + 1,)),
            pltpu.SemaphoreType.DMA((dp,)),
            pltpu.VMEM((width, rows * seq), BF16),
            pltpu.VMEM((rows, PAIR, seq), BF16),
            pltpu.VMEM((rows, PAIR, seq), BF16),
            pltpu.VMEM((rows, seq, PAIR), F32),
            pltpu.VMEM((rows, seq, PAIR), F32),
            pltpu.VMEM((rows * seq, 3 * PAIR), BF16),
            pltpu.VMEM((rows, seq, width), F32),
            pltpu.VMEM(sums.shape, F32),
            pltpu.VMEM((dp, side, side, 2, weight_rows, c), BF16),
            pltpu.VMEM((dp, side, side, 2, place_rows, c), BF16),
            pltpu.VMEM((dp, side, side, late_rows, c), BF16),
            pltpu.SemaphoreType.DMA,
            pltpu.SemaphoreType.DMA,
        ]
        + Reduce.scratch(dp, side, late_rows, c)
        + Reduce.scratch(dp, side, weight_rows, c)
        + Reduce.scratch(dp, side, place_rows, c),
        out_shape=[jax.ShapeDtypeStruct(grad.shape, BF16)] + [jax.ShapeDtypeStruct(x, F32) for x in totals],
        compiler_params=pltpu.CompilerParams(
            vmem_limit_bytes=VMEM_LIMIT, collective_id=1, has_side_effects=True
        ),
        name="backward_attention",
    )(lengths, q, qt, k, kt, v, lse, grad, first, lowt, weight, late, sums, bsum)


def run_hand_out(late, weight, place, grad, shapes):
    vmem, anywhere = pl.BlockSpec(memory_space=pltpu.VMEM), pl.BlockSpec(memory_space=pl.ANY)
    tokens = grad.reshape(-1, grad.shape[-1])
    return pl.pallas_call(
        hand_out,
        in_specs=[vmem, vmem, vmem, anywhere],
        out_specs=[anywhere] + [vmem] * len(shapes),
        out_shape=[jax.ShapeDtypeStruct(tokens.shape, BF16)] + [jax.ShapeDtypeStruct(x, F32) for x in shapes],
        scratch_shapes=[
            pltpu.VMEM(tokens.shape, BF16), pltpu.SemaphoreType.DMA((4,)), pltpu.SemaphoreType.DMA((4,)),
        ],
        name="hand_out",
    )(late, weight, place, tokens)


def run_feed_forward(ctx, act, pos, cot, late, vec, bias, tile=512):
    tokens, width = ctx.shape
    seq = pos.shape[0]
    hidden = bias.shape[1]
    per_row = seq // tile
    tok = pl.BlockSpec((tile, width), lambda t: (t, 0))
    return pl.pallas_call(
        feed_forward,
        grid=(tokens // tile,),
        in_specs=[tok, tok, pl.BlockSpec((tile, width), lambda t: (t % per_row, 0)), tok,
                  pl.BlockSpec(memory_space=pl.ANY), whole(vec.shape), whole(bias.shape)],
        out_specs=[tok, tok, tok, pl.BlockSpec(memory_space=pl.ANY), whole((8, width)),
                   whole((1, hidden))],
        scratch_shapes=[
            pltpu.VMEM((width, width), F32),
            pltpu.VMEM((width, hidden), F32),
            pltpu.VMEM((width, hidden), F32),
            pltpu.VMEM((tile, hidden), F32),
            pltpu.VMEM((width, width), BF16),
            pltpu.VMEM((width, hidden), BF16),
            pltpu.VMEM((hidden, width), BF16),
            pltpu.VMEM(late.shape, BF16),
            pltpu.SemaphoreType.DMA((6,)),
        ],
        out_shape=[
            jax.ShapeDtypeStruct((tokens, width), BF16),
            jax.ShapeDtypeStruct((tokens, width), F32),
            jax.ShapeDtypeStruct((tokens, width), BF16),
            jax.ShapeDtypeStruct(late.shape, BF16),
            jax.ShapeDtypeStruct((8, width), F32),
            jax.ShapeDtypeStruct((1, hidden), F32),
        ],
        compiler_params=pltpu.CompilerParams(vmem_limit_bytes=VMEM_LIMIT),
        name="feed_forward",
    )(ctx, act, pos, cot, late, vec, bias)


def shards(
    activations, window_lengths, query_weight, key_weight, value_weight, output_weight, inner_weight, outer_weight,
    vectors, positions, inner_bias, output_cotangent,
):
    rows, seq, width = activations.shape
    q, qt, k, kt, v, lowt, ctx, lse, weight, pos, vec, bias, late = run_forward(
        window_lengths, activations, query_weight, key_weight, value_weight, output_weight, inner_weight, outer_weight,
        vectors, positions.T, inner_bias.reshape(1, -1),
    )
    flat = lambda x: x.reshape(rows * seq, width)
    deep = lambda x: x.reshape(rows, seq, width)
    out, first, grad, part, sums, bsum = run_feed_forward(
        flat(ctx), flat(activations), pos, flat(output_cotangent), late, vec, bias
    )
    input_grad, *sums = run_backward(
        window_lengths, q, qt, k, kt, v, lse, deep(grad), deep(first), lowt, weight, part, sums, bsum
    )
    shapes = [x.shape for x in (query_weight, key_weight, value_weight, output_weight, inner_weight, outer_weight,
                                vectors, positions.T)] + [(1, inner_bias.shape[0])]
    owned = run_hand_out(*sums, input_grad, shapes)
    return (deep(out), owned[0].reshape(input_grad.shape)) + tuple(owned[1:8]) + (owned[8].T, owned[9].reshape(-1))


def solution(mesh):
    tokens = P(("dp", "fsdp"), None, None)
    matrix = P("fsdp", "dp")
    table = P("dp", "fsdp")
    line = P(("dp", "fsdp"))
    return jax.shard_map(
        shards,
        mesh=mesh,
        in_specs=(tokens, P(("dp", "fsdp"), None)) + (matrix,) * 6 + (table, table, line, tokens),
        out_specs=(tokens, tokens) + (matrix,) * 6 + (table, table, line),
        check_vma=False,
    )
```

```python
import functools

import jax
import jax.numpy as jnp
from jax import lax
from jax.experimental import pallas as pl
from jax.experimental.pallas import tpu as pltpu
from jax.sharding import PartitionSpec as P

H = 8
HD = 64
WIN = 256
PAIR = 2 * HD
VMEM_LIMIT = 62 * 1024 * 1024
F32 = jnp.float32
BF16 = jnp.bfloat16
MESH = pl.DeviceIdType.MESH
SMALL = 16
LATER = 2


def nn(left, right):
    return lax.dot_general(left, right, (((1,), (0,)), ((), ())), preferred_element_type=F32)


def nt(left, right):
    return lax.dot_general(left, right, (((1,), (1,)), ((), ())), preferred_element_type=F32)


def tn(left, right):
    return lax.dot_general(left, right, (((0,), (0,)), ((), ())), preferred_element_type=F32)


def column_sum(value):
    return jnp.sum(value.astype(F32), 0, keepdims=True)


def head_rows(pair, which):
    zeros = jnp.zeros((HD, pair.shape[1]), pair.dtype)
    if which == 0:
        return jnp.concatenate([pair[:HD], zeros], 0)
    return jnp.concatenate([zeros, pair[HD:]], 0)


def head_lanes(pair, which):
    lane = lax.broadcasted_iota(jnp.int32, pair.shape, 1)
    keep = (lane < HD) if which == 0 else (lane >= HD)
    return jnp.where(keep, pair, jnp.zeros_like(pair))


def causal(scores):
    key = lax.broadcasted_iota(jnp.int32, scores.shape, 0)
    query = lax.broadcasted_iota(jnp.int32, scores.shape, 1)
    return jnp.where(key <= query, scores, -1e30)


def block_of(block):
    return slice(block * WIN, (block + 1) * WIN)


def spots_of(block):
    return [block_of(n) for n in (block, block - 1) if n >= 0]


def pair_of(head):
    return slice(head // 2 * PAIR, (head // 2 + 1) * PAIR)


def staggered(tasks, stages):
    held = {}
    for step in range(len(tasks) + len(stages) - 1):
        for n, stage in enumerate(stages):
            task = step - n
            if 0 <= task < len(tasks):
                args = (held.pop(task),) if n else ()
                held[task] = stage(*tasks[task], *args)


class Place:
    def __init__(self):
        fsdp = lax.axis_index("fsdp")
        self.d, self.dp = lax.axis_index("dp"), lax.axis_size("dp")
        self.side = side_of(lax.axis_size("fsdp"))
        self.chip, self.core = fsdp // 2, lax.rem(fsdp, 2)
        y, x = self.chip // self.side, lax.rem(self.chip, self.side)
        self.a = y + self.core * (x - y)
        self.b = x + self.core * (y - x)

    def device(self, a, b):
        straight, turned = a * self.side + b, b * self.side + a
        return {"fsdp": (straight + self.core * (turned - straight)) * 2 + self.core}

    def sibling(self):
        return {"fsdp": self.chip * 2 + 1 - self.core}

    def at_a(self, n):
        return lax.rem(self.a + n + self.side, self.side)

    def at_b(self, n):
        return lax.rem(self.b + n + self.side, self.side)

    def at_dp(self, n):
        return lax.rem(self.d + n + self.dp, self.dp)


def side_of(fsdp):
    side = 1
    while side * side * 2 < fsdp:
        side += 1
    assert side * side * 2 == fsdp
    return side


def members(side):
    found = []
    for f in range(2 * side * side):
        y, x = f // 2 // side, f // 2 % side
        found.append((x, y, 1) if f % 2 else (y, x, 0))
    return found


def remote(src, dst, send, recv, device):
    return pltpu.make_async_remote_copy(
        src_ref=src, dst_ref=dst, send_sem=send, recv_sem=recv, device_id=device, device_id_type=MESH
    )


def greet(at):
    barrier = pltpu.get_barrier_semaphore()
    others = [{"dp": at.at_dp(n)} for n in range(1, at.dp)]
    others += [at.device(at.a, at.at_b(n)) for n in range(1, at.side)]
    others += [at.device(at.at_a(n), at.b) for n in range(1, at.side)]
    others.append(at.sibling())
    for other in others:
        pl.semaphore_signal(barrier, inc=1, device_id=other, device_id_type=MESH)
    return len(others)


def meet(count):
    pl.semaphore_wait(pltpu.get_barrier_semaphore(), count)


class Gather:
    COUNT = 8

    def __init__(self, buf, sems, at):
        self.buf, self.at = buf, at
        self.zs, self.zr, self.bs, self.br, self.sa, self.ra, self.cs, self.cr = sems

    @staticmethod
    def semaphores(dp, side):
        dma = pltpu.SemaphoreType.DMA
        shapes = [(dp,), (dp, side), (dp, side, side), (side, side)]
        return [dma(x) for x in shapes for _ in range(2)]

    def along_dp(self, o):
        at = self.at
        block = self.buf.at[at.d, at.a, at.b, at.core]
        return remote(block, block, self.zs.at[o], self.zr.at[o], {"dp": at.at_dp(o)})

    def along_b(self, o, p):
        at = self.at
        block = self.buf.at[at.at_dp(-o), at.a, at.b, at.core]
        return remote(block, block, self.bs.at[o, p], self.br.at[o, p], at.device(at.a, at.at_b(p)))

    def along_a(self, o, p, q):
        at = self.at
        block = self.buf.at[at.at_dp(-o), at.a, at.at_b(-p), at.core]
        return remote(block, block, self.sa.at[o, p, q], self.ra.at[o, p, q], at.device(at.at_a(q), at.b))

    def to_core(self, q, p):
        at = self.at
        block = self.buf.at[:, at.at_a(-q), at.at_b(-p), at.core]
        return remote(block, block, self.cs.at[q, p], self.cr.at[q, p], at.sibling())

    def begin(self):
        for o in range(1, self.at.dp):
            self.along_dp(o).start()

    def pass_on(self, o):
        for p in range(1, self.at.side):
            self.along_b(o, p).start()

    def far(self, o):
        for q in range(1, self.at.side):
            self.along_a(o, 0, q).start()

    def spread(self, o):
        self.along_dp(o).wait_recv()
        self.pass_on(o)

    def relay(self, o):
        for p in range(1, self.at.side):
            self.along_b(o, p).wait_recv()
            for q in range(1, self.at.side):
                self.along_a(o, p, q).start()

    def near(self):
        for p in range(self.at.side):
            self.to_core(0, p).start()

    def share(self):
        for p in range(self.at.side):
            for q in range(1, self.at.side):
                for o in range(self.at.dp):
                    self.along_a(o, p, q).wait_recv()
                self.to_core(q, p).start()

    def arrive(self):
        for q in range(self.at.side):
            for p in range(self.at.side):
                self.to_core(q, p).wait_recv()

    def close(self):
        for o in range(1, self.at.dp):
            self.along_dp(o).wait_send()
        for o in range(self.at.dp):
            for p in range(1, self.at.side):
                self.along_b(o, p).wait_send()
            for p in range(self.at.side):
                for q in range(1, self.at.side):
                    self.along_a(o, p, q).wait_send()
        for q in range(self.at.side):
            for p in range(self.at.side):
                self.to_core(q, p).wait_send()


def add_up(terms):
    if len(terms) == 2:
        return terms[0] + terms[1]
    return sum(x.astype(F32) for x in terms).astype(BF16)


class Reduce:
    COUNT = 13

    def __init__(self, part, scratch, at, own=None):
        self.part, self.at = part, at
        self.own, self.own_sem = own or (None, None)
        (self.pair, self.plane, self.row, self.mine, self.line,
         self.cs, self.cr, self.sa, self.ra, self.bs, self.br, self.zs, self.zr) = scratch

    @staticmethod
    def scratch(dp, side, rows, c):
        dma = pltpu.SemaphoreType.DMA
        return [
            pltpu.VMEM((dp, side, side, rows, c), BF16),
            pltpu.VMEM((side - 1, dp, side, rows, c), BF16),
            pltpu.VMEM((side - 1, dp, rows, c), BF16),
            pltpu.VMEM((dp, rows, c), BF16),
            pltpu.VMEM((dp - 1, rows, c), BF16),
        ] + [dma((dp,))] * 2 + [dma((dp, side))] * 4 + [dma((dp,))] * 2

    def to_core(self, e):
        at = self.at
        return remote(self.part.at[e, :, :, 1 - at.core], self.pair.at[e], self.cs.at[e], self.cr.at[e], at.sibling())

    def along_a(self, e, q):
        at = self.at
        to = at.at_a(q)
        return remote(
            self.pair.at[e, to], self.plane.at[q - 1, e], self.sa.at[e, q], self.ra.at[e, q], at.device(to, at.b)
        )

    def along_b(self, e, p):
        at = self.at
        to = at.at_b(p)
        return remote(
            self.pair.at[e, at.a, to], self.row.at[p - 1, e], self.bs.at[e, p], self.br.at[e, p], at.device(at.a, to)
        )

    def along_dp(self, o):
        at = self.at
        to = at.at_dp(o)
        return remote(self.mine.at[to], self.line.at[o - 1], self.zs.at[o], self.zr.at[o], {"dp": to})

    def own_half(self):
        return pltpu.make_async_copy(self.part.at[:, :, :, self.at.core], self.own, self.own_sem)

    def begin(self, e):
        self.to_core(e).start()

    def across(self, e):
        at = self.at
        self.to_core(e).wait_recv()
        for n in list(range(1, at.side)) + [0]:
            a = at.at_a(n)
            for b in range(at.side):
                own = self.part[e, a, b, at.core] if self.own is None else self.own[e, a, b]
                self.pair[e, a, b] = add_up([own, self.pair[e, a, b]])
            if n:
                self.along_a(e, n).start()

    def middle(self, e):
        at = self.at
        for q in range(1, at.side):
            self.along_a(e, q).wait_recv()
        for n in list(range(1, at.side)) + [0]:
            b = at.at_b(n)
            terms = [self.pair[e, at.a, b]] + [self.plane[q - 1, e, b] for q in range(1, at.side)]
            self.pair[e, at.a, b] = add_up(terms)
            if n:
                self.along_b(e, n).start()

    def along(self, e):
        at = self.at
        for p in range(1, at.side):
            self.along_b(e, p).wait_recv()
        self.mine[e] = add_up([self.pair[e, at.a, at.b]] + [self.row[p - 1, e] for p in range(1, at.side)])

        @pl.when(e != at.d)
        def _():
            self.along_dp(lax.rem(e - at.d + at.dp, at.dp)).start()

    def result(self):
        at = self.at
        for o in range(1, at.dp):
            self.along_dp(o).wait_recv()
        total = self.mine[at.d].astype(F32)
        for o in range(1, at.dp):
            total = total + self.line[o - 1].astype(F32)
        return total

    def close(self):
        at = self.at
        for e in range(at.dp):
            self.to_core(e).wait_send()
            for n in range(1, at.side):
                self.along_a(e, n).wait_send()
                self.along_b(e, n).wait_send()
        for o in range(1, at.dp):
            self.along_dp(o).wait_send()


def apart(lengths_ref, row, block):
    total = jnp.int32(0)
    cut = jnp.bool_(False)
    for n in range(lengths_ref.shape[1]):
        total = total + lengths_ref[row, n]
        cut = cut | (total == block * WIN)
    return jnp.where(cut, jnp.float32(-1e30), jnp.float32(0.0))


def forward_attention(
    lengths_ref, act_in, wq_ref, wk_ref, wv_ref, wo_ref, wi_ref, w2_ref, table_ref, place_ref, line_ref,
    q_out, qt_out, k_out, kt_out, v_out, lowt_out, ctx_ref, lse_ref, weight_out, pos_out, vec_ref, bias_ref, late_ref,
    act_ref, act_sems, q_ref, qt_ref, k_ref, kt_ref, v_ref, lowt_ref, weight_ref, pos_ref, out_sems,
    vt_ref, ctxt_ref, early_ref, own_ref, own_sem, *sems,
):
    row = pl.program_id(0)
    rows = pl.num_programs(0)
    width = act_in.shape[2]
    blocks = act_in.shape[1] // WIN
    at = Place()
    dp = at.dp
    here = (at.d, at.a, at.b, at.core)
    r, c = wq_ref.shape
    narrow, held = place_ref.shape
    folds = c // narrow
    per = held // folds
    early = Gather(early_ref, sems[: Gather.COUNT], at)
    late = Gather(late_ref, sems[Gather.COUNT :], at)

    def own_copy():
        return pltpu.make_async_copy(own_ref, late_ref.at[here], own_sem)

    def act_copy(of_row):
        return pltpu.make_async_copy(act_in.at[of_row], act_ref.at[of_row], act_sems.at[of_row])

    def row_copies(of_row):
        pairs = ((q_ref, q_out), (qt_ref, qt_out), (k_ref, k_out), (kt_ref, kt_out), (v_ref, v_out),
                 (lowt_ref, lowt_out))
        return [
            pltpu.make_async_copy(src.at[0], dst.at[of_row], out_sems.at[n]) for n, (src, dst) in enumerate(pairs)
        ]

    def table_copies():
        pairs = ((weight_ref, weight_out), (pos_ref, pos_out))
        return [pltpu.make_async_copy(src, dst, out_sems.at[6 + n]) for n, (src, dst) in enumerate(pairs)]

    @pl.when(row == 0)
    def _():
        count = greet(at)
        for n in range(act_in.shape[0]):
            act_copy(n).start()
        for n, ref in enumerate((wq_ref, wk_ref, wv_ref)):
            early_ref[here + (slice(n * r, (n + 1) * r),)] = ref[...]
        place = place_ref[...].T
        early_ref[here + (slice(3 * r, 3 * r + per),)] = jnp.concatenate(
            [place[n * per : (n + 1) * per] for n in range(folds)], 1
        )
        wide = lambda x: jnp.concatenate([x, jnp.zeros((x.shape[0], c - x.shape[1]), F32)], 1)
        table = wide(table_ref[...].astype(F32))
        line = wide(line_ref[...].astype(F32))
        few = table.shape[0]
        small = jnp.concatenate([table, line, jnp.zeros((SMALL - few - 1, c), F32)], 0)
        early_ref[here + (slice(3 * r + per, None),)] = small.astype(BF16)
        own_ref[:r, :] = wo_ref[...]
        wide_parts = wi_ref.shape[1] // c
        for n in range(wide_parts):
            own_ref[(1 + n) * r : (2 + n) * r, :] = wi_ref[:, n * c : (n + 1) * c]
        own_ref[(1 + wide_parts) * r :, :] = w2_ref[...]
        own_copy().start()
        meet(count)
        early.begin()
        early.pass_on(0)
        early.far(0)
        early.relay(0)
        for o in range(1, dp):
            early.spread(o)
        own_copy().wait()
        late.begin()
        for o in range(1, dp):
            early.relay(o)
            early.far(o)
        early.near()
        late.pass_on(0)
        late.far(0)
        early.share()
        late.relay(0)
        late.spread(1)
        late.far(1)
        early.arrive()
        group = members(at.side)
        for f, (a, b, core) in enumerate(group):
            for n in range(3):
                weight_ref[f * r : (f + 1) * r, n * width : (n + 1) * width] = jnp.concatenate(
                    [early_ref[e, a, b, core, n * r : (n + 1) * r, :] for e in range(dp)], 1
                )
        tables = []
        lines = []
        for e in range(dp):
            for n in range(folds):
                spot = slice(e * held + n * per, e * held + (n + 1) * per)
                pos_ref[spot, :] = jnp.concatenate(
                    [
                        early_ref[e, a, b, core, 3 * r : 3 * r + per, :][:, n * narrow : (n + 1) * narrow]
                        for a, b, core in group
                    ],
                    1,
                )
            smalls = [early_ref[e, a, b, core, 3 * r + per :, :].astype(F32) for a, b, core in group]
            tables.append(jnp.concatenate([x[:few, :narrow] for x in smalls], 1))
            lines.extend(x[few : few + 1, : line_ref.shape[1]] for x in smalls)
        vec_ref[...] = jnp.concatenate(tables, 0)
        bias_ref[...] = jnp.concatenate(lines, 1)
        for copy in table_copies():
            copy.start()

    @pl.when(row > 0)
    def _():
        for copy in row_copies(row - 1):
            copy.wait()

    act_copy(row).wait()

    def project(step, carry):
        spot = pl.ds(pl.multiple_of(step * WIN, WIN), WIN)
        low = (act_ref[row, spot, :].astype(F32) + pos_ref[spot, :].astype(F32)).astype(BF16)
        lowt_ref[0, :, spot] = low.T
        every = nn(low, weight_ref[...])
        q = (every[:, :width] + vec_ref[0:1, :]).astype(BF16)
        q = (q.astype(F32) * 0.125).astype(BF16)
        k = every[:, width : 2 * width].astype(BF16)
        v = (every[:, 2 * width :] + vec_ref[1:2, :]).astype(BF16)
        q_ref[0, spot, :] = q
        k_ref[0, spot, :] = k
        v_ref[0, spot, :] = v
        qt_ref[0, :, spot] = q.T
        kt_ref[0, :, spot] = k.T
        vt_ref[:, spot] = v.T
        return carry

    lax.fori_loop(0, blocks, project, 0)
    for copy in row_copies(row):
        copy.start()

    @pl.when(row == 0)
    def _():
        for o in range(2, dp // 2 + 1):
            late.spread(o)
            late.far(o)
        late.relay(1)

    def score(block, head):
        q_head = head_rows(qt_ref[0, pair_of(head), block_of(block)], head % 2)
        return [nn(k_ref[0, spot, pair_of(head)], q_head) for spot in spots_of(block)]

    def soften(block, head, scores):
        scores[0] = causal(scores[0])
        peaks = [jnp.max(x, 0, keepdims=True) for x in scores]
        peak = peaks[0]
        if block:
            peak = jnp.maximum(peak, peaks[1] + apart(lengths_ref, row, block))
        expo = [jnp.exp(scores[0] - peak)]
        if block:
            expo.append(jnp.exp(scores[1] - (peak - apart(lengths_ref, row, block))))
        total = sum(jnp.sum(x, 0, keepdims=True) for x in expo)
        lse_ref[0, head // 2, head % 2 : head % 2 + 1, block_of(block)] = peak + jnp.log(total)
        return [x.astype(BF16) for x in expo], total

    def combine(block, head, soft):
        expo, total = soft
        half = slice(head * HD, (head + 1) * HD)
        out = sum(nn(vt_ref[half, spot], x) for spot, x in zip(spots_of(block), expo))
        ctxt_ref[block % 2, half, :] = (out * (1.0 / total)).astype(BF16)
        if head == H - 1:
            ctx_ref[0, block_of(block), :] = ctxt_ref[block % 2].T

    stages = (score, soften, combine)
    tasks = [(block, head) for block in range(blocks) for head in range(H)]
    quarter = len(tasks) // 4
    staggered(tasks[:quarter], stages)

    @pl.when(row == 0)
    def _():
        for o in range(dp // 2 + 1, dp):
            late.spread(o)
            late.far(o)

    staggered(tasks[quarter : 2 * quarter], stages)

    @pl.when(row == 0)
    def _():
        for o in range(2, dp - 1):
            late.relay(o)

    @pl.when(row == rows - 1)
    def _():
        late.share()

    staggered(tasks[2 * quarter :], stages)

    @pl.when(row == 0)
    def _():
        late.relay(dp - 1)
        late.near()

    @pl.when(row == rows - 1)
    def _():
        late.arrive()
        early.close()
        late.close()
        for copy in row_copies(row) + table_copies():
            copy.wait()


def backward_attention(
    lengths_ref, q_ref, qt_ref, k_ref, kt_ref, v_ref, lse_ref, grad_ref, first_ref, lowt_in, weight_in,
    late_ref, sums_ref, bsum_ref,
    input_out, late_sum_ref, weight_sum_ref, place_sum_ref,
    weight_ref, input_ref, load_sems, input_sems, lowt_ref, gradt_ref, dqt_ref, dk_ref, dv_ref, every_ref, start_ref, total_ref, wpart_ref, ppart_ref, own_ref,
    own_sem, first_sem, *scratch,
):
    step = pl.program_id(0)
    last = H // 2 - 1
    rows, width, seq = lowt_in.shape
    blocks = seq // WIN
    at = Place()
    dp = at.dp
    group = members(at.side)
    r = width // len(group)
    c = width // dp
    narrow = r
    held = seq // dp
    folds = c // narrow
    per = held // folds
    few = sums_ref.shape[0] // dp
    single = bsum_ref.shape[1] // (dp * len(group))
    shared = dp // (H // 2)
    count = Reduce.COUNT
    late = Reduce(late_ref, scratch[:count], at, (own_ref, own_sem))
    weights = Reduce(wpart_ref, scratch[count : 2 * count], at)
    places = Reduce(ppart_ref, scratch[2 * count :], at)
    first_copy = pltpu.make_async_copy(first_ref, start_ref, first_sem)
    loads = [
        pltpu.make_async_copy(lowt_in.at[row], lowt_ref.at[:, row * seq : (row + 1) * seq], load_sems.at[row])
        for row in range(rows)
    ]
    loads.append(pltpu.make_async_copy(weight_in, weight_ref, load_sems.at[rows]))
    arriving = loads + [first_copy]

    def input_copy(e):
        spot = (slice(None), slice(e * held, (e + 1) * held))
        return pltpu.make_async_copy(input_ref.at[spot], input_out.at[spot], input_sems.at[e])

    pieces = lambda j: [j * shared + n for n in range(shared)]
    nearest = [at.at_dp(n + 1) for n in range(dp)]

    @pl.when(step == 0)
    def _():
        greet(at)
        for load in arriving:
            load.start()
        late.own_half().start()
        total_ref[...] = sums_ref[...]

    for row in range(rows):
        for block in range(blocks):
            gradt_ref[row, :, block_of(block)] = grad_ref[row, block_of(block), :].T

    def score(row, block, head):
        q_head = head_rows(qt_ref[row, :, block_of(block)], head)
        g_head = head_rows(gradt_ref[row, :, block_of(block)], head)
        scores = [nn(k_ref[row, spot, :], q_head) for spot in spots_of(block)]
        return scores, [nn(v_ref[row, spot, :], g_head) for spot in spots_of(block)]

    def soften(row, block, head, products):
        scores, prob_grads = products
        lse = lse_ref[row, 0, head : head + 1, block_of(block)]
        probs = [jnp.exp(causal(scores[0]) - lse)]
        if block:
            probs.append(jnp.exp(scores[1] - (lse - apart(lengths_ref, row, block))))
        inner = sum(jnp.sum(p * g, 0, keepdims=True) for p, g in zip(probs, prob_grads))
        score_grads = [(p * (g - inner)).astype(BF16) for p, g in zip(probs, prob_grads)]
        return [p.astype(BF16) for p in probs], score_grads

    waiting = {}

    def combine(row, block, head, soft):
        half = slice(head * HD, (head + 1) * HD)
        dq = sum(nn(kt_ref[row, half, spot], x) for spot, x in zip(spots_of(block), soft[1]))
        dqt_ref[row, half, block_of(block)] = (dq * 0.125).astype(BF16)
        if head == 0:
            waiting[row, block] = soft
            return
        even = waiting.pop((row, block))
        g = grad_ref[row, block_of(block), :]
        q = q_ref[row, block_of(block), :]
        g_both = jnp.concatenate([head_lanes(g, 0), head_lanes(g, 1)], 0)
        q_both = jnp.concatenate([head_lanes(q, 0), head_lanes(q, 1)], 0)
        for n, spot in enumerate(spots_of(block)):
            dv = nn(jnp.concatenate([even[0][n], soft[0][n]], 1), g_both)
            dk = nn(jnp.concatenate([even[1][n], soft[1][n]], 1), q_both)
            if n or block == blocks - 1:
                dv_ref[row, spot, :] = dv
                dk_ref[row, spot, :] = dk
            else:
                dv_ref[row, spot, :] += dv
                dk_ref[row, spot, :] += dk

    def attend(*chosen):
        tasks = [(row, block, head) for block in chosen for row in range(rows) for head in range(2)]
        staggered(tasks, (score, soften, combine))
        for row in range(rows):
            for block in chosen:
                spot = block_of(block)
                every = [dqt_ref[row, :, spot].T, dk_ref[row, spot, :].astype(BF16), dv_ref[row, spot, :].astype(BF16)]
                every_ref[row * seq + block * WIN : row * seq + (block + 1) * WIN, :] = jnp.concatenate(every, 1)

    half = dp // 2
    downward = list(range(blocks))[::-1]
    feats = pl.ds(pl.multiple_of(step * PAIR, PAIR), PAIR)

    def sum_tokens():
        total_ref[0:1, feats] = column_sum(every_ref[:, :PAIR])
        total_ref[1:2, feats] = column_sum(every_ref[:, 2 * PAIR :])

    def send_weights():
        owned = nn(lowt_ref[...], every_ref[...])
        for i, e in enumerate(pieces(step)):
            for f, (a, b, core) in enumerate(group):
                for n in range(3):
                    lanes = slice(n * PAIR + i * c, n * PAIR + (i + 1) * c)
                    wpart_ref[e, a, b, core, n * r : (n + 1) * r, :] = owned[f * r : (f + 1) * r, lanes].astype(BF16)
            weights.begin(e)

    def column():
        return jnp.concatenate(
            [weight_ref[:, pl.ds(pl.multiple_of(n * width + step * PAIR, PAIR), PAIR)] for n in range(3)], 1
        )

    def weights_on():
        @pl.when(step > 0)
        def _():
            for e in pieces(step - 1):
                weights.across(e)

    @pl.when(step < last)
    def _():
        attend(*downward[: blocks // 2])

        @pl.when(step == 0)
        def _():
            meet(dp + 2 * at.side - 2)
            for e in nearest:
                late.begin(e)

        @pl.when(step == 1)
        def _():
            for e in nearest[: half // 2]:
                late.middle(e)

        @pl.when(step == 2)
        def _():
            for e in nearest[half : half + half // 2]:
                late.middle(e)
            for e in nearest[: half // 2]:
                late.along(e)

        weights_on()
        attend(*downward[blocks // 2 :])

        @pl.when(step == 0)
        def _():
            late.own_half().wait()
            for e in nearest:
                late.across(e)
            for load in arriving:
                load.wait()

        sum_tokens()
        send_weights()

        @pl.when(step == 1)
        def _():
            for e in nearest[half // 2 : half]:
                late.middle(e)

        @pl.when(step == 2)
        def _():
            for e in nearest[half + half // 2 :]:
                late.middle(e)
            for e in nearest[half // 2 : half]:
                late.along(e)
            for e in pieces(0):
                weights.middle(e)

        tile = 2 * WIN
        turned = column()
        for row in range(rows):
            for n in range(seq // tile):
                spot = slice(n * tile, (n + 1) * tile)
                start_ref[row, spot, :] += nt(every_ref[row * seq + n * tile : row * seq + (n + 1) * tile, :], turned)

    @pl.when(step == last)
    def _():
        wide = lambda x: jnp.concatenate([x, jnp.zeros((x.shape[0], c - x.shape[1]), F32)], 1)
        turned = column()

        def finish(e):
            total = None
            for row in range(rows):
                spot = slice(e * held, (e + 1) * held)
                grad = start_ref[row, spot, :] + nt(every_ref[row * seq + e * held : row * seq + (e + 1) * held, :], turned)
                input_ref[row, spot, :] = grad.astype(BF16)
                total = grad if total is None else total + grad
            total = total.astype(BF16)
            for f, (a, b, core) in enumerate(group):
                lanes = slice(f * narrow, (f + 1) * narrow)
                ppart_ref[e, a, b, core, :per, :] = jnp.concatenate(
                    [total[n * per : (n + 1) * per, lanes] for n in range(folds)], 1
                )
                table = total_ref[e * few : (e + 1) * few, lanes]
                spot = (e * len(group) + f) * single
                line = bsum_ref[:, spot : spot + single]
                filler = jnp.zeros((SMALL - few - 1, c), F32)
                ppart_ref[e, a, b, core, per:, :] = jnp.concatenate([wide(table), wide(line), filler], 0).astype(BF16)
            places.begin(e)
            input_copy(e).start()

        def places_of(block):
            return [e for e in range(dp) if e * held // WIN == block]

        def on(step_of, *chosen):
            for block in chosen:
                for e in places_of(block):
                    step_of(e)

        attend(*downward[: blocks // 2])
        for e in nearest[half:]:
            late.along(e)
        weights_on()
        on(finish, *downward[: blocks // 2])
        attend(*downward[blocks // 2 : -1])
        on(places.across, *downward[: blocks // 2])
        on(finish, *downward[blocks // 2 : -1])
        for e in pieces(last - 2):
            weights.middle(e)
        for e in pieces(last - 3):
            weights.along(e)
        attend(downward[-1])
        sum_tokens()
        on(finish, downward[-1])
        on(places.across, *downward[blocks // 2 : -1])
        send_weights()
        for e in pieces(last - 1):
            weights.middle(e)
        on(places.middle, *downward[: blocks // 2])
        on(places.across, downward[-1])
        for e in pieces(last):
            weights.across(e)
        on(places.middle, *downward[blocks // 2 : -1])
        on(places.along, *downward[: blocks // 2])
        for e in pieces(last - 2) + pieces(last - 1):
            weights.along(e)
        on(places.middle, downward[-1])
        on(places.along, *downward[blocks // 2 : -1])
        for e in pieces(last):
            weights.middle(e)
        late_sum_ref[...] = late.result()
        on(places.along, downward[-1])
        for e in pieces(last):
            weights.along(e)
        place_sum_ref[...] = places.result()
        weight_sum_ref[...] = weights.result()
        late.close()
        weights.close()
        places.close()
        for e in range(dp):
            input_copy(e).wait()


def hand_out(late_in, weight_in, place_in, input_in, *refs):
    count = (len(refs) - 7) // 2
    outs, (late_ref, weight_ref, place_ref, input_ref), stages = refs[: count + 1], refs[count + 1 : count + 5], refs[count + 5 : -2]
    load_sems, store_sems = refs[-2:]
    wq_ref, wk_ref, wv_ref, wo_ref, wi_ref, w2_ref, table_ref, placet_ref, line_ref = stages
    copy = pltpu.make_async_copy
    small = [(late_in, late_ref), (weight_in, weight_ref), (place_in, place_ref)]
    loads = [copy(src, dst, load_sems.at[n]) for n, (src, dst) in enumerate(small)]
    pieces = load_sems.shape[0] - len(small)
    some = input_in.shape[0] // pieces
    spots = [slice(n * some, (n + 1) * some) for n in range(pieces)]
    loads += [copy(input_in.at[x], input_ref.at[x], load_sems.at[3 + n]) for n, x in enumerate(spots)]
    stores = [copy(src, dst, store_sems.at[n]) for n, (src, dst) in enumerate(zip(stages, outs[1:]))]
    stores += [copy(input_ref.at[x], outs[0].at[x], store_sems.at[count + n]) for n, x in enumerate(spots)]
    for load in loads:
        load.start()
    r, c = wq_ref.shape
    few, narrow = table_ref.shape
    held = placet_ref.shape[1]
    folds = c // narrow
    per = held // folds
    for load in loads[:3]:
        load.wait()
    for n, ref in enumerate((wq_ref, wk_ref, wv_ref)):
        ref[...] = weight_ref[n * r : (n + 1) * r, :]
    wide_parts = wi_ref.shape[1] // c
    wo_ref[...] = late_ref[:r, :]
    for n in range(wide_parts):
        wi_ref[:, n * c : (n + 1) * c] = late_ref[(1 + n) * r : (2 + n) * r, :]
    w2_ref[...] = late_ref[(1 + wide_parts) * r :, :]
    place = place_ref[:per, :]
    placet_ref[...] = jnp.concatenate([place[:, n * narrow : (n + 1) * narrow] for n in range(folds)], 0).T
    table_ref[...] = place_ref[per : per + few, :narrow]
    line_ref[...] = place_ref[per + few : per + few + 1, : line_ref.shape[1]]
    for store in stores[:count]:
        store.start()
    for n in range(pieces):
        loads[3 + n].wait()
        stores[count + n].start()
    for store in stores:
        store.wait()


def feed_forward(
    ctx_ref, act_ref, pos_ref, cot_ref, late_ref, vec_ref, bias_ref,
    out_ref, first_ref, grad_ref, part_out, sums_ref, bsum_ref,
    wo_acc, wi_acc, w2_acc, slope_ref, wo_ref, wi_ref, w2_ref, part_ref, sems,
):
    step = pl.program_id(0)
    width = ctx_ref.shape[1]
    dp, side, _, _, _, c = late_ref.shape
    group = members(side)
    r = width // len(group)
    parts = bias_ref.shape[1] // dp // c
    tall = bias_ref.shape[1] // len(group)
    spans = [slice(0, r), slice(r, (1 + parts) * r), slice((1 + parts) * r, (1 + parts) * r + tall)]
    everywhere = (slice(None),) * 4

    def fetch(n):
        at = everywhere + (spans[n],)
        return pltpu.make_async_copy(late_ref.at[at], part_ref.at[at], sems.at[n])

    def deliver(n):
        at = everywhere + (spans[n],)
        return pltpu.make_async_copy(part_ref.at[at], part_out.at[at], sems.at[3 + n])

    hidden = bias_ref.shape[1]
    part = 512

    last = pl.num_programs(0) - 1
    vec = lambda n: vec_ref[n : n + 1, :]
    C = hidden // part
    cols = [slice(n * part, (n + 1) * part) for n in range(C)]

    def unpack(n):
        fetch(n).wait()
        for f, (a, b, core) in enumerate(group):
            block = lambda e, lo, n: part_ref[e, a, b, core, lo : lo + n, :]
            if n == 0:
                wo_ref[f * r : (f + 1) * r, :] = jnp.concatenate([block(e, 0, r) for e in range(dp)], 1)
            elif n == 1:
                wi_ref[f * r : (f + 1) * r, :] = jnp.concatenate(
                    [block(e, (1 + m) * r, r) for e in range(dp) for m in range(parts)], 1
                )
            else:
                w2_ref[f * tall : (f + 1) * tall, :] = jnp.concatenate(
                    [block(e, (1 + parts) * r, tall) for e in range(dp)], 1
                )

    def pack(n):
        for e in range(dp):
            for f, (a, b, core) in enumerate(group):
                rows = slice(f * r, (f + 1) * r)
                if n == 0:
                    part_ref[e, a, b, core, :r, :] = wo_acc[rows, e * c : (e + 1) * c].astype(BF16)
                elif n == 1:
                    for m in range(parts):
                        wide = slice((e * parts + m) * c, (e * parts + m + 1) * c)
                        part_ref[e, a, b, core, (1 + m) * r : (2 + m) * r, :] = wi_acc[rows, wide].astype(BF16)
                else:
                    turned = w2_acc[e * c : (e + 1) * c, f * tall : (f + 1) * tall].astype(BF16)
                    part_ref[e, a, b, core, (1 + parts) * r :, :] = turned.T
        deliver(n).start()

    def body(first, final):
        def add(ref, at, value):
            if first:
                ref[at] = value
            else:
                ref[at] += value

        def add_row(n, value):
            add(sums_ref, (slice(n, n + 1), slice(None)), value)

        if first:
            for n in range(3):
                fetch(n).start()
            sums_ref[0:2, :] = jnp.zeros((2, width), F32)
            unpack(0)
        ctx = ctx_ref[...]
        first_sum = act_ref[...].astype(F32) + pos_ref[...].astype(F32) + (nn(ctx, wo_ref[...]) + vec(2))
        center = first_sum - jnp.mean(first_sum, -1, keepdims=True)
        scale_one = lax.rsqrt(jnp.mean(center * center, -1, keepdims=True) + 1e-05)
        z_one = center * scale_one
        normed = z_one * vec(3) + vec(4)
        normed_low = normed.astype(BF16)
        if first:
            unpack(1)
        branch = None
        acts = []
        pre_next = nn(normed_low, wi_ref[:, cols[0]])
        for n in range(C):
            pre = pre_next + bias_ref[:, cols[n]]
            if n + 1 < C:
                pre_next = nn(normed_low, wi_ref[:, cols[n + 1]])
            if n >= 1:
                if first and n == 1:
                    unpack(2)
                term = nn(acts[n - 1], w2_ref[cols[n - 1], :])
                branch = term if branch is None else branch + term
            square = pre * pre
            t = jnp.tanh(pre * (0.7978845608028654 + (0.7978845608028654 * 0.044715) * square))
            half = 0.5 + 0.5 * t
            acts.append((pre * half).astype(BF16))
            slope_ref[:, cols[n]] = half + (0.5 * pre) * (1.0 - t * t) * (
                0.7978845608028654 + (3.0 * 0.7978845608028654 * 0.044715) * square
            )
        branch = branch + nn(acts[C - 1], w2_ref[cols[C - 1], :])
        second_sum = normed + (branch + vec(5))
        center = second_sum - jnp.mean(second_sum, -1, keepdims=True)
        scale_two = lax.rsqrt(jnp.mean(center * center, -1, keepdims=True) + 1e-05)
        z_two = center * scale_two
        out_ref[...] = (z_two * vec(6) + vec(7)).astype(BF16)
        cot = cot_ref[...].astype(F32)
        add_row(6, column_sum(cot * z_two))
        add_row(7, column_sum(cot))
        e = cot * vec(6)
        second_grad = scale_two * (
            e - jnp.mean(e, -1, keepdims=True) - z_two * jnp.mean(e * z_two, -1, keepdims=True)
        )
        branch_grad = second_grad.astype(BF16)
        add_row(5, column_sum(branch_grad))
        branch_t = branch_grad.T
        normed_t = normed_low.T
        normed_grad = second_grad
        grad_next = nt(branch_grad, w2_ref[cols[0], :])
        lows = []
        everything = slice(None)

        def inner(n):
            add(wi_acc, (everything, cols[n]), nn(normed_t, lows[n]))

        def outer(n):
            add(w2_acc, (everything, cols[n]), nn(branch_t, acts[n]))

        for n in range(C):
            pre_grad = grad_next * slope_ref[:, cols[n]]
            if n + 1 < C:
                grad_next = nt(branch_grad, w2_ref[cols[n + 1], :])
            if n < LATER:
                outer(n)
            if n >= 1:
                inner(n - 1)
                normed_grad = normed_grad + nt(lows[n - 1], wi_ref[:, cols[n - 1]])
            lows.append(pre_grad.astype(BF16))
            add(bsum_ref, (everything, cols[n]), column_sum(lows[n]))
        normed_grad = normed_grad + nt(lows[C - 1], wi_ref[:, cols[C - 1]])
        inner(C - 1)
        add_row(3, column_sum(normed_grad * z_one))
        add_row(4, column_sum(normed_grad))
        e = normed_grad * vec(3)
        level = jnp.mean(e, -1, keepdims=True)
        slant = jnp.mean(e * z_one, -1, keepdims=True)
        for n in range(LATER, C):
            outer(n)
        if final:
            pack(1)
            pack(2)
        first_grad = scale_one * (e - level - z_one * slant)
        first_ref[...] = first_grad
        attn_grad = first_grad.astype(BF16)
        add_row(2, column_sum(attn_grad))
        add(wo_acc, (everything, everything), nn(ctx.T, attn_grad))
        grad_ref[...] = nt(attn_grad, wo_ref[...]).astype(BF16)
        if final:
            pack(0)
            for n in range(3):
                deliver(n).wait()

    @pl.when(step == 0)
    def _():
        for n in range(3):
            fetch(n).start()
        for ref in (wo_acc, wi_acc, w2_acc, sums_ref, bsum_ref):
            ref[...] = jnp.zeros_like(ref)
        for n in range(3):
            unpack(n)

    body(False, False)

    @pl.when(step == last)
    def _():
        for n in (1, 2, 0):
            pack(n)
        for n in range(3):
            deliver(n).wait()


def whole(shape):
    return pl.BlockSpec(shape, lambda *_: (0,) * len(shape))


def once(shape):
    return pl.BlockSpec(shape, lambda *_: (0,) * len(shape), pipeline_mode=pl.Buffered(1))


def run_forward(lengths, act, wq, wk, wv, wo, wi, w2, table, place, line):
    rows, seq, width = act.shape
    dp, side = lax.axis_size("dp"), side_of(lax.axis_size("fsdp"))
    r, c = wq.shape
    hidden = wi.shape[1] * dp
    first_rows = 3 * r + place.shape[0] * place.shape[1] // c + SMALL
    late_rows = r + r * wi.shape[1] // c + w2.shape[0]
    row3 = lambda shape: pl.BlockSpec((1,) + shape, lambda i: (i,) + (0,) * len(shape))
    seqs = row3((seq, width))
    st, tt = jax.ShapeDtypeStruct((rows, seq, width), BF16), jax.ShapeDtypeStruct((rows, width, seq), BF16)
    small = [x.shape for x in (wq, wk, wv, wo, wi, w2, table, place, line)]
    anywhere = pl.BlockSpec(memory_space=pl.ANY)
    return pl.pallas_call(
        forward_attention,
        grid=(rows,),
        in_specs=[pl.BlockSpec(memory_space=pltpu.SMEM), anywhere] + [whole(x) for x in small],
        out_specs=[anywhere] * 6 + [seqs, row3((H // 2, 2, seq)), anywhere, anywhere,
                                    whole((table.shape[0] * dp, width)), whole((1, hidden)), anywhere],
        scratch_shapes=[
            pltpu.VMEM(act.shape, BF16),
            pltpu.SemaphoreType.DMA((rows,)),
            pltpu.VMEM((1, seq, width), BF16),
            pltpu.VMEM((1, width, seq), BF16),
            pltpu.VMEM((1, seq, width), BF16),
            pltpu.VMEM((1, width, seq), BF16),
            pltpu.VMEM((1, seq, width), BF16),
            pltpu.VMEM((1, width, seq), BF16),
            pltpu.VMEM((width, 3 * width), BF16),
            pltpu.VMEM((seq, width), BF16),
            pltpu.SemaphoreType.DMA((8,)),
            pltpu.VMEM((width, seq), BF16),
            pltpu.VMEM((2, width, WIN), BF16),
            pltpu.VMEM((dp, side, side, 2, first_rows, c), BF16),
            pltpu.VMEM((late_rows, c), BF16),
            pltpu.SemaphoreType.DMA,
        ]
        + Gather.semaphores(dp, side) * 2,
        out_shape=[
            st, tt, st, tt, st, tt, st, jax.ShapeDtypeStruct((rows, H // 2, 2, seq), F32),
            jax.ShapeDtypeStruct((width, 3 * width), BF16),
            jax.ShapeDtypeStruct((seq, width), BF16),
            jax.ShapeDtypeStruct((table.shape[0] * dp, width), F32),
            jax.ShapeDtypeStruct((1, hidden), F32),
            jax.ShapeDtypeStruct((dp, side, side, 2, late_rows, c), BF16),
        ],
        compiler_params=pltpu.CompilerParams(
            vmem_limit_bytes=VMEM_LIMIT, collective_id=0, has_side_effects=True
        ),
        name="forward_attention",
    )(lengths, act, wq, wk, wv, wo, wi, w2, table, place, line)


def run_backward(lengths, q, qt, k, kt, v, lse, grad, first, lowt, weight, late, sums, bsum):
    rows, seq, width = grad.shape
    dp, side = late.shape[:2]
    late_rows, c = late.shape[4:]
    r = width // (2 * side * side)
    weight_rows = 3 * r
    place_rows = (seq // dp) * r // c + SMALL
    lanes = pl.BlockSpec((rows, seq, PAIR), lambda j: (0, 0, j))
    turned = pl.BlockSpec((rows, PAIR, seq), lambda j: (0, j, 0))
    anywhere = pl.BlockSpec(memory_space=pl.ANY)
    totals = [(n, c) for n in (late_rows, weight_rows, place_rows)]
    return pl.pallas_call(
        backward_attention,
        grid=(H // 2,),
        in_specs=[pl.BlockSpec(memory_space=pltpu.SMEM), lanes, turned, lanes, turned, lanes,
                  pl.BlockSpec((rows, 1, 2, seq), lambda j: (0, j, 0, 0)), lanes, anywhere, anywhere, anywhere,
                  anywhere, once(sums.shape), once(bsum.shape)],
        out_specs=[anywhere] + [whole(x) for x in totals],
        scratch_shapes=[
            pltpu.VMEM(weight.shape, BF16),
            pltpu.VMEM(grad.shape, BF16),
            pltpu.SemaphoreType.DMA((rows + 1,)),
            pltpu.SemaphoreType.DMA((dp,)),
            pltpu.VMEM((width, rows * seq), BF16),
            pltpu.VMEM((rows, PAIR, seq), BF16),
            pltpu.VMEM((rows, PAIR, seq), BF16),
            pltpu.VMEM((rows, seq, PAIR), F32),
            pltpu.VMEM((rows, seq, PAIR), F32),
            pltpu.VMEM((rows * seq, 3 * PAIR), BF16),
            pltpu.VMEM((rows, seq, width), F32),
            pltpu.VMEM(sums.shape, F32),
            pltpu.VMEM((dp, side, side, 2, weight_rows, c), BF16),
            pltpu.VMEM((dp, side, side, 2, place_rows, c), BF16),
            pltpu.VMEM((dp, side, side, late_rows, c), BF16),
            pltpu.SemaphoreType.DMA,
            pltpu.SemaphoreType.DMA,
        ]
        + Reduce.scratch(dp, side, late_rows, c)
        + Reduce.scratch(dp, side, weight_rows, c)
        + Reduce.scratch(dp, side, place_rows, c),
        out_shape=[jax.ShapeDtypeStruct(grad.shape, BF16)] + [jax.ShapeDtypeStruct(x, F32) for x in totals],
        compiler_params=pltpu.CompilerParams(
            vmem_limit_bytes=VMEM_LIMIT, collective_id=1, has_side_effects=True
        ),
        name="backward_attention",
    )(lengths, q, qt, k, kt, v, lse, grad, first, lowt, weight, late, sums, bsum)


def run_hand_out(late, weight, place, grad, shapes):
    anywhere = pl.BlockSpec(memory_space=pl.ANY)
    tokens = grad.reshape(-1, grad.shape[-1])
    dma = pltpu.SemaphoreType.DMA
    pieces = 4
    return pl.pallas_call(
        hand_out,
        in_specs=[anywhere] * 4,
        out_specs=[anywhere] * (1 + len(shapes)),
        out_shape=[jax.ShapeDtypeStruct(tokens.shape, BF16)] + [jax.ShapeDtypeStruct(x, F32) for x in shapes],
        scratch_shapes=[pltpu.VMEM(x.shape, x.dtype) for x in (late, weight, place, tokens)]
        + [pltpu.VMEM(x, F32) for x in shapes]
        + [dma((3 + pieces,)), dma((len(shapes) + pieces,))],
        name="hand_out",
    )(late, weight, place, tokens)


def run_feed_forward(ctx, act, pos, cot, late, vec, bias, tile=512):
    tokens, width = ctx.shape
    seq = pos.shape[0]
    hidden = bias.shape[1]
    per_row = seq // tile
    tok = pl.BlockSpec((tile, width), lambda t: (t, 0))
    return pl.pallas_call(
        feed_forward,
        grid=(tokens // tile,),
        in_specs=[tok, tok, pl.BlockSpec((tile, width), lambda t: (t % per_row, 0)), tok,
                  pl.BlockSpec(memory_space=pl.ANY), whole(vec.shape), whole(bias.shape)],
        out_specs=[tok, tok, tok, pl.BlockSpec(memory_space=pl.ANY), whole((8, width)),
                   whole((1, hidden))],
        scratch_shapes=[
            pltpu.VMEM((width, width), F32),
            pltpu.VMEM((width, hidden), F32),
            pltpu.VMEM((width, hidden), F32),
            pltpu.VMEM((tile, hidden), F32),
            pltpu.VMEM((width, width), BF16),
            pltpu.VMEM((width, hidden), BF16),
            pltpu.VMEM((hidden, width), BF16),
            pltpu.VMEM(late.shape, BF16),
            pltpu.SemaphoreType.DMA((6,)),
        ],
        out_shape=[
            jax.ShapeDtypeStruct((tokens, width), BF16),
            jax.ShapeDtypeStruct((tokens, width), F32),
            jax.ShapeDtypeStruct((tokens, width), BF16),
            jax.ShapeDtypeStruct(late.shape, BF16),
            jax.ShapeDtypeStruct((8, width), F32),
            jax.ShapeDtypeStruct((1, hidden), F32),
        ],
        compiler_params=pltpu.CompilerParams(vmem_limit_bytes=VMEM_LIMIT),
        name="feed_forward",
    )(ctx, act, pos, cot, late, vec, bias)


def shards(
    activations, window_lengths, query_weight, key_weight, value_weight, output_weight, inner_weight, outer_weight,
    vectors, positions, inner_bias, output_cotangent,
):
    rows, seq, width = activations.shape
    q, qt, k, kt, v, lowt, ctx, lse, weight, pos, vec, bias, late = run_forward(
        window_lengths, activations, query_weight, key_weight, value_weight, output_weight, inner_weight, outer_weight,
        vectors, positions.T, inner_bias.reshape(1, -1),
    )
    flat = lambda x: x.reshape(rows * seq, width)
    deep = lambda x: x.reshape(rows, seq, width)
    out, first, grad, part, sums, bsum = run_feed_forward(
        flat(ctx), flat(activations), pos, flat(output_cotangent), late, vec, bias
    )
    input_grad, *sums = run_backward(
        window_lengths, q, qt, k, kt, v, lse, deep(grad), deep(first), lowt, weight, part, sums, bsum
    )
    shapes = [x.shape for x in (query_weight, key_weight, value_weight, output_weight, inner_weight, outer_weight,
                                vectors, positions.T)] + [(1, inner_bias.shape[0])]
    owned = run_hand_out(*sums, input_grad, shapes)
    return (deep(out), owned[0].reshape(input_grad.shape)) + tuple(owned[1:8]) + (owned[8].T, owned[9].reshape(-1))


def solution(mesh):
    tokens = P(("dp", "fsdp"), None, None)
    matrix = P("fsdp", "dp")
    table = P("dp", "fsdp")
    line = P(("dp", "fsdp"))
    return jax.shard_map(
        shards,
        mesh=mesh,
        in_specs=(tokens, P(("dp", "fsdp"), None)) + (matrix,) * 6 + (table, table, line, tokens),
        out_specs=(tokens, tokens) + (matrix,) * 6 + (table, table, line),
        check_vma=False,
    )
```

```python
import functools

import jax
import jax.numpy as jnp
from jax import lax
from jax.experimental import pallas as pl
from jax.experimental.pallas import tpu as pltpu
from jax.sharding import PartitionSpec as P

H = 8
HD = 64
WIN = 256
PAIR = 2 * HD
VMEM_LIMIT = 62 * 1024 * 1024
F32 = jnp.float32
BF16 = jnp.bfloat16
MESH = pl.DeviceIdType.MESH
SMALL = 16
LATER = 2


def nn(left, right):
    return lax.dot_general(left, right, (((1,), (0,)), ((), ())), preferred_element_type=F32)


def nt(left, right):
    return lax.dot_general(left, right, (((1,), (1,)), ((), ())), preferred_element_type=F32)


def tn(left, right):
    return lax.dot_general(left, right, (((0,), (0,)), ((), ())), preferred_element_type=F32)


def column_sum(value):
    return jnp.sum(value.astype(F32), 0, keepdims=True)


def head_rows(pair, which):
    zeros = jnp.zeros((HD, pair.shape[1]), pair.dtype)
    if which == 0:
        return jnp.concatenate([pair[:HD], zeros], 0)
    return jnp.concatenate([zeros, pair[HD:]], 0)


def head_lanes(pair, which):
    lane = lax.broadcasted_iota(jnp.int32, pair.shape, 1)
    keep = (lane < HD) if which == 0 else (lane >= HD)
    return jnp.where(keep, pair, jnp.zeros_like(pair))


def causal(scores):
    key = lax.broadcasted_iota(jnp.int32, scores.shape, 0)
    query = lax.broadcasted_iota(jnp.int32, scores.shape, 1)
    return jnp.where(key <= query, scores, -1e30)


def block_of(block):
    return slice(block * WIN, (block + 1) * WIN)


def spots_of(block):
    return [block_of(n) for n in (block, block - 1) if n >= 0]


def pair_of(head):
    return slice(head // 2 * PAIR, (head // 2 + 1) * PAIR)


def staggered(tasks, stages):
    held = {}
    for step in range(len(tasks) + len(stages) - 1):
        for n, stage in enumerate(stages):
            task = step - n
            if 0 <= task < len(tasks):
                args = (held.pop(task),) if n else ()
                held[task] = stage(*tasks[task], *args)


class Place:
    def __init__(self):
        fsdp = lax.axis_index("fsdp")
        self.d, self.dp = lax.axis_index("dp"), lax.axis_size("dp")
        self.side = side_of(lax.axis_size("fsdp"))
        self.chip, self.core = fsdp // 2, lax.rem(fsdp, 2)
        y, x = self.chip // self.side, lax.rem(self.chip, self.side)
        self.a = y + self.core * (x - y)
        self.b = x + self.core * (y - x)

    def device(self, a, b):
        straight, turned = a * self.side + b, b * self.side + a
        return {"fsdp": (straight + self.core * (turned - straight)) * 2 + self.core}

    def sibling(self):
        return {"fsdp": self.chip * 2 + 1 - self.core}

    def at_a(self, n):
        return lax.rem(self.a + n + self.side, self.side)

    def at_b(self, n):
        return lax.rem(self.b + n + self.side, self.side)

    def at_dp(self, n):
        return lax.rem(self.d + n + self.dp, self.dp)


def side_of(fsdp):
    side = 1
    while side * side * 2 < fsdp:
        side += 1
    assert side * side * 2 == fsdp
    return side


def members(side):
    found = []
    for f in range(2 * side * side):
        y, x = f // 2 // side, f // 2 % side
        found.append((x, y, 1) if f % 2 else (y, x, 0))
    return found


def remote(src, dst, send, recv, device):
    return pltpu.make_async_remote_copy(
        src_ref=src, dst_ref=dst, send_sem=send, recv_sem=recv, device_id=device, device_id_type=MESH
    )


def greet(at):
    barrier = pltpu.get_barrier_semaphore()
    others = [{"dp": at.at_dp(n)} for n in range(1, at.dp)]
    others += [at.device(at.a, at.at_b(n)) for n in range(1, at.side)]
    others += [at.device(at.at_a(n), at.b) for n in range(1, at.side)]
    others.append(at.sibling())
    for other in others:
        pl.semaphore_signal(barrier, inc=1, device_id=other, device_id_type=MESH)
    return len(others)


def meet(count):
    pl.semaphore_wait(pltpu.get_barrier_semaphore(), count)


class Gather:
    COUNT = 8

    def __init__(self, buf, sems, at):
        self.buf, self.at = buf, at
        self.zs, self.zr, self.bs, self.br, self.sa, self.ra, self.cs, self.cr = sems

    @staticmethod
    def semaphores(dp, side):
        dma = pltpu.SemaphoreType.DMA
        shapes = [(dp,), (dp, side), (dp, side, side), (side, side)]
        return [dma(x) for x in shapes for _ in range(2)]

    def along_dp(self, o):
        at = self.at
        block = self.buf.at[at.d, at.a, at.b, at.core]
        return remote(block, block, self.zs.at[o], self.zr.at[o], {"dp": at.at_dp(o)})

    def along_b(self, o, p):
        at = self.at
        block = self.buf.at[at.at_dp(-o), at.a, at.b, at.core]
        return remote(block, block, self.bs.at[o, p], self.br.at[o, p], at.device(at.a, at.at_b(p)))

    def along_a(self, o, p, q):
        at = self.at
        block = self.buf.at[at.at_dp(-o), at.a, at.at_b(-p), at.core]
        return remote(block, block, self.sa.at[o, p, q], self.ra.at[o, p, q], at.device(at.at_a(q), at.b))

    def to_core(self, q, p):
        at = self.at
        block = self.buf.at[:, at.at_a(-q), at.at_b(-p), at.core]
        return remote(block, block, self.cs.at[q, p], self.cr.at[q, p], at.sibling())

    def begin(self):
        for o in range(1, self.at.dp):
            self.along_dp(o).start()

    def pass_on(self, o):
        for p in range(1, self.at.side):
            self.along_b(o, p).start()

    def far(self, o):
        for q in range(1, self.at.side):
            self.along_a(o, 0, q).start()

    def spread(self, o):
        self.along_dp(o).wait_recv()
        self.pass_on(o)

    def relay(self, o):
        for p in range(1, self.at.side):
            self.along_b(o, p).wait_recv()
            for q in range(1, self.at.side):
                self.along_a(o, p, q).start()

    def near(self):
        for p in range(self.at.side):
            self.to_core(0, p).start()

    def share(self):
        for p in range(self.at.side):
            for q in range(1, self.at.side):
                for o in range(self.at.dp):
                    self.along_a(o, p, q).wait_recv()
                self.to_core(q, p).start()

    def arrive(self):
        for q in range(self.at.side):
            for p in range(self.at.side):
                self.to_core(q, p).wait_recv()

    def close(self):
        for o in range(1, self.at.dp):
            self.along_dp(o).wait_send()
        for o in range(self.at.dp):
            for p in range(1, self.at.side):
                self.along_b(o, p).wait_send()
            for p in range(self.at.side):
                for q in range(1, self.at.side):
                    self.along_a(o, p, q).wait_send()
        for q in range(self.at.side):
            for p in range(self.at.side):
                self.to_core(q, p).wait_send()


def add_up(terms):
    if len(terms) == 2:
        return terms[0] + terms[1]
    return sum(x.astype(F32) for x in terms).astype(BF16)


class Reduce:
    COUNT = 13

    def __init__(self, part, scratch, at, own=None):
        self.part, self.at = part, at
        self.own, self.own_sem = own or (None, None)
        (self.pair, self.plane, self.row, self.mine, self.line,
         self.cs, self.cr, self.sa, self.ra, self.bs, self.br, self.zs, self.zr) = scratch

    @staticmethod
    def scratch(dp, side, rows, c):
        dma = pltpu.SemaphoreType.DMA
        return [
            pltpu.VMEM((dp, side, side, rows, c), BF16),
            pltpu.VMEM((side - 1, dp, side, rows, c), BF16),
            pltpu.VMEM((side - 1, dp, rows, c), BF16),
            pltpu.VMEM((dp, rows, c), BF16),
            pltpu.VMEM((dp - 1, rows, c), BF16),
        ] + [dma((dp,))] * 2 + [dma((dp, side))] * 4 + [dma((dp,))] * 2

    def to_core(self, e):
        at = self.at
        return remote(self.part.at[e, :, :, 1 - at.core], self.pair.at[e], self.cs.at[e], self.cr.at[e], at.sibling())

    def along_a(self, e, q):
        at = self.at
        to = at.at_a(q)
        return remote(
            self.pair.at[e, to], self.plane.at[q - 1, e], self.sa.at[e, q], self.ra.at[e, q], at.device(to, at.b)
        )

    def along_b(self, e, p):
        at = self.at
        to = at.at_b(p)
        return remote(
            self.pair.at[e, at.a, to], self.row.at[p - 1, e], self.bs.at[e, p], self.br.at[e, p], at.device(at.a, to)
        )

    def along_dp(self, o):
        at = self.at
        to = at.at_dp(o)
        return remote(self.mine.at[to], self.line.at[o - 1], self.zs.at[o], self.zr.at[o], {"dp": to})

    def own_half(self):
        return pltpu.make_async_copy(self.part.at[:, :, :, self.at.core], self.own, self.own_sem)

    def begin(self, e):
        self.to_core(e).start()

    def across(self, e):
        at = self.at
        self.to_core(e).wait_recv()
        for n in list(range(1, at.side)) + [0]:
            a = at.at_a(n)
            for b in range(at.side):
                own = self.part[e, a, b, at.core] if self.own is None else self.own[e, a, b]
                self.pair[e, a, b] = add_up([own, self.pair[e, a, b]])
            if n:
                self.along_a(e, n).start()

    def middle(self, e):
        at = self.at
        for q in range(1, at.side):
            self.along_a(e, q).wait_recv()
        for n in list(range(1, at.side)) + [0]:
            b = at.at_b(n)
            terms = [self.pair[e, at.a, b]] + [self.plane[q - 1, e, b] for q in range(1, at.side)]
            self.pair[e, at.a, b] = add_up(terms)
            if n:
                self.along_b(e, n).start()

    def along(self, e):
        at = self.at
        for p in range(1, at.side):
            self.along_b(e, p).wait_recv()
        self.mine[e] = add_up([self.pair[e, at.a, at.b]] + [self.row[p - 1, e] for p in range(1, at.side)])

        @pl.when(e != at.d)
        def _():
            self.along_dp(lax.rem(e - at.d + at.dp, at.dp)).start()

    def result(self):
        at = self.at
        for o in range(1, at.dp):
            self.along_dp(o).wait_recv()
        total = self.mine[at.d].astype(F32)
        for o in range(1, at.dp):
            total = total + self.line[o - 1].astype(F32)
        return total

    def close(self):
        at = self.at
        for e in range(at.dp):
            self.to_core(e).wait_send()
            for n in range(1, at.side):
                self.along_a(e, n).wait_send()
                self.along_b(e, n).wait_send()
        for o in range(1, at.dp):
            self.along_dp(o).wait_send()


def apart(lengths_ref, row, block):
    total = jnp.int32(0)
    cut = jnp.bool_(False)
    for n in range(lengths_ref.shape[1]):
        total = total + lengths_ref[row, n]
        cut = cut | (total == block * WIN)
    return jnp.where(cut, jnp.float32(-1e30), jnp.float32(0.0))


def forward_attention(
    lengths_ref, act_in, wq_ref, wk_ref, wv_ref, wo_ref, wi_ref, w2_ref, table_ref, place_ref, line_ref,
    q_out, qt_out, k_out, kt_out, v_out, lowt_out, ctx_ref, lse_ref, weight_out, pos_out, vec_ref, bias_ref, late_ref,
    act_ref, act_sems, q_ref, qt_ref, k_ref, kt_ref, v_ref, lowt_ref, weight_ref, pos_ref, out_sems,
    vt_ref, ctxt_ref, early_ref, own_ref, own_sem, *sems,
):
    row = pl.program_id(0)
    rows = pl.num_programs(0)
    width = act_in.shape[2]
    blocks = act_in.shape[1] // WIN
    at = Place()
    dp = at.dp
    here = (at.d, at.a, at.b, at.core)
    r, c = wq_ref.shape
    narrow, held = place_ref.shape
    folds = c // narrow
    per = held // folds
    early = Gather(early_ref, sems[: Gather.COUNT], at)
    late = Gather(late_ref, sems[Gather.COUNT :], at)

    def own_copy():
        return pltpu.make_async_copy(own_ref, late_ref.at[here], own_sem)

    def act_copy(of_row):
        return pltpu.make_async_copy(act_in.at[of_row], act_ref.at[of_row], act_sems.at[of_row])

    def row_copies(of_row):
        pairs = ((q_ref, q_out), (qt_ref, qt_out), (k_ref, k_out), (kt_ref, kt_out), (v_ref, v_out),
                 (lowt_ref, lowt_out))
        return [
            pltpu.make_async_copy(src.at[0], dst.at[of_row], out_sems.at[n]) for n, (src, dst) in enumerate(pairs)
        ]

    def table_copies():
        pairs = ((weight_ref, weight_out), (pos_ref, pos_out))
        return [pltpu.make_async_copy(src, dst, out_sems.at[6 + n]) for n, (src, dst) in enumerate(pairs)]

    @pl.when(row == 0)
    def _():
        count = greet(at)
        for n in range(act_in.shape[0]):
            act_copy(n).start()
        for n, ref in enumerate((wq_ref, wk_ref, wv_ref)):
            early_ref[here + (slice(n * r, (n + 1) * r),)] = ref[...]
        place = place_ref[...].T
        early_ref[here + (slice(3 * r, 3 * r + per),)] = jnp.concatenate(
            [place[n * per : (n + 1) * per] for n in range(folds)], 1
        )
        wide = lambda x: jnp.concatenate([x, jnp.zeros((x.shape[0], c - x.shape[1]), F32)], 1)
        table = wide(table_ref[...].astype(F32))
        line = wide(line_ref[...].astype(F32))
        few = table.shape[0]
        small = jnp.concatenate([table, line, jnp.zeros((SMALL - few - 1, c), F32)], 0)
        early_ref[here + (slice(3 * r + per, None),)] = small.astype(BF16)
        own_ref[:r, :] = wo_ref[...]
        wide_parts = wi_ref.shape[1] // c
        for n in range(wide_parts):
            own_ref[(1 + n) * r : (2 + n) * r, :] = wi_ref[:, n * c : (n + 1) * c]
        own_ref[(1 + wide_parts) * r :, :] = w2_ref[...]
        own_copy().start()
        meet(count)
        early.begin()
        early.pass_on(0)
        early.far(0)
        early.relay(0)
        for o in range(1, dp):
            early.spread(o)
        own_copy().wait()
        late.begin()
        for o in range(1, dp):
            early.relay(o)
            early.far(o)
        early.near()
        late.pass_on(0)
        late.far(0)
        early.share()
        late.relay(0)
        late.spread(1)
        late.far(1)
        early.arrive()
        group = members(at.side)
        for f, (a, b, core) in enumerate(group):
            for n in range(3):
                weight_ref[f * r : (f + 1) * r, n * width : (n + 1) * width] = jnp.concatenate(
                    [early_ref[e, a, b, core, n * r : (n + 1) * r, :] for e in range(dp)], 1
                )
        tables = []
        lines = []
        for e in range(dp):
            for n in range(folds):
                spot = slice(e * held + n * per, e * held + (n + 1) * per)
                pos_ref[spot, :] = jnp.concatenate(
                    [
                        early_ref[e, a, b, core, 3 * r : 3 * r + per, :][:, n * narrow : (n + 1) * narrow]
                        for a, b, core in group
                    ],
                    1,
                )
            smalls = [early_ref[e, a, b, core, 3 * r + per :, :].astype(F32) for a, b, core in group]
            tables.append(jnp.concatenate([x[:few, :narrow] for x in smalls], 1))
            lines.extend(x[few : few + 1, : line_ref.shape[1]] for x in smalls)
        vec_ref[...] = jnp.concatenate(tables, 0)
        bias_ref[...] = jnp.concatenate(lines, 1)
        for copy in table_copies():
            copy.start()

    @pl.when(row > 0)
    def _():
        for copy in row_copies(row - 1):
            copy.wait()

    act_copy(row).wait()

    def project(step, carry):
        spot = pl.ds(pl.multiple_of(step * WIN, WIN), WIN)
        low = (act_ref[row, spot, :].astype(F32) + pos_ref[spot, :].astype(F32)).astype(BF16)
        lowt_ref[0, :, spot] = low.T
        every = nn(low, weight_ref[...])
        q = (every[:, :width] + vec_ref[0:1, :]).astype(BF16)
        q = (q.astype(F32) * 0.125).astype(BF16)
        k = every[:, width : 2 * width].astype(BF16)
        v = (every[:, 2 * width :] + vec_ref[1:2, :]).astype(BF16)
        q_ref[0, spot, :] = q
        k_ref[0, spot, :] = k
        v_ref[0, spot, :] = v
        qt_ref[0, :, spot] = q.T
        kt_ref[0, :, spot] = k.T
        vt_ref[:, spot] = v.T
        return carry

    lax.fori_loop(0, blocks, project, 0)
    for copy in row_copies(row):
        copy.start()

    @pl.when(row == 0)
    def _():
        for o in range(2, dp // 2 + 1):
            late.spread(o)
            late.far(o)
        late.relay(1)

    def score(block, head):
        q_head = head_rows(qt_ref[0, pair_of(head), block_of(block)], head % 2)
        return [nn(k_ref[0, spot, pair_of(head)], q_head) for spot in spots_of(block)]

    def soften(block, head, scores):
        scores[0] = causal(scores[0])
        peaks = [jnp.max(x, 0, keepdims=True) for x in scores]
        peak = peaks[0]
        if block:
            peak = jnp.maximum(peak, peaks[1] + apart(lengths_ref, row, block))
        expo = [jnp.exp(scores[0] - peak)]
        if block:
            expo.append(jnp.exp(scores[1] - (peak - apart(lengths_ref, row, block))))
        total = sum(jnp.sum(x, 0, keepdims=True) for x in expo)
        lse_ref[0, head // 2, head % 2 : head % 2 + 1, block_of(block)] = peak + jnp.log(total)
        return [x.astype(BF16) for x in expo], total

    def combine(block, head, soft):
        expo, total = soft
        half = slice(head * HD, (head + 1) * HD)
        out = sum(nn(vt_ref[half, spot], x) for spot, x in zip(spots_of(block), expo))
        ctxt_ref[block % 2, half, :] = (out * (1.0 / total)).astype(BF16)
        if head == H - 1:
            ctx_ref[0, block_of(block), :] = ctxt_ref[block % 2].T

    stages = (score, soften, combine)
    tasks = [(block, head) for block in range(blocks) for head in range(H)]
    quarter = len(tasks) // 4
    staggered(tasks[:quarter], stages)

    @pl.when(row == 0)
    def _():
        for o in range(dp // 2 + 1, dp):
            late.spread(o)
            late.far(o)

    staggered(tasks[quarter : 2 * quarter], stages)

    @pl.when(row == 0)
    def _():
        for o in range(2, dp - 1):
            late.relay(o)

    @pl.when(row == rows - 1)
    def _():
        late.share()

    staggered(tasks[2 * quarter :], stages)

    @pl.when(row == 0)
    def _():
        late.relay(dp - 1)
        late.near()

    @pl.when(row == rows - 1)
    def _():
        late.arrive()
        early.close()
        late.close()
        for copy in row_copies(row) + table_copies():
            copy.wait()


def backward_attention(
    lengths_ref, q_ref, qt_ref, k_ref, kt_ref, v_ref, lse_ref, grad_ref, first_ref, lowt_in, weight_in,
    late_ref, sums_ref, bsum_ref,
    input_out, late_sum_ref, weight_sum_ref, place_sum_ref,
    weight_ref, input_ref, load_sems, input_sems, lowt_ref, gradt_ref, dqt_ref, dk_ref, dv_ref, every_ref, start_ref, total_ref, wpart_ref, ppart_ref, own_ref,
    own_sem, first_sem, *scratch,
):
    step = pl.program_id(0)
    last = H // 2 - 1
    rows, width, seq = lowt_in.shape
    blocks = seq // WIN
    at = Place()
    dp = at.dp
    group = members(at.side)
    r = width // len(group)
    c = width // dp
    narrow = r
    held = seq // dp
    folds = c // narrow
    per = held // folds
    few = sums_ref.shape[0] // dp
    single = bsum_ref.shape[1] // (dp * len(group))
    shared = dp // (H // 2)
    count = Reduce.COUNT
    late = Reduce(late_ref, scratch[:count], at, (own_ref, own_sem))
    weights = Reduce(wpart_ref, scratch[count : 2 * count], at)
    places = Reduce(ppart_ref, scratch[2 * count :], at)
    first_copy = pltpu.make_async_copy(first_ref, start_ref, first_sem)
    loads = [
        pltpu.make_async_copy(lowt_in.at[row], lowt_ref.at[:, row * seq : (row + 1) * seq], load_sems.at[row])
        for row in range(rows)
    ]
    loads.append(pltpu.make_async_copy(weight_in, weight_ref, load_sems.at[rows]))
    arriving = loads + [first_copy]

    def input_copy(e):
        spot = (slice(None), slice(e * held, (e + 1) * held))
        return pltpu.make_async_copy(input_ref.at[spot], input_out.at[spot], input_sems.at[e])

    pieces = lambda j: [j * shared + n for n in range(shared)]
    nearest = [at.at_dp(n + 1) for n in range(dp)]

    @pl.when(step == 0)
    def _():
        greet(at)
        for load in arriving:
            load.start()
        late.own_half().start()
        total_ref[...] = sums_ref[...]

    for row in range(rows):
        for block in range(blocks):
            gradt_ref[row, :, block_of(block)] = grad_ref[row, block_of(block), :].T

    def score(row, block, head):
        q_head = head_rows(qt_ref[row, :, block_of(block)], head)
        g_head = head_rows(gradt_ref[row, :, block_of(block)], head)
        scores = [nn(k_ref[row, spot, :], q_head) for spot in spots_of(block)]
        return scores, [nn(v_ref[row, spot, :], g_head) for spot in spots_of(block)]

    def soften(row, block, head, products):
        scores, prob_grads = products
        lse = lse_ref[row, 0, head : head + 1, block_of(block)]
        probs = [jnp.exp(causal(scores[0]) - lse)]
        if block:
            probs.append(jnp.exp(scores[1] - (lse - apart(lengths_ref, row, block))))
        inner = sum(jnp.sum(p * g, 0, keepdims=True) for p, g in zip(probs, prob_grads))
        score_grads = [(p * (g - inner)).astype(BF16) for p, g in zip(probs, prob_grads)]
        return [p.astype(BF16) for p in probs], score_grads

    waiting = {}

    def combine(row, block, head, soft):
        half = slice(head * HD, (head + 1) * HD)
        dq = sum(nn(kt_ref[row, half, spot], x) for spot, x in zip(spots_of(block), soft[1]))
        dqt_ref[row, half, block_of(block)] = (dq * 0.125).astype(BF16)
        if head == 0:
            waiting[row, block] = soft
            return
        even = waiting.pop((row, block))
        g = grad_ref[row, block_of(block), :]
        q = q_ref[row, block_of(block), :]
        g_both = jnp.concatenate([head_lanes(g, 0), head_lanes(g, 1)], 0)
        q_both = jnp.concatenate([head_lanes(q, 0), head_lanes(q, 1)], 0)
        for n, spot in enumerate(spots_of(block)):
            dv = nn(jnp.concatenate([even[0][n], soft[0][n]], 1), g_both)
            dk = nn(jnp.concatenate([even[1][n], soft[1][n]], 1), q_both)
            if n or block == blocks - 1:
                dv_ref[row, spot, :] = dv
                dk_ref[row, spot, :] = dk
            else:
                dv_ref[row, spot, :] += dv
                dk_ref[row, spot, :] += dk

    def attend(*chosen):
        tasks = [(row, block, head) for block in chosen for row in range(rows) for head in range(2)]
        staggered(tasks, (score, soften, combine))
        for row in range(rows):
            for block in chosen:
                spot = block_of(block)
                every = [dqt_ref[row, :, spot].T, dk_ref[row, spot, :].astype(BF16), dv_ref[row, spot, :].astype(BF16)]
                every_ref[row * seq + block * WIN : row * seq + (block + 1) * WIN, :] = jnp.concatenate(every, 1)

    half = dp // 2
    downward = list(range(blocks))[::-1]
    feats = pl.ds(pl.multiple_of(step * PAIR, PAIR), PAIR)

    def sum_tokens():
        total_ref[0:1, feats] = column_sum(every_ref[:, :PAIR])
        total_ref[1:2, feats] = column_sum(every_ref[:, 2 * PAIR :])

    def send_weights():
        owned = nn(lowt_ref[...], every_ref[...])
        for i, e in enumerate(pieces(step)):
            for f, (a, b, core) in enumerate(group):
                for n in range(3):
                    lanes = slice(n * PAIR + i * c, n * PAIR + (i + 1) * c)
                    wpart_ref[e, a, b, core, n * r : (n + 1) * r, :] = owned[f * r : (f + 1) * r, lanes].astype(BF16)
            weights.begin(e)

    def column():
        return jnp.concatenate(
            [weight_ref[:, pl.ds(pl.multiple_of(n * width + step * PAIR, PAIR), PAIR)] for n in range(3)], 1
        )

    def weights_on():
        @pl.when(step > 0)
        def _():
            for e in pieces(step - 1):
                weights.across(e)

    @pl.when(step < last)
    def _():
        attend(*downward[: blocks // 2])

        @pl.when(step == 0)
        def _():
            meet(dp + 2 * at.side - 2)
            for e in nearest:
                late.begin(e)

        @pl.when(step == 1)
        def _():
            for e in nearest[: half // 2]:
                late.middle(e)

        @pl.when(step == 2)
        def _():
            for e in nearest[half : half + half // 2]:
                late.middle(e)
            for e in nearest[: half // 2]:
                late.along(e)

        weights_on()
        attend(*downward[blocks // 2 :])

        @pl.when(step == 0)
        def _():
            late.own_half().wait()
            for e in nearest:
                late.across(e)
            for load in arriving:
                load.wait()

        sum_tokens()
        send_weights()

        @pl.when(step == 1)
        def _():
            for e in nearest[half // 2 : half]:
                late.middle(e)

        @pl.when(step == 2)
        def _():
            for e in nearest[half + half // 2 :]:
                late.middle(e)
            for e in nearest[half // 2 : half]:
                late.along(e)
            for e in pieces(0):
                weights.middle(e)

        tile = 2 * WIN
        turned = column()
        for row in range(rows):
            for n in range(seq // tile):
                spot = slice(n * tile, (n + 1) * tile)
                start_ref[row, spot, :] += nt(every_ref[row * seq + n * tile : row * seq + (n + 1) * tile, :], turned)

    @pl.when(step == last)
    def _():
        wide = lambda x: jnp.concatenate([x, jnp.zeros((x.shape[0], c - x.shape[1]), F32)], 1)
        turned = column()

        def finish(e):
            total = None
            for row in range(rows):
                spot = slice(e * held, (e + 1) * held)
                grad = start_ref[row, spot, :] + nt(every_ref[row * seq + e * held : row * seq + (e + 1) * held, :], turned)
                input_ref[row, spot, :] = grad.astype(BF16)
                total = grad if total is None else total + grad
            total = total.astype(BF16)
            for f, (a, b, core) in enumerate(group):
                lanes = slice(f * narrow, (f + 1) * narrow)
                ppart_ref[e, a, b, core, :per, :] = jnp.concatenate(
                    [total[n * per : (n + 1) * per, lanes] for n in range(folds)], 1
                )
                table = total_ref[e * few : (e + 1) * few, lanes]
                spot = (e * len(group) + f) * single
                line = bsum_ref[:, spot : spot + single]
                filler = jnp.zeros((SMALL - few - 1, c), F32)
                ppart_ref[e, a, b, core, per:, :] = jnp.concatenate([wide(table), wide(line), filler], 0).astype(BF16)
            places.begin(e)
            input_copy(e).start()

        def places_of(block):
            return [e for e in range(dp) if e * held // WIN == block]

        def on(step_of, *chosen):
            for block in chosen:
                for e in places_of(block):
                    step_of(e)

        attend(*downward[: blocks // 2])
        for e in nearest[half:]:
            late.along(e)
        weights_on()
        on(finish, *downward[: blocks // 2])
        attend(*downward[blocks // 2 : -1])
        on(places.across, *downward[: blocks // 2])
        on(finish, *downward[blocks // 2 : -1])
        for e in pieces(last - 2):
            weights.middle(e)
        for e in pieces(last - 3):
            weights.along(e)
        attend(downward[-1])
        sum_tokens()
        on(finish, downward[-1])
        on(places.across, *downward[blocks // 2 : -1])
        on(places.across, downward[-1])
        send_weights()
        for e in pieces(last - 1):
            weights.middle(e)
        on(places.middle, *downward[: blocks // 2])
        on(places.middle, *downward[blocks // 2 : -1])
        on(places.middle, downward[-1])
        for e in pieces(last):
            weights.across(e)
        on(places.along, *downward[: blocks // 2])
        on(places.along, *downward[blocks // 2 : -1])
        on(places.along, downward[-1])
        for e in pieces(last - 2):
            weights.along(e)
        for e in pieces(last - 1):
            weights.along(e)
        for e in pieces(last):
            weights.middle(e)
        late_sum_ref[...] = late.result()
        for e in pieces(last):
            weights.along(e)
        place_sum_ref[...] = places.result()
        weight_sum_ref[...] = weights.result()
        late.close()
        weights.close()
        places.close()
        for e in range(dp):
            input_copy(e).wait()


def hand_out(late_in, weight_in, place_in, input_in, *refs):
    count = (len(refs) - 7) // 2
    outs, (late_ref, weight_ref, place_ref, input_ref), stages = refs[: count + 1], refs[count + 1 : count + 5], refs[count + 5 : -2]
    load_sems, store_sems = refs[-2:]
    wq_ref, wk_ref, wv_ref, wo_ref, wi_ref, w2_ref, table_ref, placet_ref, line_ref = stages
    copy = pltpu.make_async_copy
    small = [(late_in, late_ref), (weight_in, weight_ref), (place_in, place_ref)]
    loads = [copy(src, dst, load_sems.at[n]) for n, (src, dst) in enumerate(small)]
    pieces = load_sems.shape[0] - len(small)
    some = input_in.shape[0] // pieces
    spots = [slice(n * some, (n + 1) * some) for n in range(pieces)]
    loads += [copy(input_in.at[x], input_ref.at[x], load_sems.at[3 + n]) for n, x in enumerate(spots)]
    stores = [copy(src, dst, store_sems.at[n]) for n, (src, dst) in enumerate(zip(stages, outs[1:]))]
    stores += [copy(input_ref.at[x], outs[0].at[x], store_sems.at[count + n]) for n, x in enumerate(spots)]
    for load in loads:
        load.start()
    r, c = wq_ref.shape
    few, narrow = table_ref.shape
    held = placet_ref.shape[1]
    folds = c // narrow
    per = held // folds
    for load in loads[:3]:
        load.wait()
    for n, ref in enumerate((wq_ref, wk_ref, wv_ref)):
        ref[...] = weight_ref[n * r : (n + 1) * r, :]
    wide_parts = wi_ref.shape[1] // c
    wo_ref[...] = late_ref[:r, :]
    for n in range(wide_parts):
        wi_ref[:, n * c : (n + 1) * c] = late_ref[(1 + n) * r : (2 + n) * r, :]
    w2_ref[...] = late_ref[(1 + wide_parts) * r :, :]
    place = place_ref[:per, :]
    placet_ref[...] = jnp.concatenate([place[:, n * narrow : (n + 1) * narrow] for n in range(folds)], 0).T
    table_ref[...] = place_ref[per : per + few, :narrow]
    line_ref[...] = place_ref[per + few : per + few + 1, : line_ref.shape[1]]
    for store in stores[:count]:
        store.start()
    for n in range(pieces):
        loads[3 + n].wait()
        stores[count + n].start()
    for store in stores:
        store.wait()


def feed_forward(
    ctx_ref, act_ref, pos_ref, cot_ref, late_ref, vec_ref, bias_ref,
    out_ref, first_ref, grad_ref, part_out, sums_ref, bsum_ref,
    wo_acc, wi_acc, w2_acc, slope_ref, wo_ref, wi_ref, w2_ref, part_ref, sems,
):
    step = pl.program_id(0)
    width = ctx_ref.shape[1]
    dp, side, _, _, _, c = late_ref.shape
    group = members(side)
    r = width // len(group)
    parts = bias_ref.shape[1] // dp // c
    tall = bias_ref.shape[1] // len(group)
    spans = [slice(0, r), slice(r, (1 + parts) * r), slice((1 + parts) * r, (1 + parts) * r + tall)]
    everywhere = (slice(None),) * 4

    def fetch(n):
        at = everywhere + (spans[n],)
        return pltpu.make_async_copy(late_ref.at[at], part_ref.at[at], sems.at[n])

    def deliver(n):
        at = everywhere + (spans[n],)
        return pltpu.make_async_copy(part_ref.at[at], part_out.at[at], sems.at[3 + n])

    hidden = bias_ref.shape[1]
    part = 512

    last = pl.num_programs(0) - 1
    vec = lambda n: vec_ref[n : n + 1, :]
    C = hidden // part
    cols = [slice(n * part, (n + 1) * part) for n in range(C)]

    def unpack(n):
        fetch(n).wait()
        for f, (a, b, core) in enumerate(group):
            block = lambda e, lo, n: part_ref[e, a, b, core, lo : lo + n, :]
            if n == 0:
                wo_ref[f * r : (f + 1) * r, :] = jnp.concatenate([block(e, 0, r) for e in range(dp)], 1)
            elif n == 1:
                wi_ref[f * r : (f + 1) * r, :] = jnp.concatenate(
                    [block(e, (1 + m) * r, r) for e in range(dp) for m in range(parts)], 1
                )
            else:
                w2_ref[f * tall : (f + 1) * tall, :] = jnp.concatenate(
                    [block(e, (1 + parts) * r, tall) for e in range(dp)], 1
                )

    def pack(n):
        for e in range(dp):
            for f, (a, b, core) in enumerate(group):
                rows = slice(f * r, (f + 1) * r)
                if n == 0:
                    part_ref[e, a, b, core, :r, :] = wo_acc[rows, e * c : (e + 1) * c].astype(BF16)
                elif n == 1:
                    for m in range(parts):
                        wide = slice((e * parts + m) * c, (e * parts + m + 1) * c)
                        part_ref[e, a, b, core, (1 + m) * r : (2 + m) * r, :] = wi_acc[rows, wide].astype(BF16)
                else:
                    turned = w2_acc[e * c : (e + 1) * c, f * tall : (f + 1) * tall].astype(BF16)
                    part_ref[e, a, b, core, (1 + parts) * r :, :] = turned.T
        deliver(n).start()

    def body(first, final):
        def add(ref, at, value):
            if first:
                ref[at] = value
            else:
                ref[at] += value

        def add_row(n, value):
            add(sums_ref, (slice(n, n + 1), slice(None)), value)

        if first:
            for n in range(3):
                fetch(n).start()
            sums_ref[0:2, :] = jnp.zeros((2, width), F32)
            unpack(0)
        ctx = ctx_ref[...]
        first_sum = act_ref[...].astype(F32) + pos_ref[...].astype(F32) + (nn(ctx, wo_ref[...]) + vec(2))
        center = first_sum - jnp.mean(first_sum, -1, keepdims=True)
        scale_one = lax.rsqrt(jnp.mean(center * center, -1, keepdims=True) + 1e-05)
        z_one = center * scale_one
        normed = z_one * vec(3) + vec(4)
        normed_low = normed.astype(BF16)
        if first:
            unpack(1)
        branch = None
        acts = []
        pre_next = nn(normed_low, wi_ref[:, cols[0]])
        for n in range(C):
            pre = pre_next + bias_ref[:, cols[n]]
            if n + 1 < C:
                pre_next = nn(normed_low, wi_ref[:, cols[n + 1]])
            if n >= 1:
                if first and n == 1:
                    unpack(2)
                term = nn(acts[n - 1], w2_ref[cols[n - 1], :])
                branch = term if branch is None else branch + term
            square = pre * pre
            t = jnp.tanh(pre * (0.7978845608028654 + (0.7978845608028654 * 0.044715) * square))
            half = 0.5 + 0.5 * t
            acts.append((pre * half).astype(BF16))
            slope_ref[:, cols[n]] = half + (0.5 * pre) * (1.0 - t * t) * (
                0.7978845608028654 + (3.0 * 0.7978845608028654 * 0.044715) * square
            )
        branch = branch + nn(acts[C - 1], w2_ref[cols[C - 1], :])
        second_sum = normed + (branch + vec(5))
        center = second_sum - jnp.mean(second_sum, -1, keepdims=True)
        scale_two = lax.rsqrt(jnp.mean(center * center, -1, keepdims=True) + 1e-05)
        z_two = center * scale_two
        out_ref[...] = (z_two * vec(6) + vec(7)).astype(BF16)
        cot = cot_ref[...].astype(F32)
        add_row(6, column_sum(cot * z_two))
        add_row(7, column_sum(cot))
        e = cot * vec(6)
        second_grad = scale_two * (
            e - jnp.mean(e, -1, keepdims=True) - z_two * jnp.mean(e * z_two, -1, keepdims=True)
        )
        branch_grad = second_grad.astype(BF16)
        add_row(5, column_sum(branch_grad))
        branch_t = branch_grad.T
        normed_t = normed_low.T
        normed_grad = second_grad
        grad_next = nt(branch_grad, w2_ref[cols[0], :])
        lows = []
        everything = slice(None)

        def inner(n):
            add(wi_acc, (everything, cols[n]), nn(normed_t, lows[n]))

        def outer(n):
            add(w2_acc, (everything, cols[n]), nn(branch_t, acts[n]))

        for n in range(C):
            pre_grad = grad_next * slope_ref[:, cols[n]]
            if n + 1 < C:
                grad_next = nt(branch_grad, w2_ref[cols[n + 1], :])
            if n < LATER:
                outer(n)
            if n >= 1:
                inner(n - 1)
                normed_grad = normed_grad + nt(lows[n - 1], wi_ref[:, cols[n - 1]])
            lows.append(pre_grad.astype(BF16))
            add(bsum_ref, (everything, cols[n]), column_sum(lows[n]))
        normed_grad = normed_grad + nt(lows[C - 1], wi_ref[:, cols[C - 1]])
        inner(C - 1)
        add_row(3, column_sum(normed_grad * z_one))
        add_row(4, column_sum(normed_grad))
        e = normed_grad * vec(3)
        level = jnp.mean(e, -1, keepdims=True)
        slant = jnp.mean(e * z_one, -1, keepdims=True)
        for n in range(LATER, C):
            outer(n)
        if final:
            pack(1)
            pack(2)
        first_grad = scale_one * (e - level - z_one * slant)
        first_ref[...] = first_grad
        attn_grad = first_grad.astype(BF16)
        add_row(2, column_sum(attn_grad))
        add(wo_acc, (everything, everything), nn(ctx.T, attn_grad))
        grad_ref[...] = nt(attn_grad, wo_ref[...]).astype(BF16)
        if final:
            pack(0)
            for n in range(3):
                deliver(n).wait()

    @pl.when(step == 0)
    def _():
        for n in range(3):
            fetch(n).start()
        for ref in (wo_acc, wi_acc, w2_acc, sums_ref, bsum_ref):
            ref[...] = jnp.zeros_like(ref)
        for n in range(3):
            unpack(n)

    body(False, False)

    @pl.when(step == last)
    def _():
        for n in (1, 2, 0):
            pack(n)
        for n in range(3):
            deliver(n).wait()


def whole(shape):
    return pl.BlockSpec(shape, lambda *_: (0,) * len(shape))


def once(shape):
    return pl.BlockSpec(shape, lambda *_: (0,) * len(shape), pipeline_mode=pl.Buffered(1))


def run_forward(lengths, act, wq, wk, wv, wo, wi, w2, table, place, line):
    rows, seq, width = act.shape
    dp, side = lax.axis_size("dp"), side_of(lax.axis_size("fsdp"))
    r, c = wq.shape
    hidden = wi.shape[1] * dp
    first_rows = 3 * r + place.shape[0] * place.shape[1] // c + SMALL
    late_rows = r + r * wi.shape[1] // c + w2.shape[0]
    row3 = lambda shape: pl.BlockSpec((1,) + shape, lambda i: (i,) + (0,) * len(shape))
    seqs = row3((seq, width))
    st, tt = jax.ShapeDtypeStruct((rows, seq, width), BF16), jax.ShapeDtypeStruct((rows, width, seq), BF16)
    small = [x.shape for x in (wq, wk, wv, wo, wi, w2, table, place, line)]
    anywhere = pl.BlockSpec(memory_space=pl.ANY)
    return pl.pallas_call(
        forward_attention,
        grid=(rows,),
        in_specs=[pl.BlockSpec(memory_space=pltpu.SMEM), anywhere] + [whole(x) for x in small],
        out_specs=[anywhere] * 6 + [seqs, row3((H // 2, 2, seq)), anywhere, anywhere,
                                    whole((table.shape[0] * dp, width)), whole((1, hidden)), anywhere],
        scratch_shapes=[
            pltpu.VMEM(act.shape, BF16),
            pltpu.SemaphoreType.DMA((rows,)),
            pltpu.VMEM((1, seq, width), BF16),
            pltpu.VMEM((1, width, seq), BF16),
            pltpu.VMEM((1, seq, width), BF16),
            pltpu.VMEM((1, width, seq), BF16),
            pltpu.VMEM((1, seq, width), BF16),
            pltpu.VMEM((1, width, seq), BF16),
            pltpu.VMEM((width, 3 * width), BF16),
            pltpu.VMEM((seq, width), BF16),
            pltpu.SemaphoreType.DMA((8,)),
            pltpu.VMEM((width, seq), BF16),
            pltpu.VMEM((2, width, WIN), BF16),
            pltpu.VMEM((dp, side, side, 2, first_rows, c), BF16),
            pltpu.VMEM((late_rows, c), BF16),
            pltpu.SemaphoreType.DMA,
        ]
        + Gather.semaphores(dp, side) * 2,
        out_shape=[
            st, tt, st, tt, st, tt, st, jax.ShapeDtypeStruct((rows, H // 2, 2, seq), F32),
            jax.ShapeDtypeStruct((width, 3 * width), BF16),
            jax.ShapeDtypeStruct((seq, width), BF16),
            jax.ShapeDtypeStruct((table.shape[0] * dp, width), F32),
            jax.ShapeDtypeStruct((1, hidden), F32),
            jax.ShapeDtypeStruct((dp, side, side, 2, late_rows, c), BF16),
        ],
        compiler_params=pltpu.CompilerParams(
            vmem_limit_bytes=VMEM_LIMIT, collective_id=0, has_side_effects=True
        ),
        name="forward_attention",
    )(lengths, act, wq, wk, wv, wo, wi, w2, table, place, line)


def run_backward(lengths, q, qt, k, kt, v, lse, grad, first, lowt, weight, late, sums, bsum):
    rows, seq, width = grad.shape
    dp, side = late.shape[:2]
    late_rows, c = late.shape[4:]
    r = width // (2 * side * side)
    weight_rows = 3 * r
    place_rows = (seq // dp) * r // c + SMALL
    lanes = pl.BlockSpec((rows, seq, PAIR), lambda j: (0, 0, j))
    turned = pl.BlockSpec((rows, PAIR, seq), lambda j: (0, j, 0))
    anywhere = pl.BlockSpec(memory_space=pl.ANY)
    totals = [(n, c) for n in (late_rows, weight_rows, place_rows)]
    return pl.pallas_call(
        backward_attention,
        grid=(H // 2,),
        in_specs=[pl.BlockSpec(memory_space=pltpu.SMEM), lanes, turned, lanes, turned, lanes,
                  pl.BlockSpec((rows, 1, 2, seq), lambda j: (0, j, 0, 0)), lanes, anywhere, anywhere, anywhere,
                  anywhere, once(sums.shape), once(bsum.shape)],
        out_specs=[anywhere] + [whole(x) for x in totals],
        scratch_shapes=[
            pltpu.VMEM(weight.shape, BF16),
            pltpu.VMEM(grad.shape, BF16),
            pltpu.SemaphoreType.DMA((rows + 1,)),
            pltpu.SemaphoreType.DMA((dp,)),
            pltpu.VMEM((width, rows * seq), BF16),
            pltpu.VMEM((rows, PAIR, seq), BF16),
            pltpu.VMEM((rows, PAIR, seq), BF16),
            pltpu.VMEM((rows, seq, PAIR), F32),
            pltpu.VMEM((rows, seq, PAIR), F32),
            pltpu.VMEM((rows * seq, 3 * PAIR), BF16),
            pltpu.VMEM((rows, seq, width), F32),
            pltpu.VMEM(sums.shape, F32),
            pltpu.VMEM((dp, side, side, 2, weight_rows, c), BF16),
            pltpu.VMEM((dp, side, side, 2, place_rows, c), BF16),
            pltpu.VMEM((dp, side, side, late_rows, c), BF16),
            pltpu.SemaphoreType.DMA,
            pltpu.SemaphoreType.DMA,
        ]
        + Reduce.scratch(dp, side, late_rows, c)
        + Reduce.scratch(dp, side, weight_rows, c)
        + Reduce.scratch(dp, side, place_rows, c),
        out_shape=[jax.ShapeDtypeStruct(grad.shape, BF16)] + [jax.ShapeDtypeStruct(x, F32) for x in totals],
        compiler_params=pltpu.CompilerParams(
            vmem_limit_bytes=VMEM_LIMIT, collective_id=1, has_side_effects=True
        ),
        name="backward_attention",
    )(lengths, q, qt, k, kt, v, lse, grad, first, lowt, weight, late, sums, bsum)


def run_hand_out(late, weight, place, grad, shapes):
    anywhere = pl.BlockSpec(memory_space=pl.ANY)
    tokens = grad.reshape(-1, grad.shape[-1])
    dma = pltpu.SemaphoreType.DMA
    pieces = 4
    return pl.pallas_call(
        hand_out,
        in_specs=[anywhere] * 4,
        out_specs=[anywhere] * (1 + len(shapes)),
        out_shape=[jax.ShapeDtypeStruct(tokens.shape, BF16)] + [jax.ShapeDtypeStruct(x, F32) for x in shapes],
        scratch_shapes=[pltpu.VMEM(x.shape, x.dtype) for x in (late, weight, place, tokens)]
        + [pltpu.VMEM(x, F32) for x in shapes]
        + [dma((3 + pieces,)), dma((len(shapes) + pieces,))],
        name="hand_out",
    )(late, weight, place, tokens)


def run_feed_forward(ctx, act, pos, cot, late, vec, bias, tile=512):
    tokens, width = ctx.shape
    seq = pos.shape[0]
    hidden = bias.shape[1]
    per_row = seq // tile
    tok = pl.BlockSpec((tile, width), lambda t: (t, 0))
    return pl.pallas_call(
        feed_forward,
        grid=(tokens // tile,),
        in_specs=[tok, tok, pl.BlockSpec((tile, width), lambda t: (t % per_row, 0)), tok,
                  pl.BlockSpec(memory_space=pl.ANY), whole(vec.shape), whole(bias.shape)],
        out_specs=[tok, tok, tok, pl.BlockSpec(memory_space=pl.ANY), whole((8, width)),
                   whole((1, hidden))],
        scratch_shapes=[
            pltpu.VMEM((width, width), F32),
            pltpu.VMEM((width, hidden), F32),
            pltpu.VMEM((width, hidden), F32),
            pltpu.VMEM((tile, hidden), F32),
            pltpu.VMEM((width, width), BF16),
            pltpu.VMEM((width, hidden), BF16),
            pltpu.VMEM((hidden, width), BF16),
            pltpu.VMEM(late.shape, BF16),
            pltpu.SemaphoreType.DMA((6,)),
        ],
        out_shape=[
            jax.ShapeDtypeStruct((tokens, width), BF16),
            jax.ShapeDtypeStruct((tokens, width), F32),
            jax.ShapeDtypeStruct((tokens, width), BF16),
            jax.ShapeDtypeStruct(late.shape, BF16),
            jax.ShapeDtypeStruct((8, width), F32),
            jax.ShapeDtypeStruct((1, hidden), F32),
        ],
        compiler_params=pltpu.CompilerParams(vmem_limit_bytes=VMEM_LIMIT),
        name="feed_forward",
    )(ctx, act, pos, cot, late, vec, bias)


def shards(
    activations, window_lengths, query_weight, key_weight, value_weight, output_weight, inner_weight, outer_weight,
    vectors, positions, inner_bias, output_cotangent,
):
    rows, seq, width = activations.shape
    q, qt, k, kt, v, lowt, ctx, lse, weight, pos, vec, bias, late = run_forward(
        window_lengths, activations, query_weight, key_weight, value_weight, output_weight, inner_weight, outer_weight,
        vectors, positions.T, inner_bias.reshape(1, -1),
    )
    flat = lambda x: x.reshape(rows * seq, width)
    deep = lambda x: x.reshape(rows, seq, width)
    out, first, grad, part, sums, bsum = run_feed_forward(
        flat(ctx), flat(activations), pos, flat(output_cotangent), late, vec, bias
    )
    input_grad, *sums = run_backward(
        window_lengths, q, qt, k, kt, v, lse, deep(grad), deep(first), lowt, weight, part, sums, bsum
    )
    shapes = [x.shape for x in (query_weight, key_weight, value_weight, output_weight, inner_weight, outer_weight,
                                vectors, positions.T)] + [(1, inner_bias.shape[0])]
    owned = run_hand_out(*sums, input_grad, shapes)
    return (deep(out), owned[0].reshape(input_grad.shape)) + tuple(owned[1:8]) + (owned[8].T, owned[9].reshape(-1))


def solution(mesh):
    tokens = P(("dp", "fsdp"), None, None)
    matrix = P("fsdp", "dp")
    table = P("dp", "fsdp")
    line = P(("dp", "fsdp"))
    return jax.shard_map(
        shards,
        mesh=mesh,
        in_specs=(tokens, P(("dp", "fsdp"), None)) + (matrix,) * 6 + (table, table, line, tokens),
        out_specs=(tokens, tokens) + (matrix,) * 6 + (table, table, line),
        check_vma=False,
    )
```

```python
import functools

import jax
import jax.numpy as jnp
from jax import lax
from jax.experimental import pallas as pl
from jax.experimental.pallas import tpu as pltpu
from jax.sharding import PartitionSpec as P

H = 8
HD = 64
WIN = 256
PAIR = 2 * HD
VMEM_LIMIT = 62 * 1024 * 1024
F32 = jnp.float32
BF16 = jnp.bfloat16
MESH = pl.DeviceIdType.MESH
SMALL = 16
LATER = 2


def nn(left, right):
    return lax.dot_general(left, right, (((1,), (0,)), ((), ())), preferred_element_type=F32)


def nt(left, right):
    return lax.dot_general(left, right, (((1,), (1,)), ((), ())), preferred_element_type=F32)


def tn(left, right):
    return lax.dot_general(left, right, (((0,), (0,)), ((), ())), preferred_element_type=F32)


def column_sum(value):
    return jnp.sum(value.astype(F32), 0, keepdims=True)


def head_rows(pair, which):
    zeros = jnp.zeros((HD, pair.shape[1]), pair.dtype)
    if which == 0:
        return jnp.concatenate([pair[:HD], zeros], 0)
    return jnp.concatenate([zeros, pair[HD:]], 0)


def head_lanes(pair, which):
    lane = lax.broadcasted_iota(jnp.int32, pair.shape, 1)
    keep = (lane < HD) if which == 0 else (lane >= HD)
    return jnp.where(keep, pair, jnp.zeros_like(pair))


def causal(scores):
    key = lax.broadcasted_iota(jnp.int32, scores.shape, 0)
    query = lax.broadcasted_iota(jnp.int32, scores.shape, 1)
    return jnp.where(key <= query, scores, -1e30)


def block_of(block):
    return slice(block * WIN, (block + 1) * WIN)


def spots_of(block):
    return [block_of(n) for n in (block, block - 1) if n >= 0]


def pair_of(head):
    return slice(head // 2 * PAIR, (head // 2 + 1) * PAIR)


def staggered(tasks, stages):
    held = {}
    for step in range(len(tasks) + len(stages) - 1):
        for n, stage in enumerate(stages):
            task = step - n
            if 0 <= task < len(tasks):
                args = (held.pop(task),) if n else ()
                held[task] = stage(*tasks[task], *args)


class Place:
    def __init__(self):
        fsdp = lax.axis_index("fsdp")
        self.d, self.dp = lax.axis_index("dp"), lax.axis_size("dp")
        self.side = side_of(lax.axis_size("fsdp"))
        self.chip, self.core = fsdp // 2, lax.rem(fsdp, 2)
        y, x = self.chip // self.side, lax.rem(self.chip, self.side)
        self.a = y + self.core * (x - y)
        self.b = x + self.core * (y - x)

    def device(self, a, b):
        straight, turned = a * self.side + b, b * self.side + a
        return {"fsdp": (straight + self.core * (turned - straight)) * 2 + self.core}

    def sibling(self):
        return {"fsdp": self.chip * 2 + 1 - self.core}

    def at_a(self, n):
        return lax.rem(self.a + n + self.side, self.side)

    def at_b(self, n):
        return lax.rem(self.b + n + self.side, self.side)

    def at_dp(self, n):
        return lax.rem(self.d + n + self.dp, self.dp)


def side_of(fsdp):
    side = 1
    while side * side * 2 < fsdp:
        side += 1
    assert side * side * 2 == fsdp
    return side


def members(side):
    found = []
    for f in range(2 * side * side):
        y, x = f // 2 // side, f // 2 % side
        found.append((x, y, 1) if f % 2 else (y, x, 0))
    return found


def remote(src, dst, send, recv, device):
    return pltpu.make_async_remote_copy(
        src_ref=src, dst_ref=dst, send_sem=send, recv_sem=recv, device_id=device, device_id_type=MESH
    )


def greet(at):
    barrier = pltpu.get_barrier_semaphore()
    others = [{"dp": at.at_dp(n)} for n in range(1, at.dp)]
    others += [at.device(at.a, at.at_b(n)) for n in range(1, at.side)]
    others += [at.device(at.at_a(n), at.b) for n in range(1, at.side)]
    others.append(at.sibling())
    for other in others:
        pl.semaphore_signal(barrier, inc=1, device_id=other, device_id_type=MESH)
    return len(others)


def meet(count):
    pl.semaphore_wait(pltpu.get_barrier_semaphore(), count)


class Gather:
    COUNT = 8

    def __init__(self, buf, sems, at):
        self.buf, self.at = buf, at
        self.zs, self.zr, self.bs, self.br, self.sa, self.ra, self.cs, self.cr = sems

    @staticmethod
    def semaphores(dp, side):
        dma = pltpu.SemaphoreType.DMA
        shapes = [(dp,), (dp, side), (dp, side, side), (side, side)]
        return [dma(x) for x in shapes for _ in range(2)]

    def along_dp(self, o):
        at = self.at
        block = self.buf.at[at.d, at.a, at.b, at.core]
        return remote(block, block, self.zs.at[o], self.zr.at[o], {"dp": at.at_dp(o)})

    def along_b(self, o, p):
        at = self.at
        block = self.buf.at[at.at_dp(-o), at.a, at.b, at.core]
        return remote(block, block, self.bs.at[o, p], self.br.at[o, p], at.device(at.a, at.at_b(p)))

    def along_a(self, o, p, q):
        at = self.at
        block = self.buf.at[at.at_dp(-o), at.a, at.at_b(-p), at.core]
        return remote(block, block, self.sa.at[o, p, q], self.ra.at[o, p, q], at.device(at.at_a(q), at.b))

    def to_core(self, q, p):
        at = self.at
        block = self.buf.at[:, at.at_a(-q), at.at_b(-p), at.core]
        return remote(block, block, self.cs.at[q, p], self.cr.at[q, p], at.sibling())

    def begin(self):
        for o in range(1, self.at.dp):
            self.along_dp(o).start()

    def pass_on(self, o):
        for p in range(1, self.at.side):
            self.along_b(o, p).start()

    def far(self, o):
        for q in range(1, self.at.side):
            self.along_a(o, 0, q).start()

    def spread(self, o):
        self.along_dp(o).wait_recv()
        self.pass_on(o)

    def relay(self, o):
        for p in range(1, self.at.side):
            self.along_b(o, p).wait_recv()
            for q in range(1, self.at.side):
                self.along_a(o, p, q).start()

    def near(self):
        for p in range(self.at.side):
            self.to_core(0, p).start()

    def share(self):
        for p in range(self.at.side):
            for q in range(1, self.at.side):
                for o in range(self.at.dp):
                    self.along_a(o, p, q).wait_recv()
                self.to_core(q, p).start()

    def arrive(self):
        for q in range(self.at.side):
            for p in range(self.at.side):
                self.to_core(q, p).wait_recv()

    def close(self):
        for o in range(1, self.at.dp):
            self.along_dp(o).wait_send()
        for o in range(self.at.dp):
            for p in range(1, self.at.side):
                self.along_b(o, p).wait_send()
            for p in range(self.at.side):
                for q in range(1, self.at.side):
                    self.along_a(o, p, q).wait_send()
        for q in range(self.at.side):
            for p in range(self.at.side):
                self.to_core(q, p).wait_send()


def add_up(terms):
    if len(terms) == 2:
        return terms[0] + terms[1]
    return sum(x.astype(F32) for x in terms).astype(BF16)


class Reduce:
    COUNT = 13

    def __init__(self, part, scratch, at, own=None):
        self.part, self.at = part, at
        self.own, self.own_sem = own or (None, None)
        (self.pair, self.plane, self.row, self.mine, self.line,
         self.cs, self.cr, self.sa, self.ra, self.bs, self.br, self.zs, self.zr) = scratch

    @staticmethod
    def scratch(dp, side, rows, c):
        dma = pltpu.SemaphoreType.DMA
        return [
            pltpu.VMEM((dp, side, side, rows, c), BF16),
            pltpu.VMEM((side - 1, dp, side, rows, c), BF16),
            pltpu.VMEM((side - 1, dp, rows, c), BF16),
            pltpu.VMEM((dp, rows, c), BF16),
            pltpu.VMEM((dp - 1, rows, c), BF16),
        ] + [dma((dp,))] * 2 + [dma((dp, side))] * 4 + [dma((dp,))] * 2

    def to_core(self, e):
        at = self.at
        return remote(self.part.at[e, :, :, 1 - at.core], self.pair.at[e], self.cs.at[e], self.cr.at[e], at.sibling())

    def along_a(self, e, q):
        at = self.at
        to = at.at_a(q)
        return remote(
            self.pair.at[e, to], self.plane.at[q - 1, e], self.sa.at[e, q], self.ra.at[e, q], at.device(to, at.b)
        )

    def along_b(self, e, p):
        at = self.at
        to = at.at_b(p)
        return remote(
            self.pair.at[e, at.a, to], self.row.at[p - 1, e], self.bs.at[e, p], self.br.at[e, p], at.device(at.a, to)
        )

    def along_dp(self, o):
        at = self.at
        to = at.at_dp(o)
        return remote(self.mine.at[to], self.line.at[o - 1], self.zs.at[o], self.zr.at[o], {"dp": to})

    def own_half(self):
        return pltpu.make_async_copy(self.part.at[:, :, :, self.at.core], self.own, self.own_sem)

    def begin(self, e):
        self.to_core(e).start()

    def across(self, e):
        at = self.at
        self.to_core(e).wait_recv()
        for n in list(range(1, at.side)) + [0]:
            a = at.at_a(n)
            for b in range(at.side):
                own = self.part[e, a, b, at.core] if self.own is None else self.own[e, a, b]
                self.pair[e, a, b] = add_up([own, self.pair[e, a, b]])
            if n:
                self.along_a(e, n).start()

    def middle(self, e):
        at = self.at
        for q in range(1, at.side):
            self.along_a(e, q).wait_recv()
        for n in list(range(1, at.side)) + [0]:
            b = at.at_b(n)
            terms = [self.pair[e, at.a, b]] + [self.plane[q - 1, e, b] for q in range(1, at.side)]
            self.pair[e, at.a, b] = add_up(terms)
            if n:
                self.along_b(e, n).start()

    def along(self, e):
        at = self.at
        for p in range(1, at.side):
            self.along_b(e, p).wait_recv()
        self.mine[e] = add_up([self.pair[e, at.a, at.b]] + [self.row[p - 1, e] for p in range(1, at.side)])

        @pl.when(e != at.d)
        def _():
            self.along_dp(lax.rem(e - at.d + at.dp, at.dp)).start()

    def result(self):
        at = self.at
        for o in range(1, at.dp):
            self.along_dp(o).wait_recv()
        total = self.mine[at.d].astype(F32)
        for o in range(1, at.dp):
            total = total + self.line[o - 1].astype(F32)
        return total

    def close(self):
        at = self.at
        for e in range(at.dp):
            self.to_core(e).wait_send()
            for n in range(1, at.side):
                self.along_a(e, n).wait_send()
                self.along_b(e, n).wait_send()
        for o in range(1, at.dp):
            self.along_dp(o).wait_send()


def apart(lengths_ref, row, block):
    total = jnp.int32(0)
    cut = jnp.bool_(False)
    for n in range(lengths_ref.shape[1]):
        total = total + lengths_ref[row, n]
        cut = cut | (total == block * WIN)
    return jnp.where(cut, jnp.float32(-1e30), jnp.float32(0.0))


def forward_attention(
    lengths_ref, act_in, wq_ref, wk_ref, wv_ref, wo_ref, wi_ref, w2_ref, table_ref, place_ref, line_ref,
    q_out, qt_out, k_out, kt_out, v_out, lowt_out, ctx_ref, lse_ref, weight_out, pos_out, vec_ref, bias_ref, late_ref,
    act_ref, act_sems, q_ref, qt_ref, k_ref, kt_ref, v_ref, lowt_ref, weight_ref, pos_ref, out_sems,
    vt_ref, ctxt_ref, early_ref, own_ref, own_sem, *sems,
):
    row = pl.program_id(0)
    rows = pl.num_programs(0)
    width = act_in.shape[2]
    blocks = act_in.shape[1] // WIN
    at = Place()
    dp = at.dp
    here = (at.d, at.a, at.b, at.core)
    r, c = wq_ref.shape
    narrow, held = place_ref.shape
    folds = c // narrow
    per = held // folds
    early = Gather(early_ref, sems[: Gather.COUNT], at)
    late = Gather(late_ref, sems[Gather.COUNT :], at)

    def own_copy():
        return pltpu.make_async_copy(own_ref, late_ref.at[here], own_sem)

    def act_copy(of_row):
        return pltpu.make_async_copy(act_in.at[of_row], act_ref.at[of_row], act_sems.at[of_row])

    def row_copies(of_row):
        pairs = ((q_ref, q_out), (qt_ref, qt_out), (k_ref, k_out), (kt_ref, kt_out), (v_ref, v_out),
                 (lowt_ref, lowt_out))
        return [
            pltpu.make_async_copy(src.at[0], dst.at[of_row], out_sems.at[n]) for n, (src, dst) in enumerate(pairs)
        ]

    def table_copies():
        pairs = ((weight_ref, weight_out), (pos_ref, pos_out))
        return [pltpu.make_async_copy(src, dst, out_sems.at[6 + n]) for n, (src, dst) in enumerate(pairs)]

    @pl.when(row == 0)
    def _():
        count = greet(at)
        for n in range(act_in.shape[0]):
            act_copy(n).start()
        for n, ref in enumerate((wq_ref, wk_ref, wv_ref)):
            early_ref[here + (slice(n * r, (n + 1) * r),)] = ref[...]
        place = place_ref[...].T
        early_ref[here + (slice(3 * r, 3 * r + per),)] = jnp.concatenate(
            [place[n * per : (n + 1) * per] for n in range(folds)], 1
        )
        wide = lambda x: jnp.concatenate([x, jnp.zeros((x.shape[0], c - x.shape[1]), F32)], 1)
        table = wide(table_ref[...].astype(F32))
        line = wide(line_ref[...].astype(F32))
        few = table.shape[0]
        small = jnp.concatenate([table, line, jnp.zeros((SMALL - few - 1, c), F32)], 0)
        early_ref[here + (slice(3 * r + per, None),)] = small.astype(BF16)
        own_ref[:r, :] = wo_ref[...]
        wide_parts = wi_ref.shape[1] // c
        for n in range(wide_parts):
            own_ref[(1 + n) * r : (2 + n) * r, :] = wi_ref[:, n * c : (n + 1) * c]
        own_ref[(1 + wide_parts) * r :, :] = w2_ref[...]
        own_copy().start()
        meet(count)
        early.begin()
        early.pass_on(0)
        early.far(0)
        early.relay(0)
        early.spread(1)
        early.far(1)
        for o in range(2, dp):
            early.spread(o)
            early.relay(o - 1)
            early.far(o)
        own_copy().wait()
        late.begin()
        early.relay(dp - 1)
        early.near()
        late.pass_on(0)
        late.far(0)
        early.share()
        late.relay(0)
        late.spread(1)
        late.far(1)
        early.arrive()
        group = members(at.side)
        for f, (a, b, core) in enumerate(group):
            for n in range(3):
                weight_ref[f * r : (f + 1) * r, n * width : (n + 1) * width] = jnp.concatenate(
                    [early_ref[e, a, b, core, n * r : (n + 1) * r, :] for e in range(dp)], 1
                )
        tables = []
        lines = []
        for e in range(dp):
            for n in range(folds):
                spot = slice(e * held + n * per, e * held + (n + 1) * per)
                pos_ref[spot, :] = jnp.concatenate(
                    [
                        early_ref[e, a, b, core, 3 * r : 3 * r + per, :][:, n * narrow : (n + 1) * narrow]
                        for a, b, core in group
                    ],
                    1,
                )
            smalls = [early_ref[e, a, b, core, 3 * r + per :, :].astype(F32) for a, b, core in group]
            tables.append(jnp.concatenate([x[:few, :narrow] for x in smalls], 1))
            lines.extend(x[few : few + 1, : line_ref.shape[1]] for x in smalls)
        vec_ref[...] = jnp.concatenate(tables, 0)
        bias_ref[...] = jnp.concatenate(lines, 1)
        for copy in table_copies():
            copy.start()

    @pl.when(row > 0)
    def _():
        for copy in row_copies(row - 1):
            copy.wait()

    act_copy(row).wait()

    def project(step, carry):
        spot = pl.ds(pl.multiple_of(step * WIN, WIN), WIN)
        low = (act_ref[row, spot, :].astype(F32) + pos_ref[spot, :].astype(F32)).astype(BF16)
        lowt_ref[0, :, spot] = low.T
        every = nn(low, weight_ref[...])
        q = (every[:, :width] + vec_ref[0:1, :]).astype(BF16)
        q = (q.astype(F32) * 0.125).astype(BF16)
        k = every[:, width : 2 * width].astype(BF16)
        v = (every[:, 2 * width :] + vec_ref[1:2, :]).astype(BF16)
        q_ref[0, spot, :] = q
        k_ref[0, spot, :] = k
        v_ref[0, spot, :] = v
        qt_ref[0, :, spot] = q.T
        kt_ref[0, :, spot] = k.T
        vt_ref[:, spot] = v.T
        return carry

    lax.fori_loop(0, blocks, project, 0)
    for copy in row_copies(row):
        copy.start()

    @pl.when(row == 0)
    def _():
        for o in range(2, dp // 2 + 1):
            late.spread(o)
            late.far(o)
        late.relay(1)

    def score(block, head):
        q_head = head_rows(qt_ref[0, pair_of(head), block_of(block)], head % 2)
        return [nn(k_ref[0, spot, pair_of(head)], q_head) for spot in spots_of(block)]

    def soften(block, head, scores):
        scores[0] = causal(scores[0])
        peaks = [jnp.max(x, 0, keepdims=True) for x in scores]
        peak = peaks[0]
        if block:
            peak = jnp.maximum(peak, peaks[1] + apart(lengths_ref, row, block))
        expo = [jnp.exp(scores[0] - peak)]
        if block:
            expo.append(jnp.exp(scores[1] - (peak - apart(lengths_ref, row, block))))
        total = sum(jnp.sum(x, 0, keepdims=True) for x in expo)
        lse_ref[0, head // 2, head % 2 : head % 2 + 1, block_of(block)] = peak + jnp.log(total)
        return [x.astype(BF16) for x in expo], total

    def combine(block, head, soft):
        expo, total = soft
        half = slice(head * HD, (head + 1) * HD)
        out = sum(nn(vt_ref[half, spot], x) for spot, x in zip(spots_of(block), expo))
        ctxt_ref[block % 2, half, :] = (out * (1.0 / total)).astype(BF16)
        if head == H - 1:
            ctx_ref[0, block_of(block), :] = ctxt_ref[block % 2].T

    stages = (score, soften, combine)
    tasks = [(block, head) for block in range(blocks) for head in range(H)]
    quarter = len(tasks) // 4
    staggered(tasks[:quarter], stages)

    @pl.when(row == 0)
    def _():
        for o in range(dp // 2 + 1, dp):
            late.spread(o)
            late.far(o)

    staggered(tasks[quarter : 2 * quarter], stages)

    @pl.when(row == 0)
    def _():
        for o in range(2, dp - 1):
            late.relay(o)

    @pl.when(row == rows - 1)
    def _():
        late.share()

    staggered(tasks[2 * quarter :], stages)

    @pl.when(row == 0)
    def _():
        late.relay(dp - 1)
        late.near()

    @pl.when(row == rows - 1)
    def _():
        late.arrive()
        early.close()
        late.close()
        for copy in row_copies(row) + table_copies():
            copy.wait()


def backward_attention(
    lengths_ref, q_ref, qt_ref, k_ref, kt_ref, v_ref, lse_ref, grad_ref, first_ref, lowt_in, weight_in,
    late_ref, sums_ref, bsum_ref,
    input_out, late_sum_ref, weight_sum_ref, place_sum_ref,
    weight_ref, input_ref, load_sems, input_sems, lowt_ref, gradt_ref, dqt_ref, dk_ref, dv_ref, every_ref, start_ref, total_ref, wpart_ref, ppart_ref, own_ref,
    own_sem, first_sem, *scratch,
):
    step = pl.program_id(0)
    last = H // 2 - 1
    rows, width, seq = lowt_in.shape
    blocks = seq // WIN
    at = Place()
    dp = at.dp
    group = members(at.side)
    r = width // len(group)
    c = width // dp
    narrow = r
    held = seq // dp
    folds = c // narrow
    per = held // folds
    few = sums_ref.shape[0] // dp
    single = bsum_ref.shape[1] // (dp * len(group))
    shared = dp // (H // 2)
    count = Reduce.COUNT
    late = Reduce(late_ref, scratch[:count], at, (own_ref, own_sem))
    weights = Reduce(wpart_ref, scratch[count : 2 * count], at)
    places = Reduce(ppart_ref, scratch[2 * count :], at)
    first_copy = pltpu.make_async_copy(first_ref, start_ref, first_sem)
    loads = [
        pltpu.make_async_copy(lowt_in.at[row], lowt_ref.at[:, row * seq : (row + 1) * seq], load_sems.at[row])
        for row in range(rows)
    ]
    loads.append(pltpu.make_async_copy(weight_in, weight_ref, load_sems.at[rows]))
    arriving = loads + [first_copy]

    def input_copy(e):
        spot = (slice(None), slice(e * held, (e + 1) * held))
        return pltpu.make_async_copy(input_ref.at[spot], input_out.at[spot], input_sems.at[e])

    pieces = lambda j: [j * shared + n for n in range(shared)]
    nearest = [at.at_dp(n + 1) for n in range(dp)]

    @pl.when(step == 0)
    def _():
        greet(at)
        for load in arriving:
            load.start()
        late.own_half().start()
        total_ref[...] = sums_ref[...]

    for row in range(rows):
        for block in range(blocks):
            gradt_ref[row, :, block_of(block)] = grad_ref[row, block_of(block), :].T

    def score(row, block, head):
        q_head = head_rows(qt_ref[row, :, block_of(block)], head)
        g_head = head_rows(gradt_ref[row, :, block_of(block)], head)
        scores = [nn(k_ref[row, spot, :], q_head) for spot in spots_of(block)]
        return scores, [nn(v_ref[row, spot, :], g_head) for spot in spots_of(block)]

    def soften(row, block, head, products):
        scores, prob_grads = products
        lse = lse_ref[row, 0, head : head + 1, block_of(block)]
        probs = [jnp.exp(causal(scores[0]) - lse)]
        if block:
            probs.append(jnp.exp(scores[1] - (lse - apart(lengths_ref, row, block))))
        inner = sum(jnp.sum(p * g, 0, keepdims=True) for p, g in zip(probs, prob_grads))
        score_grads = [(p * (g - inner)).astype(BF16) for p, g in zip(probs, prob_grads)]
        return [p.astype(BF16) for p in probs], score_grads

    waiting = {}

    def combine(row, block, head, soft):
        half = slice(head * HD, (head + 1) * HD)
        dq = sum(nn(kt_ref[row, half, spot], x) for spot, x in zip(spots_of(block), soft[1]))
        dqt_ref[row, half, block_of(block)] = (dq * 0.125).astype(BF16)
        if head == 0:
            waiting[row, block] = soft
            return
        even = waiting.pop((row, block))
        g = grad_ref[row, block_of(block), :]
        q = q_ref[row, block_of(block), :]
        g_both = jnp.concatenate([head_lanes(g, 0), head_lanes(g, 1)], 0)
        q_both = jnp.concatenate([head_lanes(q, 0), head_lanes(q, 1)], 0)
        for n, spot in enumerate(spots_of(block)):
            dv = nn(jnp.concatenate([even[0][n], soft[0][n]], 1), g_both)
            dk = nn(jnp.concatenate([even[1][n], soft[1][n]], 1), q_both)
            if n or block == blocks - 1:
                dv_ref[row, spot, :] = dv
                dk_ref[row, spot, :] = dk
            else:
                dv_ref[row, spot, :] += dv
                dk_ref[row, spot, :] += dk

    def attend(*chosen):
        tasks = [(row, block, head) for block in chosen for row in range(rows) for head in range(2)]
        staggered(tasks, (score, soften, combine))
        for row in range(rows):
            for block in chosen:
                spot = block_of(block)
                every = [dqt_ref[row, :, spot].T, dk_ref[row, spot, :].astype(BF16), dv_ref[row, spot, :].astype(BF16)]
                every_ref[row * seq + block * WIN : row * seq + (block + 1) * WIN, :] = jnp.concatenate(every, 1)

    half = dp // 2
    downward = list(range(blocks))[::-1]
    feats = pl.ds(pl.multiple_of(step * PAIR, PAIR), PAIR)

    def sum_tokens():
        total_ref[0:1, feats] = column_sum(every_ref[:, :PAIR])
        total_ref[1:2, feats] = column_sum(every_ref[:, 2 * PAIR :])

    def send_weights():
        owned = nn(lowt_ref[...], every_ref[...])
        for i, e in enumerate(pieces(step)):
            for f, (a, b, core) in enumerate(group):
                for n in range(3):
                    lanes = slice(n * PAIR + i * c, n * PAIR + (i + 1) * c)
                    wpart_ref[e, a, b, core, n * r : (n + 1) * r, :] = owned[f * r : (f + 1) * r, lanes].astype(BF16)
            weights.begin(e)

    def column():
        return jnp.concatenate(
            [weight_ref[:, pl.ds(pl.multiple_of(n * width + step * PAIR, PAIR), PAIR)] for n in range(3)], 1
        )

    def weights_on():
        @pl.when(step > 0)
        def _():
            for e in pieces(step - 1):
                weights.across(e)

    @pl.when(step < last)
    def _():
        attend(*downward[: blocks // 2])

        @pl.when(step == 0)
        def _():
            meet(dp + 2 * at.side - 2)
            for e in nearest:
                late.begin(e)

        @pl.when(step == 1)
        def _():
            for e in nearest[: half // 2]:
                late.middle(e)

        @pl.when(step == 2)
        def _():
            for e in nearest[half : half + half // 2]:
                late.middle(e)
            for e in nearest[: half // 2]:
                late.along(e)

        weights_on()
        attend(*downward[blocks // 2 :])

        @pl.when(step == 0)
        def _():
            late.own_half().wait()
            for e in nearest:
                late.across(e)
            for load in arriving:
                load.wait()

        sum_tokens()
        send_weights()

        @pl.when(step == 1)
        def _():
            for e in nearest[half // 2 : half]:
                late.middle(e)

        @pl.when(step == 2)
        def _():
            for e in nearest[half + half // 2 :]:
                late.middle(e)
            for e in nearest[half // 2 : half]:
                late.along(e)
            for e in pieces(0):
                weights.middle(e)

        tile = 2 * WIN
        turned = column()
        for row in range(rows):
            for n in range(seq // tile):
                spot = slice(n * tile, (n + 1) * tile)
                start_ref[row, spot, :] += nt(every_ref[row * seq + n * tile : row * seq + (n + 1) * tile, :], turned)

    @pl.when(step == last)
    def _():
        wide = lambda x: jnp.concatenate([x, jnp.zeros((x.shape[0], c - x.shape[1]), F32)], 1)
        turned = column()

        def finish(e):
            total = None
            for row in range(rows):
                spot = slice(e * held, (e + 1) * held)
                grad = start_ref[row, spot, :] + nt(every_ref[row * seq + e * held : row * seq + (e + 1) * held, :], turned)
                input_ref[row, spot, :] = grad.astype(BF16)
                total = grad if total is None else total + grad
            total = total.astype(BF16)
            for f, (a, b, core) in enumerate(group):
                lanes = slice(f * narrow, (f + 1) * narrow)
                ppart_ref[e, a, b, core, :per, :] = jnp.concatenate(
                    [total[n * per : (n + 1) * per, lanes] for n in range(folds)], 1
                )
                table = total_ref[e * few : (e + 1) * few, lanes]
                spot = (e * len(group) + f) * single
                line = bsum_ref[:, spot : spot + single]
                filler = jnp.zeros((SMALL - few - 1, c), F32)
                ppart_ref[e, a, b, core, per:, :] = jnp.concatenate([wide(table), wide(line), filler], 0).astype(BF16)
            places.begin(e)
            input_copy(e).start()

        def places_of(block):
            return [e for e in range(dp) if e * held // WIN == block]

        def on(step_of, *chosen):
            for block in chosen:
                for e in places_of(block):
                    step_of(e)

        attend(*downward[: blocks // 2])
        for e in nearest[half:]:
            late.along(e)
        weights_on()
        on(finish, *downward[: blocks // 2])
        attend(*downward[blocks // 2 : -1])
        on(places.across, *downward[: blocks // 2])
        on(finish, *downward[blocks // 2 : -1])
        for e in pieces(last - 2):
            weights.middle(e)
        for e in pieces(last - 3):
            weights.along(e)
        attend(downward[-1])
        sum_tokens()
        on(finish, downward[-1])
        on(places.across, *downward[blocks // 2 : -1])
        on(places.across, downward[-1])
        for e in pieces(last - 1):
            weights.middle(e)
        send_weights()
        on(places.middle, *downward[: blocks // 2])
        on(places.middle, *downward[blocks // 2 : -1])
        on(places.middle, downward[-1])
        for e in pieces(last):
            weights.across(e)
        on(places.along, *downward[: blocks // 2])
        on(places.along, *downward[blocks // 2 : -1])
        on(places.along, downward[-1])
        for e in pieces(last - 2):
            weights.along(e)
        for e in pieces(last - 1):
            weights.along(e)
        for e in pieces(last):
            weights.middle(e)
        late_sum_ref[...] = late.result()
        for e in pieces(last):
            weights.along(e)
        place_sum_ref[...] = places.result()
        weight_sum_ref[...] = weights.result()
        late.close()
        weights.close()
        places.close()
        for e in range(dp):
            input_copy(e).wait()


def hand_out(late_in, weight_in, place_in, input_in, *refs):
    count = (len(refs) - 7) // 2
    outs, (late_ref, weight_ref, place_ref, input_ref), stages = refs[: count + 1], refs[count + 1 : count + 5], refs[count + 5 : -2]
    load_sems, store_sems = refs[-2:]
    wq_ref, wk_ref, wv_ref, wo_ref, wi_ref, w2_ref, table_ref, placet_ref, line_ref = stages
    copy = pltpu.make_async_copy
    small = [(late_in, late_ref), (weight_in, weight_ref), (place_in, place_ref)]
    loads = [copy(src, dst, load_sems.at[n]) for n, (src, dst) in enumerate(small)]
    pieces = load_sems.shape[0] - len(small)
    some = input_in.shape[0] // pieces
    spots = [slice(n * some, (n + 1) * some) for n in range(pieces)]
    loads += [copy(input_in.at[x], input_ref.at[x], load_sems.at[3 + n]) for n, x in enumerate(spots)]
    stores = [copy(src, dst, store_sems.at[n]) for n, (src, dst) in enumerate(zip(stages, outs[1:]))]
    stores += [copy(input_ref.at[x], outs[0].at[x], store_sems.at[count + n]) for n, x in enumerate(spots)]
    for load in loads:
        load.start()
    r, c = wq_ref.shape
    few, narrow = table_ref.shape
    held = placet_ref.shape[1]
    folds = c // narrow
    per = held // folds
    for load in loads[:3]:
        load.wait()
    for n, ref in enumerate((wq_ref, wk_ref, wv_ref)):
        ref[...] = weight_ref[n * r : (n + 1) * r, :]
    wide_parts = wi_ref.shape[1] // c
    wo_ref[...] = late_ref[:r, :]
    for n in range(wide_parts):
        wi_ref[:, n * c : (n + 1) * c] = late_ref[(1 + n) * r : (2 + n) * r, :]
    w2_ref[...] = late_ref[(1 + wide_parts) * r :, :]
    place = place_ref[:per, :]
    placet_ref[...] = jnp.concatenate([place[:, n * narrow : (n + 1) * narrow] for n in range(folds)], 0).T
    table_ref[...] = place_ref[per : per + few, :narrow]
    line_ref[...] = place_ref[per + few : per + few + 1, : line_ref.shape[1]]
    for store in stores[:count]:
        store.start()
    for n in range(pieces):
        loads[3 + n].wait()
        stores[count + n].start()
    for store in stores:
        store.wait()


def feed_forward(
    ctx_ref, act_ref, pos_ref, cot_ref, late_ref, vec_ref, bias_ref,
    out_ref, first_ref, grad_ref, part_out, sums_ref, bsum_ref,
    wo_acc, wi_acc, w2_acc, slope_ref, wo_ref, wi_ref, w2_ref, part_ref, sems,
):
    step = pl.program_id(0)
    width = ctx_ref.shape[1]
    dp, side, _, _, _, c = late_ref.shape
    group = members(side)
    r = width // len(group)
    parts = bias_ref.shape[1] // dp // c
    tall = bias_ref.shape[1] // len(group)
    spans = [slice(0, r), slice(r, (1 + parts) * r), slice((1 + parts) * r, (1 + parts) * r + tall)]
    everywhere = (slice(None),) * 4

    def fetch(n):
        at = everywhere + (spans[n],)
        return pltpu.make_async_copy(late_ref.at[at], part_ref.at[at], sems.at[n])

    def deliver(n):
        at = everywhere + (spans[n],)
        return pltpu.make_async_copy(part_ref.at[at], part_out.at[at], sems.at[3 + n])

    hidden = bias_ref.shape[1]
    part = 512

    last = pl.num_programs(0) - 1
    vec = lambda n: vec_ref[n : n + 1, :]
    C = hidden // part
    cols = [slice(n * part, (n + 1) * part) for n in range(C)]

    def unpack(n):
        fetch(n).wait()
        for f, (a, b, core) in enumerate(group):
            block = lambda e, lo, n: part_ref[e, a, b, core, lo : lo + n, :]
            if n == 0:
                wo_ref[f * r : (f + 1) * r, :] = jnp.concatenate([block(e, 0, r) for e in range(dp)], 1)
            elif n == 1:
                wi_ref[f * r : (f + 1) * r, :] = jnp.concatenate(
                    [block(e, (1 + m) * r, r) for e in range(dp) for m in range(parts)], 1
                )
            else:
                w2_ref[f * tall : (f + 1) * tall, :] = jnp.concatenate(
                    [block(e, (1 + parts) * r, tall) for e in range(dp)], 1
                )

    def pack(n):
        for e in range(dp):
            for f, (a, b, core) in enumerate(group):
                rows = slice(f * r, (f + 1) * r)
                if n == 0:
                    part_ref[e, a, b, core, :r, :] = wo_acc[rows, e * c : (e + 1) * c].astype(BF16)
                elif n == 1:
                    for m in range(parts):
                        wide = slice((e * parts + m) * c, (e * parts + m + 1) * c)
                        part_ref[e, a, b, core, (1 + m) * r : (2 + m) * r, :] = wi_acc[rows, wide].astype(BF16)
                else:
                    turned = w2_acc[e * c : (e + 1) * c, f * tall : (f + 1) * tall].astype(BF16)
                    part_ref[e, a, b, core, (1 + parts) * r :, :] = turned.T
        deliver(n).start()

    def body(first, final):
        def add(ref, at, value):
            if first:
                ref[at] = value
            else:
                ref[at] += value

        def add_row(n, value):
            add(sums_ref, (slice(n, n + 1), slice(None)), value)

        if first:
            for n in range(3):
                fetch(n).start()
            sums_ref[0:2, :] = jnp.zeros((2, width), F32)
            unpack(0)
        ctx = ctx_ref[...]
        first_sum = act_ref[...].astype(F32) + pos_ref[...].astype(F32) + (nn(ctx, wo_ref[...]) + vec(2))
        center = first_sum - jnp.mean(first_sum, -1, keepdims=True)
        scale_one = lax.rsqrt(jnp.mean(center * center, -1, keepdims=True) + 1e-05)
        z_one = center * scale_one
        normed = z_one * vec(3) + vec(4)
        normed_low = normed.astype(BF16)
        if first:
            unpack(1)
        branch = None
        acts = []
        pre_next = nn(normed_low, wi_ref[:, cols[0]])
        for n in range(C):
            pre = pre_next + bias_ref[:, cols[n]]
            if n + 1 < C:
                pre_next = nn(normed_low, wi_ref[:, cols[n + 1]])
            if n >= 1:
                if first and n == 1:
                    unpack(2)
                term = nn(acts[n - 1], w2_ref[cols[n - 1], :])
                branch = term if branch is None else branch + term
            square = pre * pre
            t = jnp.tanh(pre * (0.7978845608028654 + (0.7978845608028654 * 0.044715) * square))
            half = 0.5 + 0.5 * t
            acts.append((pre * half).astype(BF16))
            slope_ref[:, cols[n]] = half + (0.5 * pre) * (1.0 - t * t) * (
                0.7978845608028654 + (3.0 * 0.7978845608028654 * 0.044715) * square
            )
        branch = branch + nn(acts[C - 1], w2_ref[cols[C - 1], :])
        second_sum = normed + (branch + vec(5))
        center = second_sum - jnp.mean(second_sum, -1, keepdims=True)
        scale_two = lax.rsqrt(jnp.mean(center * center, -1, keepdims=True) + 1e-05)
        z_two = center * scale_two
        out_ref[...] = (z_two * vec(6) + vec(7)).astype(BF16)
        cot = cot_ref[...].astype(F32)
        add_row(6, column_sum(cot * z_two))
        add_row(7, column_sum(cot))
        e = cot * vec(6)
        second_grad = scale_two * (
            e - jnp.mean(e, -1, keepdims=True) - z_two * jnp.mean(e * z_two, -1, keepdims=True)
        )
        branch_grad = second_grad.astype(BF16)
        add_row(5, column_sum(branch_grad))
        branch_t = branch_grad.T
        normed_t = normed_low.T
        normed_grad = second_grad
        grad_next = nt(branch_grad, w2_ref[cols[0], :])
        lows = []
        everything = slice(None)

        def inner(n):
            add(wi_acc, (everything, cols[n]), nn(normed_t, lows[n]))

        def outer(n):
            add(w2_acc, (everything, cols[n]), nn(branch_t, acts[n]))

        for n in range(C):
            pre_grad = grad_next * slope_ref[:, cols[n]]
            if n + 1 < C:
                grad_next = nt(branch_grad, w2_ref[cols[n + 1], :])
            if n < LATER:
                outer(n)
            if n >= 1:
                inner(n - 1)
                normed_grad = normed_grad + nt(lows[n - 1], wi_ref[:, cols[n - 1]])
            lows.append(pre_grad.astype(BF16))
            add(bsum_ref, (everything, cols[n]), column_sum(lows[n]))
        normed_grad = normed_grad + nt(lows[C - 1], wi_ref[:, cols[C - 1]])
        inner(C - 1)
        add_row(3, column_sum(normed_grad * z_one))
        add_row(4, column_sum(normed_grad))
        e = normed_grad * vec(3)
        level = jnp.mean(e, -1, keepdims=True)
        slant = jnp.mean(e * z_one, -1, keepdims=True)
        for n in range(LATER, C):
            outer(n)
        if final:
            pack(1)
            pack(2)
        first_grad = scale_one * (e - level - z_one * slant)
        first_ref[...] = first_grad
        attn_grad = first_grad.astype(BF16)
        add_row(2, column_sum(attn_grad))
        add(wo_acc, (everything, everything), nn(ctx.T, attn_grad))
        grad_ref[...] = nt(attn_grad, wo_ref[...]).astype(BF16)
        if final:
            pack(0)
            for n in range(3):
                deliver(n).wait()

    @pl.when(step == 0)
    def _():
        for n in range(3):
            fetch(n).start()
        for ref in (wo_acc, wi_acc, w2_acc, sums_ref, bsum_ref):
            ref[...] = jnp.zeros_like(ref)
        for n in range(3):
            unpack(n)

    body(False, False)

    @pl.when(step == last)
    def _():
        for n in (1, 2, 0):
            pack(n)
        for n in range(3):
            deliver(n).wait()


def whole(shape):
    return pl.BlockSpec(shape, lambda *_: (0,) * len(shape))


def once(shape):
    return pl.BlockSpec(shape, lambda *_: (0,) * len(shape), pipeline_mode=pl.Buffered(1))


def run_forward(lengths, act, wq, wk, wv, wo, wi, w2, table, place, line):
    rows, seq, width = act.shape
    dp, side = lax.axis_size("dp"), side_of(lax.axis_size("fsdp"))
    r, c = wq.shape
    hidden = wi.shape[1] * dp
    first_rows = 3 * r + place.shape[0] * place.shape[1] // c + SMALL
    late_rows = r + r * wi.shape[1] // c + w2.shape[0]
    row3 = lambda shape: pl.BlockSpec((1,) + shape, lambda i: (i,) + (0,) * len(shape))
    seqs = row3((seq, width))
    st, tt = jax.ShapeDtypeStruct((rows, seq, width), BF16), jax.ShapeDtypeStruct((rows, width, seq), BF16)
    small = [x.shape for x in (wq, wk, wv, wo, wi, w2, table, place, line)]
    anywhere = pl.BlockSpec(memory_space=pl.ANY)
    return pl.pallas_call(
        forward_attention,
        grid=(rows,),
        in_specs=[pl.BlockSpec(memory_space=pltpu.SMEM), anywhere] + [whole(x) for x in small],
        out_specs=[anywhere] * 6 + [seqs, row3((H // 2, 2, seq)), anywhere, anywhere,
                                    whole((table.shape[0] * dp, width)), whole((1, hidden)), anywhere],
        scratch_shapes=[
            pltpu.VMEM(act.shape, BF16),
            pltpu.SemaphoreType.DMA((rows,)),
            pltpu.VMEM((1, seq, width), BF16),
            pltpu.VMEM((1, width, seq), BF16),
            pltpu.VMEM((1, seq, width), BF16),
            pltpu.VMEM((1, width, seq), BF16),
            pltpu.VMEM((1, seq, width), BF16),
            pltpu.VMEM((1, width, seq), BF16),
            pltpu.VMEM((width, 3 * width), BF16),
            pltpu.VMEM((seq, width), BF16),
            pltpu.SemaphoreType.DMA((8,)),
            pltpu.VMEM((width, seq), BF16),
            pltpu.VMEM((2, width, WIN), BF16),
            pltpu.VMEM((dp, side, side, 2, first_rows, c), BF16),
            pltpu.VMEM((late_rows, c), BF16),
            pltpu.SemaphoreType.DMA,
        ]
        + Gather.semaphores(dp, side) * 2,
        out_shape=[
            st, tt, st, tt, st, tt, st, jax.ShapeDtypeStruct((rows, H // 2, 2, seq), F32),
            jax.ShapeDtypeStruct((width, 3 * width), BF16),
            jax.ShapeDtypeStruct((seq, width), BF16),
            jax.ShapeDtypeStruct((table.shape[0] * dp, width), F32),
            jax.ShapeDtypeStruct((1, hidden), F32),
            jax.ShapeDtypeStruct((dp, side, side, 2, late_rows, c), BF16),
        ],
        compiler_params=pltpu.CompilerParams(
            vmem_limit_bytes=VMEM_LIMIT, collective_id=0, has_side_effects=True
        ),
        name="forward_attention",
    )(lengths, act, wq, wk, wv, wo, wi, w2, table, place, line)


def run_backward(lengths, q, qt, k, kt, v, lse, grad, first, lowt, weight, late, sums, bsum):
    rows, seq, width = grad.shape
    dp, side = late.shape[:2]
    late_rows, c = late.shape[4:]
    r = width // (2 * side * side)
    weight_rows = 3 * r
    place_rows = (seq // dp) * r // c + SMALL
    lanes = pl.BlockSpec((rows, seq, PAIR), lambda j: (0, 0, j))
    turned = pl.BlockSpec((rows, PAIR, seq), lambda j: (0, j, 0))
    anywhere = pl.BlockSpec(memory_space=pl.ANY)
    totals = [(n, c) for n in (late_rows, weight_rows, place_rows)]
    return pl.pallas_call(
        backward_attention,
        grid=(H // 2,),
        in_specs=[pl.BlockSpec(memory_space=pltpu.SMEM), lanes, turned, lanes, turned, lanes,
                  pl.BlockSpec((rows, 1, 2, seq), lambda j: (0, j, 0, 0)), lanes, anywhere, anywhere, anywhere,
                  anywhere, once(sums.shape), once(bsum.shape)],
        out_specs=[anywhere] + [whole(x) for x in totals],
        scratch_shapes=[
            pltpu.VMEM(weight.shape, BF16),
            pltpu.VMEM(grad.shape, BF16),
            pltpu.SemaphoreType.DMA((rows + 1,)),
            pltpu.SemaphoreType.DMA((dp,)),
            pltpu.VMEM((width, rows * seq), BF16),
            pltpu.VMEM((rows, PAIR, seq), BF16),
            pltpu.VMEM((rows, PAIR, seq), BF16),
            pltpu.VMEM((rows, seq, PAIR), F32),
            pltpu.VMEM((rows, seq, PAIR), F32),
            pltpu.VMEM((rows * seq, 3 * PAIR), BF16),
            pltpu.VMEM((rows, seq, width), F32),
            pltpu.VMEM(sums.shape, F32),
            pltpu.VMEM((dp, side, side, 2, weight_rows, c), BF16),
            pltpu.VMEM((dp, side, side, 2, place_rows, c), BF16),
            pltpu.VMEM((dp, side, side, late_rows, c), BF16),
            pltpu.SemaphoreType.DMA,
            pltpu.SemaphoreType.DMA,
        ]
        + Reduce.scratch(dp, side, late_rows, c)
        + Reduce.scratch(dp, side, weight_rows, c)
        + Reduce.scratch(dp, side, place_rows, c),
        out_shape=[jax.ShapeDtypeStruct(grad.shape, BF16)] + [jax.ShapeDtypeStruct(x, F32) for x in totals],
        compiler_params=pltpu.CompilerParams(
            vmem_limit_bytes=VMEM_LIMIT, collective_id=1, has_side_effects=True
        ),
        name="backward_attention",
    )(lengths, q, qt, k, kt, v, lse, grad, first, lowt, weight, late, sums, bsum)


def run_hand_out(late, weight, place, grad, shapes):
    anywhere = pl.BlockSpec(memory_space=pl.ANY)
    tokens = grad.reshape(-1, grad.shape[-1])
    dma = pltpu.SemaphoreType.DMA
    pieces = 4
    return pl.pallas_call(
        hand_out,
        in_specs=[anywhere] * 4,
        out_specs=[anywhere] * (1 + len(shapes)),
        out_shape=[jax.ShapeDtypeStruct(tokens.shape, BF16)] + [jax.ShapeDtypeStruct(x, F32) for x in shapes],
        scratch_shapes=[pltpu.VMEM(x.shape, x.dtype) for x in (late, weight, place, tokens)]
        + [pltpu.VMEM(x, F32) for x in shapes]
        + [dma((3 + pieces,)), dma((len(shapes) + pieces,))],
        name="hand_out",
    )(late, weight, place, tokens)


def run_feed_forward(ctx, act, pos, cot, late, vec, bias, tile=512):
    tokens, width = ctx.shape
    seq = pos.shape[0]
    hidden = bias.shape[1]
    per_row = seq // tile
    tok = pl.BlockSpec((tile, width), lambda t: (t, 0))
    return pl.pallas_call(
        feed_forward,
        grid=(tokens // tile,),
        in_specs=[tok, tok, pl.BlockSpec((tile, width), lambda t: (t % per_row, 0)), tok,
                  pl.BlockSpec(memory_space=pl.ANY), whole(vec.shape), whole(bias.shape)],
        out_specs=[tok, tok, tok, pl.BlockSpec(memory_space=pl.ANY), whole((8, width)),
                   whole((1, hidden))],
        scratch_shapes=[
            pltpu.VMEM((width, width), F32),
            pltpu.VMEM((width, hidden), F32),
            pltpu.VMEM((width, hidden), F32),
            pltpu.VMEM((tile, hidden), F32),
            pltpu.VMEM((width, width), BF16),
            pltpu.VMEM((width, hidden), BF16),
            pltpu.VMEM((hidden, width), BF16),
            pltpu.VMEM(late.shape, BF16),
            pltpu.SemaphoreType.DMA((6,)),
        ],
        out_shape=[
            jax.ShapeDtypeStruct((tokens, width), BF16),
            jax.ShapeDtypeStruct((tokens, width), F32),
            jax.ShapeDtypeStruct((tokens, width), BF16),
            jax.ShapeDtypeStruct(late.shape, BF16),
            jax.ShapeDtypeStruct((8, width), F32),
            jax.ShapeDtypeStruct((1, hidden), F32),
        ],
        compiler_params=pltpu.CompilerParams(vmem_limit_bytes=VMEM_LIMIT),
        name="feed_forward",
    )(ctx, act, pos, cot, late, vec, bias)


def shards(
    activations, window_lengths, query_weight, key_weight, value_weight, output_weight, inner_weight, outer_weight,
    vectors, positions, inner_bias, output_cotangent,
):
    rows, seq, width = activations.shape
    q, qt, k, kt, v, lowt, ctx, lse, weight, pos, vec, bias, late = run_forward(
        window_lengths, activations, query_weight, key_weight, value_weight, output_weight, inner_weight, outer_weight,
        vectors, positions.T, inner_bias.reshape(1, -1),
    )
    flat = lambda x: x.reshape(rows * seq, width)
    deep = lambda x: x.reshape(rows, seq, width)
    out, first, grad, part, sums, bsum = run_feed_forward(
        flat(ctx), flat(activations), pos, flat(output_cotangent), late, vec, bias
    )
    input_grad, *sums = run_backward(
        window_lengths, q, qt, k, kt, v, lse, deep(grad), deep(first), lowt, weight, part, sums, bsum
    )
    shapes = [x.shape for x in (query_weight, key_weight, value_weight, output_weight, inner_weight, outer_weight,
                                vectors, positions.T)] + [(1, inner_bias.shape[0])]
    owned = run_hand_out(*sums, input_grad, shapes)
    return (deep(out), owned[0].reshape(input_grad.shape)) + tuple(owned[1:8]) + (owned[8].T, owned[9].reshape(-1))


def solution(mesh):
    tokens = P(("dp", "fsdp"), None, None)
    matrix = P("fsdp", "dp")
    table = P("dp", "fsdp")
    line = P(("dp", "fsdp"))
    return jax.shard_map(
        shards,
        mesh=mesh,
        in_specs=(tokens, P(("dp", "fsdp"), None)) + (matrix,) * 6 + (table, table, line, tokens),
        out_specs=(tokens, tokens) + (matrix,) * 6 + (table, table, line),
        check_vma=False,
    )
```
